32 devices in a mesh: section: 4 (over x, core), mp: 8 (over z, y).
Axes of the slice: x: 2, y: 2, z: 4, core: 2. Of those that a mesh axis runs over, the one named last changes fastest.
Arguments:
- text_state: bfloat16 [4, 512, 8192], P('section', 'mp'), may hold values from -1.5 to 1.5
- tile_feats: bfloat16 [1280, 7680], P('section', 'mp'), may hold values from -6 to 6
- w_proj: bfloat16 [7680, 8192], P('mp'), may hold values from -0.0625 to 0.0625
- w_query: bfloat16 [4, 8192, 4096], P('section', None, 'mp'), may hold values from -0.0625 to 0.0625
- w_kv: bfloat16 [4, 8192, 1024], P('section', 'mp'), may hold values from -0.0625 to 0.0625
- w_out: bfloat16 [4, 4096, 8192], P('section', 'mp'), may hold values from -0.09375 to 0.09375
- attn_gate: float32 [4], P('section'), may hold values from 0.3 to 1.5
- tile_counts: int32 [16], replicated, may hold values from 1 to 4, 40 in all
- section_table: int32 [16], replicated, may hold values from 0 to 3, as said below
Outputs:
- advanced: bfloat16 [4, 512, 8192], P('section', 'mp')
The draws below stay inside these ranges and needn't reach their ends.
Inputs may be any that keep to these rules, and one draw needn't show every extreme that they name: `section_table`: each section is named by exactly 4 samples. `tile_counts`: the counts add up to 40, and some sample has exactly 4 tiles.
All inputs are finite; a program needn't handle non-finite values.
Results may differ from the reference program's by a relative error of at most 0.02.
Values may be sent and summed in bfloat16 or wider, within the bound.
No kernel may reach another device: no remote copies, remote signals or barrier semaphores. Data moves between devices by JAX's collectives and lax.ppermute only.
A program may use at most 128 MiB of HBM per device.

```python
import math
import jax
import jax.numpy as jnp
import numpy as np
from jax import lax

D = 8192
VF = 7680
HD = 128
HEADS = 32
KVH = 4
SAMP_SECTION = 4
TXT = 128
TT = 32
MAXT = 4
TILES_SECTION = 10
SAMPLES = 16
TOKENS = 512
VROWS = 1280
N_SECTION = 4
N_MP = 8


def draw_section_table(key, part):
    key = jax.random.fold_in(key, 7)
    shuffled = jax.random.permutation(key, SAMPLES)
    return (shuffled // SAMP_SECTION).astype(jnp.int32)


def block_scale(key, dims, split, low, largest):
    gain = 1.0
    for axis_at, shards_of in split:
        draws = jax.random.uniform(jax.random.fold_in(jax.random.fold_in(key, 6), axis_at), (shards_of,), jnp.float32, low / len(split), largest / len(split))
        gain = gain * jnp.repeat(jnp.exp(draws), dims[axis_at] // shards_of).reshape((-1,) + (1,) * (len(dims) - 1 - axis_at))
    return gain


def split_up(count, total, limit, lean):
    loads = [(1 << 20) // math.isqrt(rank ** lean) + 1 for rank in range(2, count + 1)]
    spare, given = total - limit - (count - 1), [1] * (count - 1)
    while spare > 0:
        movable = [i for i in range(count - 1) if given[i] < limit]
        pool, left = sum([loads[i] for i in movable]), spare
        for i in movable:
            extra = min(limit - given[i], max(1, left * loads[i] // pool), spare)
            given[i] = given[i] + extra
            spare = spare - extra
    return np.array([limit] + given)


def ragged(rng, count, total, limit, skew):
    if count == 2:
        one = jax.random.randint(rng, (), max(1, total - limit), min(limit, total - 1) + 1)
        return jnp.stack([one, total - one])
    sizes = jnp.asarray(split_up(count, total, limit, skew), jnp.int32)
    couples = (count - 1) // 2
    giver, receiver = sizes[1:1 + 2 * couples:2], sizes[2:2 + 2 * couples:2]
    room = jnp.minimum(giver - 1, limit - receiver)
    passed = jax.random.randint(jax.random.fold_in(rng, 1), (couples,), 0, 1 << 20) % (room + 1)
    sizes = sizes.at[1:1 + 2 * couples:2].set(giver - passed).at[2:2 + 2 * couples:2].set(receiver + passed)
    return sizes[jax.random.permutation(jax.random.fold_in(rng, 2), count)]


def noise(key, shape, deviation, most, shards=(), kind=jnp.bfloat16):
    gain = block_scale(key, shape, shards, -0.22, 0.18) if shards else 1.0
    values = jax.random.normal(key, shape, jnp.float32) * deviation * gain
    return jnp.minimum(jnp.maximum(values, -most), most).astype(kind)


def setup_inputs(seed: int = 0) -> dict:
    key_of = jax.random.split(jax.random.key(seed), 10)
    text_state = noise(key_of[0], (N_SECTION, TOKENS, D), 0.25, 1.5, ((0, 4), (1, 8)))
    tile_feats = noise(key_of[1], (VROWS, VF), 1.0, 6.0, ((0, 4), (1, 8)))
    w_proj = noise(key_of[2], (VF, D), VF ** -0.5, 0.0625, ((0, 8),))
    w_query = noise(key_of[3], (N_SECTION, D, HEADS * HD), D ** -0.5, 0.0625, ((0, 4), (2, 8)))
    w_kv = noise(key_of[4], (N_SECTION, D, 2 * KVH * HD), D ** -0.5, 0.0625, ((0, 4), (1, 8)))
    w_out = noise(key_of[5], (N_SECTION, HEADS * HD, D), (HEADS * HD) ** -0.5, 0.09375, ((0, 4), (1, 8)))
    attn_gate = jnp.clip(0.3 + 1.2 * jax.random.uniform(key_of[6], (N_SECTION,), jnp.float32) ** block_scale(key_of[6], (N_SECTION,), ((0, 4),), -0.2, 0.2), 0.3, 1.5)
    tile_counts = ragged(key_of[7], SAMPLES, TILES_SECTION * N_SECTION, MAXT, 2).astype(jnp.int32)
    section_table = draw_section_table(jax.random.fold_in(key_of[9], 71), 0)
    return {"text_state": text_state, "tile_feats": tile_feats, "w_proj": w_proj, "w_query": w_query, "w_kv": w_kv, "w_out": w_out, "attn_gate": attn_gate, "tile_counts": tile_counts, "section_table": section_table}


def root_scale(values, epsilon):
    return values * lax.rsqrt(lax.optimization_barrier(jnp.mean(values * values, axis=-1, keepdims=True)) + epsilon)

def slot_index(tile_counts, section_table, section_id):
    samples_all = tile_counts.shape[0]
    sample_ids = jnp.arange(samples_all, dtype=jnp.int32)
    same_section = section_table[None, :] == section_table[:, None]
    before = sample_ids[None, :] < sample_ids[:, None]
    ranking = lax.optimization_barrier(jnp.sum((same_section & before).astype(jnp.int32), axis=1)).astype(jnp.int32)
    picked = (section_table[None, :] == section_id) & (ranking[None, :] == jnp.arange(SAMP_SECTION, dtype=jnp.int32)[:, None])
    first_row = (TT * (jnp.cumsum(tile_counts) - tile_counts)).astype(jnp.int32)
    counts_own = lax.optimization_barrier(jnp.sum(jnp.where(picked, tile_counts[None, :], 0), axis=1)).astype(jnp.int32)
    starts_own = lax.optimization_barrier(jnp.sum(jnp.where(picked, first_row[None, :], 0), axis=1)).astype(jnp.int32)
    offsets = jnp.arange(MAXT * TT, dtype=jnp.int32)
    live_slot = offsets[None, :] < (TT * counts_own)[:, None]
    row_index = jnp.where(live_slot, starts_own[:, None] + offsets[None, :], 0).astype(jnp.int32)
    return (row_index.reshape(-1), live_slot)

def reference(text_state, tile_feats, w_proj, w_query, w_kv, w_out, attn_gate, tile_counts, section_table):
    block_size = VF // N_MP
    image_sum = jnp.zeros((tile_feats.shape[0], D), jnp.float32)
    for block_id in range(N_MP):
        lower = block_id * block_size
        partial_sum = jnp.dot(tile_feats[:, lower:lower + block_size], w_proj[lower:lower + block_size], preferred_element_type=jnp.float32)
        rounded = lax.optimization_barrier(partial_sum.astype(jnp.bfloat16))
        image_sum = image_sum + rounded.astype(jnp.float32)
    image_rows = image_sum.astype(jnp.bfloat16)
    group_size = HEADS // KVH
    slots_all = SAMP_SECTION * MAXT * TT
    head_block = HEADS * HD // N_MP
    results = []
    for section_id in range(N_SECTION):
        row_index, live_slot = slot_index(tile_counts, section_table, section_id)
        slot_image = jnp.where(live_slot.reshape(-1)[:, None], image_rows[row_index], 0).astype(jnp.bfloat16)
        key_value = jnp.dot(slot_image, w_kv[section_id], preferred_element_type=jnp.float32)
        keys_all = root_scale(key_value[:, :KVH * HD].reshape(slots_all, KVH, HD), 1e-06).astype(jnp.bfloat16)
        values_all = key_value[:, KVH * HD:].reshape(slots_all, KVH, HD).astype(jnp.bfloat16)
        current = text_state[section_id].astype(jnp.float32)
        normed = root_scale(current, 1e-05).astype(jnp.bfloat16)
        queries = jnp.dot(normed, w_query[section_id], preferred_element_type=jnp.float32)
        queries = root_scale(queries.reshape(-1, HEADS, HD), 1e-06).astype(jnp.bfloat16)
        query_grid = queries.reshape(SAMP_SECTION, TXT, KVH, group_size, HD).astype(jnp.float32)
        key_grid = keys_all.reshape(SAMP_SECTION, MAXT * TT, KVH, HD).astype(jnp.float32)
        value_grid = values_all.reshape(SAMP_SECTION, MAXT * TT, KVH, HD).astype(jnp.float32)
        scores = jnp.einsum('stcgd,skcd->scgtk', query_grid, key_grid) / math.sqrt(HD)
        raised = jnp.where(live_slot[:, None, None, None, :], jnp.exp(scores), 0.0)
        weights = (raised / lax.optimization_barrier(jnp.sum(raised, axis=-1, keepdims=True))).astype(jnp.bfloat16)
        attended = jnp.einsum('scgtk,skcd->stcgd', weights.astype(jnp.float32), value_grid)
        attended = attended.astype(jnp.bfloat16).reshape(SAMP_SECTION * TXT, HEADS * HD)
        branch = jnp.zeros((SAMP_SECTION * TXT, D), jnp.float32)
        for block_id in range(N_MP):
            lower = block_id * head_block
            partial_out = jnp.dot(attended[:, lower:lower + head_block], w_out[section_id][lower:lower + head_block], preferred_element_type=jnp.float32)
            rounded_out = lax.optimization_barrier(partial_out.astype(jnp.bfloat16))
            branch = branch + rounded_out.astype(jnp.float32)
        results.append((current + jnp.tanh(attn_gate[section_id]) * branch).astype(jnp.bfloat16))
    return jnp.roll(jnp.stack(results), 1, axis=0)
```

```python
import math

import jax
import jax.numpy as jnp
from jax import lax
from jax.sharding import PartitionSpec as P

HD = 128
HEADS = 32
KVH = 4
SAMP_SECTION = 4
TXT = 128
TT = 32
MAXT = 4
F32 = jnp.float32
BF16 = jnp.bfloat16


def ring_order(count):
    wide = 2 if count <= 8 else 4
    tall = count // wide
    if count < 4 or count % wide or tall % 2:
        return list(range(count))
    order = [row * wide for row in range(tall)]
    for turn, row in enumerate(reversed(range(tall))):
        columns = range(1, wide) if turn % 2 == 0 else range(wide - 1, 0, -1)
        order += [row * wide + column for column in columns]
    return order


def slot_index(tile_counts, section_table, section_id):
    samples_all = tile_counts.shape[0]
    sample_ids = jnp.arange(samples_all, dtype=jnp.int32)
    same_section = section_table[None, :] == section_table[:, None]
    before = sample_ids[None, :] < sample_ids[:, None]
    ranking = jnp.sum((same_section & before).astype(jnp.int32), axis=1)
    picked = (section_table[None, :] == section_id) & (
        ranking[None, :] == jnp.arange(SAMP_SECTION, dtype=jnp.int32)[:, None]
    )
    first_row = TT * jnp.sum(jnp.where(before, tile_counts[None, :], 0), axis=1)
    counts_own = jnp.sum(jnp.where(picked, tile_counts[None, :], 0), axis=1)
    starts_own = jnp.sum(jnp.where(picked, first_row[None, :], 0), axis=1)
    offsets = jnp.arange(MAXT * TT, dtype=jnp.int32)
    live_slot = offsets[None, :] < (TT * counts_own)[:, None]
    row_index = jnp.where(live_slot, starts_own[:, None] + offsets[None, :], -1)
    return (row_index.reshape(-1), live_slot)


def add(one, other):
    return (one.astype(F32) + other.astype(F32)).astype(BF16)


def local(
    mesh_shape,
    text_state,
    tile_feats,
    w_proj,
    w_query,
    w_kv,
    w_out,
    attn_gate,
    tile_counts,
    section_table,
):
    mp_count, section_count = mesh_shape["mp"], mesh_shape["section"]
    section_id = lax.axis_index("section")
    mp_place = lax.axis_index("mp")
    ring = ring_order(mp_count)
    far = mp_count // 2
    place = jnp.asarray([ring.index(i) for i in range(mp_count)], jnp.int32)[mp_place]
    ring_ids = jnp.asarray(ring, jnp.int32)

    def member(offset):
        return ring_ids[(place + offset) % mp_count]

    up_pairs = [(ring[i], ring[(i + 1) % mp_count]) for i in range(mp_count)]
    down_pairs = [(target, source) for source, target in up_pairs]

    def up(value):
        return lax.ppermute(value, "mp", up_pairs)

    def down(value):
        return lax.ppermute(value, "mp", down_pairs)

    def across(pairs):
        return [
            (s * mp_count + a, ((s + 1) % section_count) * mp_count + b)
            for s in range(section_count)
            for a, b in pairs
        ]

    def up_across(value):
        return lax.ppermute(value, ("section", "mp"), across(up_pairs))

    def down_across(value):
        return lax.ppermute(value, ("section", "mp"), across(down_pairs))

    def to_next(value):
        return lax.ppermute(
            value, "section", [(s, (s + 1) % section_count) for s in range(section_count)]
        )

    def ring_sum(part, start_up, start_down, last_up=up, last_down=down):
        arrived = []
        for start, sign, move, last in (
            (start_up, 1, up, last_up),
            (start_down, -1, down, last_down),
        ):
            running = part(sign * start)
            for distance in range(start, 1, -1):
                running = add(move(running), part(sign * (distance - 1)))
            arrived.append(last(running))
        return arrived

    text_own = text_state[0]
    text_rows = text_own.shape[0]
    cut = text_rows // 2
    halves = (text_own[:cut], text_own[cut:])
    from_below = [halves]
    from_above = [halves]
    for distance in range(1, far + 1):
        top_up = up(from_below[-1][0])
        low_down = down(from_above[-1][1])
        if distance < far:
            low_up = up(from_below[-1][1])
            top_down = down(from_above[-1][0])
        else:
            low_up = top_down = None
        from_below.append((top_up, low_up))
        from_above.append((top_down, low_down))
    text_next = to_next(text_own)
    gate_next = to_next(attn_gate)

    image_part = lax.optimization_barrier(
        jnp.dot(tile_feats, w_proj, preferred_element_type=F32).astype(BF16)
    )
    feat_rows = tile_feats.shape[0]
    wide = w_proj.shape[1] // mp_count
    image_halves = []
    for half, (start_up, start_down) in enumerate(((far, far - 1), (far - 1, far))):
        rows = feat_rows // 2

        def image_block(offset, half=half, rows=rows):
            return lax.dynamic_slice(
                image_part, (half * rows, member(offset) * wide), (rows, wide)
            )

        arrived = ring_sum(image_block, start_up, start_down)
        total = image_block(0).astype(F32) + arrived[0].astype(F32) + arrived[1].astype(F32)
        image_halves.append(total.astype(BF16))
    image_cols = jnp.concatenate(image_halves, axis=0)

    def pair_swap(value):
        return lax.ppermute(value, "section", [(s, s ^ 1) for s in range(section_count)])

    own_ids = jnp.arange(feat_rows, dtype=jnp.int32)
    pieces, piece_ids = [], []
    moving, moving_from = image_cols, section_id
    for step in range(section_count // 2):
        pieces += [moving, pair_swap(moving)]
        piece_ids += [
            moving_from * feat_rows + own_ids,
            (moving_from ^ 1) * feat_rows + own_ids,
        ]
        if step + 1 < section_count // 2:
            moving = lax.ppermute(
                moving,
                "section",
                [(s, (s + 2) % section_count) for s in range(section_count)],
            )
            moving_from = (moving_from + section_count - 2) % section_count
    row_index, live_slot = slot_index(tile_counts, section_table, section_id)
    choose = (row_index[:, None] == jnp.concatenate(piece_ids)[None, :]).astype(BF16)
    slot_image = jnp.dot(
        choose, jnp.concatenate(pieces, axis=0), preferred_element_type=F32
    ).astype(BF16)

    weight_kv = w_kv[0]
    kv_part = lax.optimization_barrier(
        jnp.dot(slot_image, weight_kv, preferred_element_type=F32).astype(BF16)
    )
    slots = kv_part.shape[0]
    half_width = weight_kv.shape[1] // 2
    sharing = mp_count // KVH
    kv_rows = slots // sharing

    def kv_block(offset):
        target = member(offset)
        row = (target % sharing) * kv_rows
        column = (target // sharing) * HD
        return jnp.concatenate(
            [
                lax.dynamic_slice(kv_part, (row, column), (kv_rows, HD)),
                lax.dynamic_slice(kv_part, (row, half_width + column), (kv_rows, HD)),
            ],
            axis=1,
        )

    arrived = ring_sum(kv_block, far, far - 1)
    kv_own = (
        kv_block(0).astype(F32) + arrived[0].astype(F32) + arrived[1].astype(F32)
    ).astype(BF16)
    kv_pieces = [kv_own]
    for step in range(1, sharing):
        pairs = [
            (m, m // sharing * sharing + (m % sharing + step) % sharing) for m in range(mp_count)
        ]
        kv_pieces.insert(0, lax.ppermute(kv_own, "mp", pairs))
    mine = mp_place % sharing
    kv_twice = jnp.concatenate(kv_pieces + kv_pieces, axis=0)
    kv_all = lax.dynamic_slice(
        kv_twice, ((sharing - 1 - mine) % sharing * kv_rows, 0), (slots, 2 * HD)
    ).astype(F32)
    keys = kv_all[:, :HD]
    keys = keys * lax.rsqrt(jnp.mean(keys * keys, axis=-1, keepdims=True) + 1e-06)
    keys = keys.astype(BF16).reshape(SAMP_SECTION, MAXT * TT, HD)
    values = kv_all[:, HD:].astype(BF16).reshape(SAMP_SECTION, MAXT * TT, HD)

    head_dev = HEADS // mp_count
    weight_query, weight_out = w_query[0], w_out[0]

    def query_of(rows):
        wide_rows = rows.astype(F32)
        scale = lax.rsqrt(jnp.mean(wide_rows * wide_rows, axis=-1, keepdims=True) + 1e-05)
        projected = jnp.dot(rows, weight_query, preferred_element_type=F32) * scale
        projected = projected.reshape(rows.shape[0], head_dev, HD)
        projected = projected * lax.rsqrt(
            jnp.mean(projected * projected, axis=-1, keepdims=True) + 1e-06
        )
        return projected.astype(BF16).reshape(rows.shape[0], head_dev * HD)

    def attend(queries, offsets):
        samples = jnp.stack([member(o) * text_rows // TXT for o in offsets])
        grid = queries.reshape(len(offsets), text_rows, head_dev, HD)
        scores = jnp.einsum(
            "sthd,skd->shtk", grid, keys[samples], preferred_element_type=F32
        ) / math.sqrt(HD)
        raised = jnp.where(live_slot[samples][:, None, None, :], jnp.exp(scores), 0.0)
        weights = (raised / jnp.sum(raised, axis=-1, keepdims=True)).astype(BF16)
        attended = jnp.einsum(
            "shtk,skd->sthd", weights, values[samples], preferred_element_type=F32
        )
        return attended.astype(BF16).reshape(len(offsets) * text_rows, head_dev * HD)

    near = [0]
    near_queries = [None]
    for distance in range(1, far):
        near += [-distance, distance]
        rows = from_below[distance] + from_above[distance]
        if distance == 1:
            rows = halves + rows
        near_queries.append(query_of(jnp.concatenate(rows, axis=0)))
    near_queries = jnp.concatenate(near_queries[1:], axis=0)
    far_rows = jnp.concatenate([from_below[far][0], from_above[far][1]], axis=0)
    far_attended = attend(query_of(far_rows), [far])
    far_part = lax.optimization_barrier(
        jnp.dot(far_attended, weight_out, preferred_element_type=F32).astype(BF16)
    )
    near_attended = attend(near_queries, near)
    near_part = lax.optimization_barrier(
        jnp.dot(near_attended, weight_out, preferred_element_type=F32).astype(BF16)
    )

    own_next = to_next(near_part[:text_rows])
    results = []
    for half, (start_up, start_down) in enumerate(((far, far - 1), (far - 1, far))):

        def out_block(offset, half=half):
            if abs(offset) == far:
                return far_part[half * cut : (half + 1) * cut]
            first = near.index(offset) * text_rows + half * cut
            return near_part[first : first + cut]

        arrived = ring_sum(out_block, start_up, start_down, up_across, down_across)
        rows = slice(half * cut, (half + 1) * cut)
        branch = own_next[rows].astype(F32) + arrived[0].astype(F32) + arrived[1].astype(F32)
        results.append(
            (text_next[rows].astype(F32) + jnp.tanh(gate_next[0]) * branch).astype(BF16)
        )
    return jnp.concatenate(results, axis=0)[None]


def solution(mesh):
    mesh_shape = dict(mesh.shape)

    def body(*arrays):
        return local(mesh_shape, *arrays)

    return jax.shard_map(
        body,
        mesh=mesh,
        in_specs=(
            P("section", "mp", None),
            P("section", "mp"),
            P("mp", None),
            P("section", None, "mp"),
            P("section", "mp", None),
            P("section", "mp", None),
            P("section"),
            P(),
            P(),
        ),
        out_specs=P("section", "mp", None),
        check_vma=False,
    )
```

```python
import math

import jax
import jax.numpy as jnp
import numpy as np
from jax import lax
from jax.experimental import pallas as pl
from jax.experimental.pallas import tpu as pltpu
from jax.sharding import PartitionSpec as P

HD = 128
HEADS = 32
KVH = 4
SAMP_SECTION = 4
TXT = 128
TT = 32
MAXT = 4
BLOCK = MAXT * TT
SLOTS = SAMP_SECTION * BLOCK
F32 = jnp.float32
BF16 = jnp.bfloat16
VMEM_LIMIT = 40 * 1024 * 1024


def ring_order(count):
    wide = 2 if count <= 8 else 4
    tall = count // wide
    if count < 4 or count % wide or tall % 2:
        return list(range(count))
    order = [row * wide for row in range(tall)]
    for turn, row in enumerate(reversed(range(tall))):
        columns = range(1, wide) if turn % 2 == 0 else range(wide - 1, 0, -1)
        order += [row * wide + column for column in columns]
    return order


def own_samples(tile_counts, section_table, section_id):
    samples_all = tile_counts.shape[0]
    sample_ids = jnp.arange(samples_all, dtype=jnp.int32)
    same_section = section_table[None, :] == section_table[:, None]
    before = sample_ids[None, :] < sample_ids[:, None]
    ranking = jnp.sum((same_section & before).astype(jnp.int32), axis=1)
    picked = (section_table[None, :] == section_id) & (
        ranking[None, :] == jnp.arange(SAMP_SECTION, dtype=jnp.int32)[:, None]
    )
    first_row = TT * jnp.sum(jnp.where(before, tile_counts[None, :], 0), axis=1)
    counts_own = jnp.sum(jnp.where(picked, tile_counts[None, :], 0), axis=1)
    starts_own = jnp.sum(jnp.where(picked, first_row[None, :], 0), axis=1)
    return starts_own, counts_own


def add(one, other):
    return (one.astype(F32) + other.astype(F32)).astype(BF16)


def params():
    return pltpu.CompilerParams(vmem_limit_bytes=VMEM_LIMIT)


def project(meta, feats, weight, order_len):
    rows, depth = feats.shape
    wide = weight.shape[1] // order_len

    def kernel(meta_ref, feats_ref, weight_ref, out_ref):
        out_ref[0] = jnp.dot(
            feats_ref[...], weight_ref[...], preferred_element_type=F32
        ).astype(BF16)

    return pl.pallas_call(
        kernel,
        grid_spec=pltpu.PrefetchScalarGridSpec(
            num_scalar_prefetch=1,
            grid=(order_len,),
            in_specs=[
                pl.BlockSpec((rows, depth), lambda i, meta: (0, 0)),
                pl.BlockSpec((depth, wide), lambda i, meta: (0, meta[i])),
            ],
            out_specs=pl.BlockSpec((1, rows, wide), lambda i, meta: (i, 0, 0)),
        ),
        out_shape=jax.ShapeDtypeStruct((order_len, rows, wide), BF16),
        compiler_params=params(),
        cost_estimate=pl.CostEstimate(
            flops=2 * rows * depth * weight.shape[1],
            bytes_accessed=2 * (depth + rows) * weight.shape[1],
            transcendentals=0,
        ),
        name="project",
    )(meta, feats, weight)


def key_values(meta, pieces, weight, order_len, section_count, sharing):
    feat_rows = pieces[0].shape[0]
    depth, width = weight.shape
    kv_rows = SLOTS // sharing
    half_width = width // 2
    count = len(pieces)

    def kernel(meta_ref, *refs):
        piece_refs, weight_ref, out_ref, kv_ref = refs[:count], refs[count], refs[-2], refs[-1]
        section = meta_ref[order_len + 1]
        slot = lax.broadcasted_iota(jnp.int32, (BLOCK, feat_rows), 0)
        packed = lax.broadcasted_iota(jnp.int32, (BLOCK, feat_rows), 1)
        for sample in range(SAMP_SECTION):
            start = meta_ref[order_len + 2 + sample]
            live = TT * meta_ref[order_len + 2 + SAMP_SECTION + sample]
            image = jnp.zeros((BLOCK, depth), F32)
            for index in range(count):
                step, swapped = index // 2, index % 2
                origin = lax.rem(section + (section_count - 2 * step), section_count)
                if swapped:
                    origin = origin + 1 - 2 * lax.rem(origin, 2)
                chosen = (slot < live) & (packed == slot + (start - origin * feat_rows))
                image += jnp.dot(
                    chosen.astype(F32).astype(BF16),
                    piece_refs[index][...],
                    preferred_element_type=F32,
                )
            kv_ref[sample * BLOCK : (sample + 1) * BLOCK, :] = jnp.dot(
                image.astype(BF16), weight_ref[...], preferred_element_type=F32
            ).astype(BF16)
        for index in range(order_len):
            target = meta_ref[index]
            row = pl.multiple_of(lax.rem(target, sharing) * kv_rows, kv_rows)
            column = pl.multiple_of(target // sharing * HD, HD)
            out_ref[index, :, :HD] = kv_ref[pl.ds(row, kv_rows), pl.ds(column, HD)]
            out_ref[index, :, HD:] = kv_ref[
                pl.ds(row, kv_rows), pl.ds(pl.multiple_of(column + half_width, HD), HD)
            ]

    whole = pl.BlockSpec(memory_space=pltpu.VMEM)
    return pl.pallas_call(
        kernel,
        in_specs=[pl.BlockSpec(memory_space=pltpu.SMEM)] + [whole] * (count + 1),
        out_specs=whole,
        out_shape=jax.ShapeDtypeStruct((order_len, kv_rows, 2 * HD), BF16),
        scratch_shapes=[pltpu.VMEM((SLOTS, width), BF16)],
        compiler_params=params(),
        cost_estimate=pl.CostEstimate(
            flops=2 * SLOTS * depth * (width + feat_rows * count),
            bytes_accessed=2 * depth * (width + feat_rows * count),
            transcendentals=0,
        ),
        name="key_values",
    )(meta, *pieces, weight)


def query(chunks, weight):
    rows = sum(chunk.shape[0] for chunk in chunks)
    depth, width = weight.shape
    wide = min(2 * HD, width)
    count = len(chunks)

    def kernel(*refs):
        chunk_refs, weight_ref, out_ref = refs[:count], refs[count], refs[count + 1]
        first = 0
        for chunk_ref in chunk_refs:
            size = chunk_ref.shape[0]
            chunk = chunk_ref[...]
            wider = chunk.astype(F32)
            scale = lax.rsqrt(jnp.mean(wider * wider, axis=-1, keepdims=True) + 1e-05)
            projected = jnp.dot(chunk, weight_ref[...], preferred_element_type=F32) * scale
            for head in range(wide // HD):
                one = projected[:, head * HD : (head + 1) * HD]
                one = one * lax.rsqrt(jnp.mean(one * one, axis=-1, keepdims=True) + 1e-06)
                out_ref[first : first + size, head * HD : (head + 1) * HD] = one.astype(BF16)
            first += size

    return pl.pallas_call(
        kernel,
        grid=(width // wide,),
        in_specs=[pl.BlockSpec(chunk.shape, lambda i: (0, 0)) for chunk in chunks]
        + [pl.BlockSpec((depth, wide), lambda i: (0, i))],
        out_specs=pl.BlockSpec((rows, wide), lambda i: (0, i)),
        out_shape=jax.ShapeDtypeStruct((rows, width), BF16),
        compiler_params=params(),
        cost_estimate=pl.CostEstimate(
            flops=2 * rows * depth * width,
            bytes_accessed=2 * depth * (width + rows),
            transcendentals=0,
        ),
        name="query",
    )(*chunks, weight)


def attend(meta, queries, kv_pieces, weight, indices, text_rows, order_len):
    rows, width = queries.shape
    heads = width // HD
    sharing = len(kv_pieces)
    kv_rows = SLOTS // sharing
    columns = weight.shape[1]
    wide = min(1024, columns)

    def kernel(meta_ref, query_ref, *refs):
        kv_refs, weight_ref, out_ref = refs[:sharing], refs[sharing], refs[sharing + 1]
        key_ref, value_ref, attended_ref = refs[sharing + 2 :]

        @pl.when(pl.program_id(0) == 0)
        def _():
            mine = lax.rem(meta_ref[order_len], sharing)
            for step in range(sharing):
                row = pl.multiple_of(
                    lax.rem(mine + sharing - step, sharing) * kv_rows, kv_rows
                )
                keys = kv_refs[step][:, :HD].astype(F32)
                keys = keys * lax.rsqrt(jnp.mean(keys * keys, axis=-1, keepdims=True) + 1e-06)
                key_ref[pl.ds(row, kv_rows), :] = keys.astype(BF16)
                value_ref[pl.ds(row, kv_rows), :] = kv_refs[step][:, HD:]
            for place, index in enumerate(indices):
                sample = meta_ref[index] * text_rows // TXT
                slots = pl.ds(pl.multiple_of(sample * BLOCK, BLOCK), BLOCK)
                live = TT * meta_ref[order_len + 2 + SAMP_SECTION + sample]
                first = place * text_rows
                own = query_ref[first : first + text_rows, :]
                stacked = jnp.concatenate(
                    [own[:, h * HD : (h + 1) * HD] for h in range(heads)], axis=0
                )
                scores = lax.dot_general(
                    stacked,
                    key_ref[slots, :],
                    (((1,), (1,)), ((), ())),
                    preferred_element_type=F32,
                ) * (1.0 / math.sqrt(HD))
                slot = lax.broadcasted_iota(jnp.int32, scores.shape, 1)
                raised = jnp.where(slot < live, jnp.exp(scores), 0.0)
                weights = (raised / jnp.sum(raised, axis=-1, keepdims=True)).astype(BF16)
                result = jnp.dot(
                    weights, value_ref[slots, :], preferred_element_type=F32
                ).astype(BF16)
                for h in range(heads):
                    attended_ref[first : first + text_rows, h * HD : (h + 1) * HD] = result[
                        h * text_rows : (h + 1) * text_rows
                    ]

        out_ref[...] = jnp.dot(
            attended_ref[...], weight_ref[...], preferred_element_type=F32
        ).astype(BF16)

    return pl.pallas_call(
        kernel,
        grid_spec=pltpu.PrefetchScalarGridSpec(
            num_scalar_prefetch=1,
            grid=(columns // wide,),
            in_specs=[pl.BlockSpec((rows, width), lambda i, meta: (0, 0))]
            + [pl.BlockSpec(piece.shape, lambda i, meta: (0, 0)) for piece in kv_pieces]
            + [pl.BlockSpec((width, wide), lambda i, meta: (0, i))],
            out_specs=pl.BlockSpec((rows, wide), lambda i, meta: (0, i)),
            scratch_shapes=[
                pltpu.VMEM((SLOTS, HD), BF16),
                pltpu.VMEM((SLOTS, HD), BF16),
                pltpu.VMEM((rows, width), BF16),
            ],
        ),
        out_shape=jax.ShapeDtypeStruct((rows, columns), BF16),
        compiler_params=params(),
        cost_estimate=pl.CostEstimate(
            flops=2 * rows * width * (columns + 2 * BLOCK),
            bytes_accessed=2 * columns * (width + rows),
            transcendentals=rows * heads * BLOCK,
        ),
        name="attend",
    )(meta, queries, *kv_pieces, weight)


def after(value, *others):
    return lax.optimization_barrier((value, *others))[0]


def local(
    mesh_shape,
    text_state,
    tile_feats,
    w_proj,
    w_query,
    w_kv,
    w_out,
    attn_gate,
    tile_counts,
    section_table,
):
    mp_count, section_count = mesh_shape["mp"], mesh_shape["section"]
    ring = ring_order(mp_count)
    far = mp_count // 2
    sharing = mp_count // KVH
    order = [far]
    for distance in range(far - 1, 0, -1):
        order += [-distance, distance]
    order.append(0)
    index_of = {offset: index for index, offset in enumerate(order)}
    index_of[-far] = 0
    table = np.array(
        [
            [ring[(ring.index(m) + offset) % mp_count] for offset in order] + [m, s]
            for s in range(section_count)
            for m in range(mp_count)
        ],
        np.int32,
    )
    device = lax.axis_index(("section", "mp"))
    places = lax.dynamic_slice(
        jnp.asarray(table), (device, 0), (1, mp_count + 2)
    ).reshape(-1)
    starts, counts = own_samples(tile_counts, section_table, places[mp_count + 1])
    meta = jnp.concatenate([places, starts, counts])

    up_pairs = [(ring[i], ring[(i + 1) % mp_count]) for i in range(mp_count)]
    down_pairs = [(target, source) for source, target in up_pairs]

    def up(value):
        return lax.ppermute(value, "mp", up_pairs)

    def down(value):
        return lax.ppermute(value, "mp", down_pairs)

    def across(pairs):
        return [
            (s * mp_count + a, ((s + 1) % section_count) * mp_count + b)
            for s in range(section_count)
            for a, b in pairs
        ]

    def up_across(value):
        return lax.ppermute(value, ("section", "mp"), across(up_pairs))

    def down_across(value):
        return lax.ppermute(value, ("section", "mp"), across(down_pairs))

    def to_next(value):
        return lax.ppermute(
            value, "section", [(s, (s + 1) % section_count) for s in range(section_count)]
        )

    def ring_sum(part, start_up, start_down, last_up=up, last_down=down):
        hops = []
        for start, sign, move, last in (
            (start_up, 1, up, last_up),
            (start_down, -1, down, last_down),
        ):
            running = part(sign * start)
            came = []
            for distance in range(start, 1, -1):
                came.append(move(running))
                running = add(came[-1], part(sign * (distance - 1)))
            came.append(last(running))
            hops.append(came)
        return hops

    text_own = text_state[0]
    text_rows = text_own.shape[0]
    parts = 2 if text_rows % 32 == 0 else 1
    cut = text_rows // parts
    halves = [text_own[i * cut : (i + 1) * cut] for i in range(parts)]
    reach = [(far, far - 1), (far - 1, far)][:parts]
    from_below, from_above = [halves], [halves]

    def text_round(distance, *first):
        below, above = [], []
        for part, (reach_up, reach_down) in enumerate(reach):
            if distance <= reach_up:
                below.append(up(after(from_below[-1][part], *first)))
            if distance <= reach_down:
                above.append(down(after(from_above[-1][part], *first)))
        from_below.append(below)
        from_above.append(above)

    text_round(1)

    image_part = project(meta, tile_feats, w_proj, mp_count)
    feat_rows = tile_feats.shape[0]
    image_rows = feat_rows // 2
    image_halves, image_hops = [], []
    for half, (start_up, start_down) in enumerate(((far, far - 1), (far - 1, far))):

        def image_block(offset, half=half):
            return image_part[
                index_of[offset], half * image_rows : (half + 1) * image_rows
            ]

        hops = ring_sum(image_block, start_up, start_down)
        image_hops += hops
        total = image_block(0).astype(F32) + hops[0][-1].astype(F32) + hops[1][-1].astype(F32)
        image_halves.append(total.astype(BF16))
    image_cols = jnp.concatenate(image_halves, axis=0)

    for distance in range(2, far + 1):
        text_round(distance, *([hops[-2] for hops in image_hops] if distance == 2 else []))
    text_next = to_next(text_own)
    gate_next = to_next(attn_gate)

    pieces = []
    moving = image_cols
    for step in range(section_count // 2):
        pieces += [
            moving,
            lax.ppermute(moving, "section", [(s, s ^ 1) for s in range(section_count)]),
        ]
        if step + 1 < section_count // 2:
            moving = lax.ppermute(
                moving,
                "section",
                [(s, (s + 2) % section_count) for s in range(section_count)],
            )

    kv_part = key_values(meta, pieces, w_kv[0], mp_count, section_count, sharing)

    def kv_block(offset):
        return kv_part[index_of[offset]]

    hops = ring_sum(kv_block, far, far - 1)
    kv_own = (
        kv_block(0).astype(F32) + hops[0][-1].astype(F32) + hops[1][-1].astype(F32)
    ).astype(BF16)
    kv_pieces = [kv_own]
    for step in range(1, sharing):
        pairs = [
            (m, m // sharing * sharing + (m % sharing + step) % sharing) for m in range(mp_count)
        ]
        kv_pieces.append(lax.ppermute(kv_own, "mp", pairs))

    weight_query, weight_out = w_query[0], w_out[0]
    near = []
    near_queries = []
    for distance in range(1, far):
        chunks = from_below[distance] + from_above[distance]
        near += [-distance, distance]
        if distance == 1:
            chunks = chunks + halves
            near.append(0)
        near_queries.append(query(chunks, weight_query))
    near_queries = jnp.concatenate(near_queries, axis=0)
    far_queries = query(from_below[far] + from_above[far], weight_query)
    far_part = attend(
        meta, far_queries, kv_pieces, weight_out, [index_of[far]], text_rows, mp_count
    )
    near_part = attend(
        meta,
        near_queries,
        kv_pieces,
        weight_out,
        [index_of[offset] for offset in near],
        text_rows,
        mp_count,
    )

    own_first = near.index(0) * text_rows
    own_next = to_next(near_part[own_first : own_first + text_rows])
    results = []
    for part, (start_up, start_down) in enumerate(reach):

        def out_block(offset, part=part):
            if abs(offset) == far:
                return far_part[part * cut : (part + 1) * cut]
            first = near.index(offset) * text_rows + part * cut
            return near_part[first : first + cut]

        hops = ring_sum(out_block, start_up, start_down, up_across, down_across)
        rows = slice(part * cut, (part + 1) * cut)
        branch = own_next[rows].astype(F32) + hops[0][-1].astype(F32) + hops[1][-1].astype(F32)
        results.append(
            (text_next[rows].astype(F32) + jnp.tanh(gate_next[0]) * branch).astype(BF16)
        )
    return jnp.concatenate(results, axis=0)[None]


def solution(mesh):
    mesh_shape = dict(mesh.shape)

    def body(*arrays):
        return local(mesh_shape, *arrays)

    return jax.shard_map(
        body,
        mesh=mesh,
        in_specs=(
            P("section", "mp", None),
            P("section", "mp"),
            P("mp", None),
            P("section", None, "mp"),
            P("section", "mp", None),
            P("section", "mp", None),
            P("section"),
            P(),
            P(),
        ),
        out_specs=P("section", "mp", None),
        check_vma=False,
    )
```

```python
import math

import jax
import jax.numpy as jnp
import numpy as np
from jax import lax
from jax.experimental import pallas as pl
from jax.experimental.pallas import tpu as pltpu
from jax.sharding import PartitionSpec as P

HD = 128
HEADS = 32
KVH = 4
SAMP_SECTION = 4
TXT = 128
TT = 32
MAXT = 4
BLOCK = MAXT * TT
SLOTS = SAMP_SECTION * BLOCK
F32 = jnp.float32
BF16 = jnp.bfloat16
VMEM_LIMIT = 40 * 1024 * 1024


def ring_order(count):
    wide = 2 if count <= 8 else 4
    tall = count // wide
    if count < 4 or count % wide or tall % 2:
        return list(range(count))
    order = [row * wide for row in range(tall)]
    for turn, row in enumerate(reversed(range(tall))):
        columns = range(1, wide) if turn % 2 == 0 else range(wide - 1, 0, -1)
        order += [row * wide + column for column in columns]
    return order


def own_samples(tile_counts, section_table, section_id):
    samples_all = tile_counts.shape[0]
    sample_ids = jnp.arange(samples_all, dtype=jnp.int32)
    same_section = section_table[None, :] == section_table[:, None]
    before = sample_ids[None, :] < sample_ids[:, None]
    ranking = jnp.sum((same_section & before).astype(jnp.int32), axis=1)
    picked = (section_table[None, :] == section_id) & (
        ranking[None, :] == jnp.arange(SAMP_SECTION, dtype=jnp.int32)[:, None]
    )
    first_row = TT * jnp.sum(jnp.where(before, tile_counts[None, :], 0), axis=1)
    counts_own = jnp.sum(jnp.where(picked, tile_counts[None, :], 0), axis=1)
    starts_own = jnp.sum(jnp.where(picked, first_row[None, :], 0), axis=1)
    return starts_own, counts_own


def add(one, other):
    return (one.astype(F32) + other.astype(F32)).astype(BF16)


def params():
    return pltpu.CompilerParams(vmem_limit_bytes=VMEM_LIMIT)


def project(places, feats, weight, order_len, first, blocks):
    rows, depth = feats.shape
    wide = weight.shape[1] // order_len

    def kernel(places_ref, feats_ref, weight_ref, out_ref):
        out_ref[0] = jnp.dot(
            feats_ref[...], weight_ref[...], preferred_element_type=F32
        ).astype(BF16)

    return pl.pallas_call(
        kernel,
        grid_spec=pltpu.PrefetchScalarGridSpec(
            num_scalar_prefetch=1,
            grid=(blocks,),
            in_specs=[
                pl.BlockSpec((rows, depth), lambda i, places: (0, 0)),
                pl.BlockSpec((depth, wide), lambda i, places: (0, places[first + i])),
            ],
            out_specs=pl.BlockSpec((1, rows, wide), lambda i, places: (i, 0, 0)),
        ),
        out_shape=jax.ShapeDtypeStruct((blocks, rows, wide), BF16),
        compiler_params=params(),
        cost_estimate=pl.CostEstimate(
            flops=2 * rows * depth * wide * (blocks - 1),
            bytes_accessed=2 * (depth + rows) * wide * (blocks - 1),
            transcendentals=0,
        ),
        name="project",
    )(places, feats, weight)


def key_values(meta, pieces, weight, order_len, section_count, sharing):
    feat_rows = pieces[0].shape[0]
    depth, width = weight.shape
    kv_rows = SLOTS // sharing
    half_width = width // 2
    count = len(pieces)

    def kernel(meta_ref, *refs):
        piece_refs, weight_ref, out_ref, kv_ref = refs[:count], refs[count], refs[-2], refs[-1]
        section = meta_ref[order_len + 1]
        slot = lax.broadcasted_iota(jnp.int32, (BLOCK, feat_rows), 0)
        packed = lax.broadcasted_iota(jnp.int32, (BLOCK, feat_rows), 1)
        for sample in range(SAMP_SECTION):
            start = meta_ref[order_len + 2 + sample]
            live = TT * meta_ref[order_len + 2 + SAMP_SECTION + sample]
            image = jnp.zeros((BLOCK, depth), F32)
            for index in range(count):
                step, swapped = index // 2, index % 2
                origin = lax.rem(section + (section_count - 2 * step), section_count)
                if swapped:
                    origin = origin + 1 - 2 * lax.rem(origin, 2)
                chosen = (slot < live) & (packed == slot + (start - origin * feat_rows))
                image += jnp.dot(
                    chosen.astype(F32).astype(BF16),
                    piece_refs[index][...],
                    preferred_element_type=F32,
                )
            kv_ref[sample * BLOCK : (sample + 1) * BLOCK, :] = jnp.dot(
                image.astype(BF16), weight_ref[...], preferred_element_type=F32
            ).astype(BF16)
        for index in range(order_len):
            target = meta_ref[index]
            row = pl.multiple_of(lax.rem(target, sharing) * kv_rows, kv_rows)
            column = pl.multiple_of(target // sharing * HD, HD)
            out_ref[index, :, :HD] = kv_ref[pl.ds(row, kv_rows), pl.ds(column, HD)]
            out_ref[index, :, HD:] = kv_ref[
                pl.ds(row, kv_rows), pl.ds(pl.multiple_of(column + half_width, HD), HD)
            ]

    whole = pl.BlockSpec(memory_space=pltpu.VMEM)
    return pl.pallas_call(
        kernel,
        in_specs=[pl.BlockSpec(memory_space=pltpu.SMEM)] + [whole] * (count + 1),
        out_specs=whole,
        out_shape=jax.ShapeDtypeStruct((order_len, kv_rows, 2 * HD), BF16),
        scratch_shapes=[pltpu.VMEM((SLOTS, width), BF16)],
        compiler_params=params(),
        cost_estimate=pl.CostEstimate(
            flops=2 * SLOTS * depth * (width + feat_rows * count),
            bytes_accessed=2 * depth * (width + feat_rows * count),
            transcendentals=0,
        ),
        name="key_values",
    )(meta, *pieces, weight)


def query(chunks, weight):
    rows = sum(chunk.shape[0] for chunk in chunks)
    depth, width = weight.shape
    wide = min(2 * HD, width)
    count = len(chunks)

    def kernel(*refs):
        chunk_refs, weight_ref, out_ref = refs[:count], refs[count], refs[count + 1]
        rows_ref, scale_ref = refs[count + 2 :]

        @pl.when(pl.program_id(0) == 0)
        def _():
            first = 0
            for chunk_ref in chunk_refs:
                place = slice(first, first + chunk_ref.shape[0])
                chunk = chunk_ref[...]
                wider = chunk.astype(F32)
                rows_ref[place, :] = chunk
                scale_ref[place, :] = lax.rsqrt(
                    jnp.mean(wider * wider, axis=-1, keepdims=True) + 1e-05
                )
                first += chunk_ref.shape[0]

        projected = jnp.dot(rows_ref[...], weight_ref[...], preferred_element_type=F32)
        projected = projected * scale_ref[...]
        for head in range(wide // HD):
            one = projected[:, head * HD : (head + 1) * HD]
            one = one * lax.rsqrt(jnp.mean(one * one, axis=-1, keepdims=True) + 1e-06)
            out_ref[:, head * HD : (head + 1) * HD] = one.astype(BF16)

    return pl.pallas_call(
        kernel,
        grid=(width // wide,),
        in_specs=[pl.BlockSpec(chunk.shape, lambda i: (0, 0)) for chunk in chunks]
        + [pl.BlockSpec((depth, wide), lambda i: (0, i))],
        out_specs=pl.BlockSpec((rows, wide), lambda i: (0, i)),
        out_shape=jax.ShapeDtypeStruct((rows, width), BF16),
        scratch_shapes=[pltpu.VMEM((rows, depth), BF16), pltpu.VMEM((rows, 1), F32)],
        compiler_params=params(),
        cost_estimate=pl.CostEstimate(
            flops=2 * rows * depth * width,
            bytes_accessed=2 * depth * (width + rows),
            transcendentals=0,
        ),
        name="query",
    )(*chunks, weight)


def attend(meta, queries, kv_pieces, weight, indices, text_rows, order_len):
    rows, width = queries.shape
    heads = width // HD
    sharing = len(kv_pieces)
    kv_rows = SLOTS // sharing
    columns = weight.shape[1]
    wide = min(1024, columns)

    def kernel(meta_ref, query_ref, *refs):
        kv_refs, weight_ref, out_ref = refs[:sharing], refs[sharing], refs[sharing + 1]
        key_ref, value_ref, attended_ref = refs[sharing + 2 :]

        @pl.when(pl.program_id(0) == 0)
        def _():
            mine = lax.rem(meta_ref[order_len], sharing)
            for step in range(sharing):
                row = pl.multiple_of(
                    lax.rem(mine + sharing - step, sharing) * kv_rows, kv_rows
                )
                keys = kv_refs[step][:, :HD].astype(F32)
                keys = keys * lax.rsqrt(jnp.mean(keys * keys, axis=-1, keepdims=True) + 1e-06)
                key_ref[pl.ds(row, kv_rows), :] = keys.astype(BF16)
                value_ref[pl.ds(row, kv_rows), :] = kv_refs[step][:, HD:]
            for place, index in enumerate(indices):
                sample = meta_ref[index] * text_rows // TXT
                slots = pl.ds(pl.multiple_of(sample * BLOCK, BLOCK), BLOCK)
                live = TT * meta_ref[order_len + 2 + SAMP_SECTION + sample]
                first = place * text_rows
                own = query_ref[first : first + text_rows, :]
                stacked = jnp.concatenate(
                    [own[:, h * HD : (h + 1) * HD] for h in range(heads)], axis=0
                )
                scores = lax.dot_general(
                    stacked,
                    key_ref[slots, :],
                    (((1,), (1,)), ((), ())),
                    preferred_element_type=F32,
                ) * (1.0 / math.sqrt(HD))
                slot = lax.broadcasted_iota(jnp.int32, scores.shape, 1)
                raised = jnp.where(slot < live, jnp.exp(scores), 0.0)
                weights = (raised / jnp.sum(raised, axis=-1, keepdims=True)).astype(BF16)
                result = jnp.dot(
                    weights, value_ref[slots, :], preferred_element_type=F32
                ).astype(BF16)
                for h in range(heads):
                    attended_ref[first : first + text_rows, h * HD : (h + 1) * HD] = result[
                        h * text_rows : (h + 1) * text_rows
                    ]

        out_ref[...] = jnp.dot(
            attended_ref[...], weight_ref[...], preferred_element_type=F32
        ).astype(BF16)

    return pl.pallas_call(
        kernel,
        grid_spec=pltpu.PrefetchScalarGridSpec(
            num_scalar_prefetch=1,
            grid=(columns // wide,),
            in_specs=[pl.BlockSpec((rows, width), lambda i, meta: (0, 0))]
            + [pl.BlockSpec(piece.shape, lambda i, meta: (0, 0)) for piece in kv_pieces]
            + [pl.BlockSpec((width, wide), lambda i, meta: (0, i))],
            out_specs=pl.BlockSpec((rows, wide), lambda i, meta: (0, i)),
            scratch_shapes=[
                pltpu.VMEM((SLOTS, HD), BF16),
                pltpu.VMEM((SLOTS, HD), BF16),
                pltpu.VMEM((rows, width), BF16),
            ],
        ),
        out_shape=jax.ShapeDtypeStruct((rows, columns), BF16),
        compiler_params=params(),
        cost_estimate=pl.CostEstimate(
            flops=2 * rows * width * (columns + 2 * BLOCK),
            bytes_accessed=2 * columns * (width + rows),
            transcendentals=rows * heads * BLOCK,
        ),
        name="attend",
    )(meta, queries, *kv_pieces, weight)


def after(value, *others):
    return lax.optimization_barrier((value, *others))[0]


def local(
    mesh_shape,
    text_state,
    tile_feats,
    w_proj,
    w_query,
    w_kv,
    w_out,
    attn_gate,
    tile_counts,
    section_table,
):
    mp_count, section_count = mesh_shape["mp"], mesh_shape["section"]
    ring = ring_order(mp_count)
    far = mp_count // 2
    sharing = mp_count // KVH
    order = [far]
    for distance in range(far - 1, 0, -1):
        order += [-distance, distance]
    order.append(0)
    index_of = {offset: index for index, offset in enumerate(order)}
    index_of[-far] = 0
    table = np.array(
        [
            [ring[(ring.index(m) + offset) % mp_count] for offset in order] + [m, s]
            for s in range(section_count)
            for m in range(mp_count)
        ],
        np.int32,
    )
    device = lax.axis_index(("section", "mp"))
    places = lax.dynamic_slice(
        jnp.asarray(table), (device, 0), (1, mp_count + 2)
    ).reshape(-1)
    starts, counts = own_samples(tile_counts, section_table, places[mp_count + 1])
    meta = jnp.concatenate([places, starts, counts])

    up_pairs = [(ring[i], ring[(i + 1) % mp_count]) for i in range(mp_count)]
    down_pairs = [(target, source) for source, target in up_pairs]

    def up(value):
        return lax.ppermute(value, "mp", up_pairs)

    def down(value):
        return lax.ppermute(value, "mp", down_pairs)

    def across(pairs):
        return [
            (s * mp_count + a, ((s + 1) % section_count) * mp_count + b)
            for s in range(section_count)
            for a, b in pairs
        ]

    def up_across(value):
        return lax.ppermute(value, ("section", "mp"), across(up_pairs))

    def down_across(value):
        return lax.ppermute(value, ("section", "mp"), across(down_pairs))

    def to_next(value):
        return lax.ppermute(
            value, "section", [(s, (s + 1) % section_count) for s in range(section_count)]
        )

    def ring_sum(part, start_up, start_down, last_up=up, last_down=down, tie=None):
        tie = tie or (lambda left, value: value)
        hops = []
        for start, sign, move, last in (
            (start_up, 1, up, last_up),
            (start_down, -1, down, last_down),
        ):
            running = part(sign * start)
            came = []
            for distance in range(start, 1, -1):
                came.append(move(tie(distance, running)))
                running = add(came[-1], part(sign * (distance - 1)))
            came.append(last(tie(1, running)))
            hops.append(came)
        return hops

    text_own = text_state[0]
    text_rows = text_own.shape[0]
    parts = 2 if text_rows % 32 == 0 else 1
    cut = text_rows // parts
    reach = [(far, far - 1), (far - 1, far)][:parts]
    text_next = to_next(text_own)
    gate_next = to_next(attn_gate)
    from_below, from_above = [text_own], [text_own]

    def text_round(*first):
        from_below.append(up(after(from_below[-1], *first)))
        from_above.append(down(after(from_above[-1], *first)))

    text_round()

    image_far = project(places, tile_feats, w_proj, mp_count, 0, 1)
    image_near = project(places, tile_feats, w_proj, mp_count, 1, mp_count - 1)
    feat_rows = tile_feats.shape[0]
    image_rows = feat_rows // 2
    image_halves = []
    for half, (start_up, start_down) in enumerate(((far, far - 1), (far - 1, far))):

        def image_block(offset, half=half):
            index = index_of[offset]
            rows = slice(half * image_rows, (half + 1) * image_rows)
            return image_far[0, rows] if index == 0 else image_near[index - 1, rows]

        def image_tie(left, value):
            if left == far - 2:
                return after(value, from_below[1], from_above[1], text_next, gate_next)
            return value

        hops = ring_sum(image_block, start_up, start_down, tie=image_tie)
        total = image_block(0).astype(F32) + hops[0][-1].astype(F32) + hops[1][-1].astype(F32)
        image_halves.append(total.astype(BF16))
    image_cols = jnp.concatenate(image_halves, axis=0)

    pieces = []
    moving = image_cols
    for step in range(section_count // 2):
        pieces += [
            moving,
            lax.ppermute(moving, "section", [(s, s ^ 1) for s in range(section_count)]),
        ]
        if step + 1 < section_count // 2:
            moving = lax.ppermute(
                moving,
                "section",
                [(s, (s + 2) % section_count) for s in range(section_count)],
            )

    for distance in range(2, far):
        text_round(*([image_cols] if distance == 2 else []))
    kv_part = key_values(meta, pieces, w_kv[0], mp_count, section_count, sharing)
    if far > 2:
        kv_part = after(kv_part, from_below[2], from_above[2])

    def kv_block(offset):
        return kv_part[index_of[offset]]

    hops = ring_sum(kv_block, far, far - 1)
    kv_own = (
        kv_block(0).astype(F32) + hops[0][-1].astype(F32) + hops[1][-1].astype(F32)
    ).astype(BF16)
    kv_pieces = [kv_own]
    for step in range(1, sharing):
        pairs = [
            (m, m // sharing * sharing + (m % sharing + step) % sharing) for m in range(mp_count)
        ]
        kv_pieces.append(lax.ppermute(kv_own, "mp", pairs))

    weight_query, weight_out = w_query[0], w_out[0]
    near = []
    near_queries = []
    for distance in range(1, far):
        chunks = [from_below[distance], from_above[distance]]
        near += [-distance, distance]
        if distance == 1:
            chunks.append(text_own)
            near.append(0)
        near_queries.append(query(chunks, weight_query))
    near_queries = jnp.concatenate(near_queries, axis=0)
    far_chunks = [up(from_below[-1][:cut])]
    if parts == 2:
        far_chunks.append(down(from_above[-1][cut:]))
    far_queries = query(far_chunks, weight_query)
    far_part = attend(
        meta, far_queries, kv_pieces, weight_out, [index_of[far]], text_rows, mp_count
    )
    near_part = attend(
        meta,
        near_queries,
        kv_pieces,
        weight_out,
        [index_of[offset] for offset in near],
        text_rows,
        mp_count,
    )

    own_first = near.index(0) * text_rows
    own_next = to_next(near_part[own_first : own_first + text_rows])
    results = []
    for part, (start_up, start_down) in enumerate(reach):

        def out_block(offset, part=part):
            if abs(offset) == far:
                return far_part[part * cut : (part + 1) * cut]
            first = near.index(offset) * text_rows + part * cut
            return near_part[first : first + cut]

        def out_tie(left, value):
            return after(value, own_next) if left == min(2, far - 1) else value

        hops = ring_sum(out_block, start_up, start_down, up_across, down_across, out_tie)
        rows = slice(part * cut, (part + 1) * cut)
        branch = own_next[rows].astype(F32) + hops[0][-1].astype(F32) + hops[1][-1].astype(F32)
        results.append(
            (text_next[rows].astype(F32) + jnp.tanh(gate_next[0]) * branch).astype(BF16)
        )
    return jnp.concatenate(results, axis=0)[None]


def solution(mesh):
    mesh_shape = dict(mesh.shape)

    def body(*arrays):
        return local(mesh_shape, *arrays)

    return jax.shard_map(
        body,
        mesh=mesh,
        in_specs=(
            P("section", "mp", None),
            P("section", "mp"),
            P("mp", None),
            P("section", None, "mp"),
            P("section", "mp", None),
            P("section", "mp", None),
            P("section"),
            P(),
            P(),
        ),
        out_specs=P("section", "mp", None),
        check_vma=False,
    )
```

```python
import math

import jax
import jax.numpy as jnp
import numpy as np
from jax import lax
from jax.experimental import pallas as pl
from jax.experimental.pallas import tpu as pltpu
from jax.sharding import PartitionSpec as P

HD = 128
HEADS = 32
KVH = 4
SAMP_SECTION = 4
TXT = 128
TT = 32
MAXT = 4
BLOCK = MAXT * TT
SLOTS = SAMP_SECTION * BLOCK
F32 = jnp.float32
BF16 = jnp.bfloat16
VMEM_LIMIT = 40 * 1024 * 1024
VMEM_MOST = 56 * 1024 * 1024
VMEM_SMALL = 16 * 1024 * 1024


def ring_order(count):
    wide = 2 if count <= 8 else 4
    tall = count // wide
    if count < 4 or count % wide or tall % 2:
        return list(range(count))
    order = [row * wide for row in range(tall)]
    for turn, row in enumerate(reversed(range(tall))):
        columns = range(1, wide) if turn % 2 == 0 else range(wide - 1, 0, -1)
        order += [row * wide + column for column in columns]
    return order


def own_samples(tile_counts, section_table, section_id):
    samples_all = tile_counts.shape[0]
    sample_ids = jnp.arange(samples_all, dtype=jnp.int32)
    same_section = section_table[None, :] == section_table[:, None]
    before = sample_ids[None, :] < sample_ids[:, None]
    ranking = jnp.sum((same_section & before).astype(jnp.int32), axis=1)
    picked = (section_table[None, :] == section_id) & (
        ranking[None, :] == jnp.arange(SAMP_SECTION, dtype=jnp.int32)[:, None]
    )
    first_row = TT * jnp.sum(jnp.where(before, tile_counts[None, :], 0), axis=1)
    counts_own = jnp.sum(jnp.where(picked, tile_counts[None, :], 0), axis=1)
    starts_own = jnp.sum(jnp.where(picked, first_row[None, :], 0), axis=1)
    return starts_own, counts_own


def add(one, other):
    return (one.astype(F32) + other.astype(F32)).astype(BF16)


def params(limit=VMEM_LIMIT):
    return pltpu.CompilerParams(vmem_limit_bytes=limit)


def total_of(groups):
    parts, count = len(groups), len(groups[0])
    part_rows, columns = groups[0][0].shape
    rows = parts * part_rows
    wide = columns // 4 if columns % 512 == 0 else columns

    def kernel(*refs):
        for part in range(parts):
            total = refs[part * count][...].astype(F32)
            for ref in refs[part * count + 1 : (part + 1) * count]:
                total += ref[...].astype(F32)
            refs[-1][part * part_rows : (part + 1) * part_rows, :] = total.astype(BF16)

    return pl.pallas_call(
        kernel,
        grid=(columns // wide,),
        in_specs=[pl.BlockSpec((part_rows, wide), lambda i: (0, i))] * (parts * count),
        out_specs=pl.BlockSpec((rows, wide), lambda i: (0, i)),
        out_shape=jax.ShapeDtypeStruct((rows, columns), BF16),
        compiler_params=params(VMEM_SMALL),
        name="total_of",
    )(*[value for group in groups for value in group])


def finish(gate, text, own, arrivals):
    rows, columns = text.shape
    parts = len(arrivals)
    part_rows = rows // parts
    wide = columns // 4
    flat = [value for came in arrivals for value in came]
    count = len(flat) // parts

    def kernel(gate_ref, text_ref, own_ref, *refs):
        factor = jnp.tanh(gate_ref[...])
        for part in range(parts):
            place = slice(part * part_rows, (part + 1) * part_rows)
            branch = own_ref[place, :].astype(F32)
            for ref in refs[part * count : (part + 1) * count]:
                branch += ref[...].astype(F32)
            refs[-1][0, place, :] = (text_ref[place, :].astype(F32) + factor * branch).astype(
                BF16
            )

    return pl.pallas_call(
        kernel,
        grid=(columns // wide,),
        in_specs=[pl.BlockSpec((1, 1), lambda i: (0, 0))]
        + [pl.BlockSpec((rows, wide), lambda i: (0, i))] * 2
        + [pl.BlockSpec((part_rows, wide), lambda i: (0, i))] * len(flat),
        out_specs=pl.BlockSpec((1, rows, wide), lambda i: (0, 0, i)),
        out_shape=jax.ShapeDtypeStruct((1, rows, columns), BF16),
        compiler_params=params(VMEM_SMALL),
        name="finish",
    )(gate.reshape(1, 1), text, own, *flat)


def project(places, feats, weight, order_len, first, blocks):
    rows, depth = feats.shape
    half = rows // 2
    wide = weight.shape[1] // order_len

    def kernel(places_ref, feats_ref, weight_ref, *out_refs):
        product = jnp.dot(
            feats_ref[...], weight_ref[...], preferred_element_type=F32
        ).astype(BF16)
        for block in range(blocks):

            @pl.when(pl.program_id(0) == block)
            def _():
                out_refs[2 * block][...] = product[:half]
                out_refs[2 * block + 1][...] = product[half:]

    halves = pl.pallas_call(
        kernel,
        grid_spec=pltpu.PrefetchScalarGridSpec(
            num_scalar_prefetch=1,
            grid=(blocks,),
            in_specs=[
                pl.BlockSpec((rows, depth), lambda i, places: (0, 0)),
                pl.BlockSpec((depth, wide), lambda i, places: (0, places[first + i])),
            ],
            out_specs=[pl.BlockSpec((half, wide), lambda i, places: (0, 0))] * (2 * blocks),
        ),
        out_shape=[jax.ShapeDtypeStruct((half, wide), BF16)] * (2 * blocks),
        compiler_params=params(),
        cost_estimate=pl.CostEstimate(
            flops=2 * rows * depth * wide * (blocks - 1),
            bytes_accessed=2 * (depth + rows) * wide * (blocks - 1),
            transcendentals=0,
        ),
        name="project",
    )(places, feats, weight)
    return [halves[2 * block : 2 * block + 2] for block in range(blocks)]


def key_values(meta, pieces, weight, order_len, section_count, sharing):
    feat_rows = pieces[0].shape[0]
    depth, width = weight.shape
    kv_rows = SLOTS // sharing
    half_width = width // 2
    count = len(pieces)

    def kernel(meta_ref, *refs):
        piece_refs, weight_ref = refs[:count], refs[count]
        out_refs, kv_ref = refs[count + 1 : -1], refs[-1]
        section = meta_ref[order_len + 1]
        slot = lax.broadcasted_iota(jnp.int32, (BLOCK, feat_rows), 0)
        packed = lax.broadcasted_iota(jnp.int32, (BLOCK, feat_rows), 1)
        for sample in range(SAMP_SECTION):
            start = meta_ref[order_len + 2 + sample]
            live = TT * meta_ref[order_len + 2 + SAMP_SECTION + sample]
            image = jnp.zeros((BLOCK, depth), F32)
            for index in range(count):
                step, swapped = index // 2, index % 2
                origin = lax.rem(section + (section_count - 2 * step), section_count)
                if swapped:
                    origin = origin + 1 - 2 * lax.rem(origin, 2)
                chosen = (slot < live) & (packed == slot + (start - origin * feat_rows))
                image += jnp.dot(
                    chosen.astype(F32).astype(BF16),
                    piece_refs[index][...],
                    preferred_element_type=F32,
                )
            kv_ref[sample * BLOCK : (sample + 1) * BLOCK, :] = jnp.dot(
                image.astype(BF16), weight_ref[...], preferred_element_type=F32
            ).astype(BF16)
        for index in range(order_len):
            target = meta_ref[index]
            row = pl.multiple_of(lax.rem(target, sharing) * kv_rows, kv_rows)
            column = pl.multiple_of(target // sharing * HD, HD)
            out_refs[index][:, :HD] = kv_ref[pl.ds(row, kv_rows), pl.ds(column, HD)]
            out_refs[index][:, HD:] = kv_ref[
                pl.ds(row, kv_rows), pl.ds(pl.multiple_of(column + half_width, HD), HD)
            ]

    whole = pl.BlockSpec(memory_space=pltpu.VMEM)
    return pl.pallas_call(
        kernel,
        in_specs=[pl.BlockSpec(memory_space=pltpu.SMEM)] + [whole] * (count + 1),
        out_specs=[whole] * order_len,
        out_shape=[jax.ShapeDtypeStruct((kv_rows, 2 * HD), BF16)] * order_len,
        scratch_shapes=[pltpu.VMEM((SLOTS, width), BF16)],
        compiler_params=params(),
        cost_estimate=pl.CostEstimate(
            flops=2 * SLOTS * depth * (width + feat_rows * count),
            bytes_accessed=2 * depth * (width + feat_rows * count),
            transcendentals=0,
        ),
        name="key_values",
    )(meta, *pieces, weight)


def query(chunks, weight):
    rows = sum(chunk.shape[0] for chunk in chunks)
    depth, width = weight.shape
    wide = min(2 * HD, width)
    count = len(chunks)

    def kernel(*refs):
        chunk_refs, weight_ref, out_ref = refs[:count], refs[count], refs[count + 1]
        rows_ref, scale_ref = refs[count + 2 :]

        @pl.when(pl.program_id(0) == 0)
        def _():
            first = 0
            for chunk_ref in chunk_refs:
                place = slice(first, first + chunk_ref.shape[0])
                chunk = chunk_ref[...]
                wider = chunk.astype(F32)
                rows_ref[place, :] = chunk
                scale_ref[place, :] = lax.rsqrt(
                    jnp.mean(wider * wider, axis=-1, keepdims=True) + 1e-05
                )
                first += chunk_ref.shape[0]

        projected = jnp.dot(rows_ref[...], weight_ref[...], preferred_element_type=F32)
        projected = projected * scale_ref[...]
        for head in range(wide // HD):
            one = projected[:, head * HD : (head + 1) * HD]
            one = one * lax.rsqrt(jnp.mean(one * one, axis=-1, keepdims=True) + 1e-06)
            out_ref[:, head * HD : (head + 1) * HD] = one.astype(BF16)

    return pl.pallas_call(
        kernel,
        grid=(width // wide,),
        in_specs=[pl.BlockSpec(chunk.shape, lambda i: (0, 0)) for chunk in chunks]
        + [pl.BlockSpec((depth, wide), lambda i: (0, i))],
        out_specs=pl.BlockSpec((rows, wide), lambda i: (0, i)),
        out_shape=jax.ShapeDtypeStruct((rows, width), BF16),
        scratch_shapes=[pltpu.VMEM((rows, depth), BF16), pltpu.VMEM((rows, 1), F32)],
        compiler_params=params(),
        cost_estimate=pl.CostEstimate(
            flops=2 * rows * depth * width,
            bytes_accessed=2 * depth * (width + rows),
            transcendentals=0,
        ),
        name="query",
    )(*chunks, weight)


def attend(meta, queries, kv_pieces, weight, indices, sizes, order_len):
    text_rows = queries.shape[0] // len(indices)
    rows, width = queries.shape
    heads = width // HD
    sharing = len(kv_pieces)
    kv_rows = SLOTS // sharing
    columns = weight.shape[1]
    wide = min(1024, columns)

    def kernel(meta_ref, query_ref, *refs):
        kv_refs, weight_ref = refs[:sharing], refs[sharing]
        out_refs = refs[sharing + 1 : -3]
        key_ref, value_ref, attended_ref = refs[-3:]

        @pl.when(pl.program_id(0) == 0)
        def _():
            mine = lax.rem(meta_ref[order_len], sharing)
            for step in range(sharing):
                row = pl.multiple_of(
                    lax.rem(mine + sharing - step, sharing) * kv_rows, kv_rows
                )
                keys = kv_refs[step][:, :HD].astype(F32)
                keys = keys * lax.rsqrt(jnp.mean(keys * keys, axis=-1, keepdims=True) + 1e-06)
                key_ref[pl.ds(row, kv_rows), :] = keys.astype(BF16)
                value_ref[pl.ds(row, kv_rows), :] = kv_refs[step][:, HD:]
            for place, index in enumerate(indices):
                sample = meta_ref[index] * text_rows // TXT
                slots = pl.ds(pl.multiple_of(sample * BLOCK, BLOCK), BLOCK)
                live = TT * meta_ref[order_len + 2 + SAMP_SECTION + sample]
                first = place * text_rows
                own = query_ref[first : first + text_rows, :]
                stacked = jnp.concatenate(
                    [own[:, h * HD : (h + 1) * HD] for h in range(heads)], axis=0
                )
                scores = lax.dot_general(
                    stacked,
                    key_ref[slots, :],
                    (((1,), (1,)), ((), ())),
                    preferred_element_type=F32,
                ) * (1.0 / math.sqrt(HD))
                slot = lax.broadcasted_iota(jnp.int32, scores.shape, 1)
                raised = jnp.where(slot < live, jnp.exp(scores), 0.0)
                weights = (raised / jnp.sum(raised, axis=-1, keepdims=True)).astype(BF16)
                result = jnp.dot(
                    weights, value_ref[slots, :], preferred_element_type=F32
                ).astype(BF16)
                for h in range(heads):
                    attended_ref[first : first + text_rows, h * HD : (h + 1) * HD] = result[
                        h * text_rows : (h + 1) * text_rows
                    ]

        product = jnp.dot(
            attended_ref[...], weight_ref[...], preferred_element_type=F32
        ).astype(BF16)
        first = 0
        for out_ref, size in zip(out_refs, sizes):
            out_ref[...] = product[first : first + size]
            first += size

    return pl.pallas_call(
        kernel,
        grid_spec=pltpu.PrefetchScalarGridSpec(
            num_scalar_prefetch=1,
            grid=(columns // wide,),
            in_specs=[pl.BlockSpec((rows, width), lambda i, meta: (0, 0))]
            + [pl.BlockSpec(piece.shape, lambda i, meta: (0, 0)) for piece in kv_pieces]
            + [pl.BlockSpec((width, wide), lambda i, meta: (0, i))],
            out_specs=[pl.BlockSpec((size, wide), lambda i, meta: (0, i)) for size in sizes],
            scratch_shapes=[
                pltpu.VMEM((SLOTS, HD), BF16),
                pltpu.VMEM((SLOTS, HD), BF16),
                pltpu.VMEM((rows, width), BF16),
            ],
        ),
        out_shape=[jax.ShapeDtypeStruct((size, columns), BF16) for size in sizes],
        compiler_params=params(VMEM_MOST),
        cost_estimate=pl.CostEstimate(
            flops=2 * rows * width * (columns + 2 * BLOCK),
            bytes_accessed=2 * columns * (width + rows),
            transcendentals=rows * heads * BLOCK,
        ),
        name="attend",
    )(meta, queries, *kv_pieces, weight)


def after(value, *others):
    return lax.optimization_barrier((value, *others))[0]


def local(
    mesh_shape,
    text_state,
    tile_feats,
    w_proj,
    w_query,
    w_kv,
    w_out,
    attn_gate,
    tile_counts,
    section_table,
):
    mp_count, section_count = mesh_shape["mp"], mesh_shape["section"]
    ring = ring_order(mp_count)
    far = mp_count // 2
    sharing = mp_count // KVH
    order = [far]
    for distance in range(far - 1, 0, -1):
        order += [-distance, distance]
    order.append(0)
    index_of = {offset: index for index, offset in enumerate(order)}
    index_of[-far] = 0
    table = np.array(
        [
            [ring[(ring.index(m) + offset) % mp_count] for offset in order] + [m, s]
            for s in range(section_count)
            for m in range(mp_count)
        ],
        np.int32,
    )
    device = lax.axis_index(("section", "mp"))
    places = lax.dynamic_slice(
        jnp.asarray(table), (device, 0), (1, mp_count + 2)
    ).reshape(-1)
    starts, counts = own_samples(tile_counts, section_table, places[mp_count + 1])
    meta = jnp.concatenate([places, starts, counts])

    up_pairs = [(ring[i], ring[(i + 1) % mp_count]) for i in range(mp_count)]
    down_pairs = [(target, source) for source, target in up_pairs]

    def up(value):
        return lax.ppermute(value, "mp", up_pairs)

    def down(value):
        return lax.ppermute(value, "mp", down_pairs)

    def across(pairs):
        return [
            (s * mp_count + a, ((s + 1) % section_count) * mp_count + b)
            for s in range(section_count)
            for a, b in pairs
        ]

    def up_across(value):
        return lax.ppermute(value, ("section", "mp"), across(up_pairs))

    def down_across(value):
        return lax.ppermute(value, ("section", "mp"), across(down_pairs))

    def to_next(value):
        return lax.ppermute(
            value, "section", [(s, (s + 1) % section_count) for s in range(section_count)]
        )

    def ring_sum(part, start_up, start_down, last_up=up, last_down=down, tie=None):
        tie = tie or (lambda left, value: value)
        arrived = []
        for start, sign, move, last in (
            (start_up, 1, up, last_up),
            (start_down, -1, down, last_down),
        ):
            running = part(sign * start)
            for distance in range(start, 1, -1):
                running = add(move(tie(distance, running)), part(sign * (distance - 1)))
            arrived.append(last(tie(1, running)))
        return arrived

    text_own = text_state[0]
    text_rows = text_own.shape[0]
    parts = 2 if text_rows % 32 == 0 else 1
    cut = text_rows // parts
    reach = [(far, far - 1), (far - 1, far)][:parts]
    text_next = to_next(text_own)
    gate_next = to_next(attn_gate)
    from_below, from_above = [text_own], [text_own]

    def text_round(*first):
        from_below.append(up(after(from_below[-1], *first)))
        from_above.append(down(after(from_above[-1], *first)))

    text_round()

    image_parts = project(places, tile_feats, w_proj, mp_count, 0, 1)
    image_parts += project(places, tile_feats, w_proj, mp_count, 1, mp_count - 1)
    image_arrivals = []
    for half, (start_up, start_down) in enumerate(((far, far - 1), (far - 1, far))):

        def image_block(offset, half=half):
            return image_parts[index_of[offset]][half]

        def image_tie(left, value):
            if left == min(2, far - 1):
                return after(value, from_below[1], from_above[1])
            if left == 1:
                return after(value, text_next, gate_next)
            return value

        image_arrivals.append(
            [image_block(0)] + ring_sum(image_block, start_up, start_down, tie=image_tie)
        )
    image_cols = total_of(image_arrivals)

    pieces = []
    moving = image_cols
    for step in range(section_count // 2):
        pieces += [
            moving,
            lax.ppermute(moving, "section", [(s, s ^ 1) for s in range(section_count)]),
        ]
        if step + 1 < section_count // 2:
            moving = lax.ppermute(
                moving,
                "section",
                [(s, (s + 2) % section_count) for s in range(section_count)],
            )

    for distance in range(2, far):
        text_round(*([image_cols] if distance == 2 else []))
    far_chunks = [up(from_below[-1][:cut])]
    if parts == 2:
        far_chunks.append(down(from_above[-1][cut:]))

    weight_query, weight_out = w_query[0], w_out[0]
    near = [-1, 1, 0]
    near_queries = [query([from_below[1], from_above[1], text_own], weight_query)]
    kv_part = list(
        key_values(
            after(meta, near_queries[0]), pieces, w_kv[0], mp_count, section_count, sharing
        )
    )
    if far > 2:
        kv_part[0] = after(kv_part[0], from_below[2], from_above[2])

    def kv_block(offset):
        return kv_part[index_of[offset]]

    def kv_tie(left, value):
        if left == min(2, far - 1):
            return after(value, *from_below[3:], *from_above[3:])
        return value

    came = ring_sum(kv_block, far, far - 1, tie=kv_tie)
    kv_own = (
        kv_block(0).astype(F32) + came[0].astype(F32) + came[1].astype(F32)
    ).astype(BF16)
    for distance in range(2, far):
        near += [-distance, distance]
        near_queries.append(query([from_below[distance], from_above[distance]], weight_query))
    kv_own = after(kv_own, *far_chunks, *near_queries)
    kv_pieces = [kv_own]
    for step in range(1, sharing):
        pairs = [
            (m, m // sharing * sharing + (m % sharing + step) % sharing) for m in range(mp_count)
        ]
        kv_pieces.append(lax.ppermute(kv_own, "mp", pairs))

    near_queries = jnp.concatenate(near_queries, axis=0)
    far_queries = query(far_chunks, weight_query)
    out_parts = {}
    far_part = attend(
        meta, far_queries, kv_pieces, weight_out, [index_of[far]], [cut] * parts, mp_count
    )
    out_parts[far] = out_parts[-far] = far_part
    sizes = [size for o in near for size in ([cut] * parts if o else [text_rows])]
    near_part = attend(
        meta,
        after(near_queries, *far_part),
        kv_pieces,
        weight_out,
        [index_of[offset] for offset in near],
        sizes,
        mp_count,
    )
    for offset in near:
        count = parts if offset else 1
        out_parts[offset], near_part = near_part[:count], near_part[count:]

    own_next = to_next(out_parts[0][0])
    branch_arrivals = []
    for part, (start_up, start_down) in enumerate(reach):

        def out_block(offset, part=part):
            return out_parts[offset][part]

        def out_tie(left, value, part=part):
            if left == min(2, far - 1) and part == 0:
                return after(value, own_next)
            return value

        branch_arrivals.append(
            ring_sum(out_block, start_up, start_down, up_across, down_across, out_tie)
        )
    return finish(gate_next, text_next, own_next, branch_arrivals)


def solution(mesh):
    mesh_shape = dict(mesh.shape)

    def body(*arrays):
        return local(mesh_shape, *arrays)

    return jax.shard_map(
        body,
        mesh=mesh,
        in_specs=(
            P("section", "mp", None),
            P("section", "mp"),
            P("mp", None),
            P("section", None, "mp"),
            P("section", "mp", None),
            P("section", "mp", None),
            P("section"),
            P(),
            P(),
        ),
        out_specs=P("section", "mp", None),
        check_vma=False,
    )
```

```python
import math

import jax
import jax.numpy as jnp
import numpy as np
from jax import lax
from jax.experimental import pallas as pl
from jax.experimental.pallas import tpu as pltpu
from jax.sharding import PartitionSpec as P

HD = 128
HEADS = 32
KVH = 4
SAMP_SECTION = 4
TXT = 128
TT = 32
MAXT = 4
BLOCK = MAXT * TT
SLOTS = SAMP_SECTION * BLOCK
F32 = jnp.float32
BF16 = jnp.bfloat16
VMEM_LIMIT = 40 * 1024 * 1024
QUICK = pl.CostEstimate(flops=1, bytes_accessed=1, transcendentals=0)
VMEM_MOST = 56 * 1024 * 1024
VMEM_SMALL = 16 * 1024 * 1024


def ring_order(count):
    wide = 2 if count <= 8 else 4
    tall = count // wide
    if count < 4 or count % wide or tall % 2:
        return list(range(count))
    order = [row * wide for row in range(tall)]
    for turn, row in enumerate(reversed(range(tall))):
        columns = range(1, wide) if turn % 2 == 0 else range(wide - 1, 0, -1)
        order += [row * wide + column for column in columns]
    return order


def own_samples(tile_counts, section_table, section_id):
    samples_all = tile_counts.shape[0]
    sample_ids = jnp.arange(samples_all, dtype=jnp.int32)
    same_section = section_table[None, :] == section_table[:, None]
    before = sample_ids[None, :] < sample_ids[:, None]
    ranking = jnp.sum((same_section & before).astype(jnp.int32), axis=1)
    picked = (section_table[None, :] == section_id) & (
        ranking[None, :] == jnp.arange(SAMP_SECTION, dtype=jnp.int32)[:, None]
    )
    first_row = TT * jnp.sum(jnp.where(before, tile_counts[None, :], 0), axis=1)
    counts_own = jnp.sum(jnp.where(picked, tile_counts[None, :], 0), axis=1)
    starts_own = jnp.sum(jnp.where(picked, first_row[None, :], 0), axis=1)
    return starts_own, counts_own


def add(one, other):
    return (one.astype(F32) + other.astype(F32)).astype(BF16)


def params(limit=VMEM_LIMIT):
    return pltpu.CompilerParams(vmem_limit_bytes=limit)


def total_of(groups):
    parts, count = len(groups), len(groups[0])
    part_rows, columns = groups[0][0].shape
    rows = parts * part_rows

    def kernel(*refs):
        for part in range(parts):
            total = refs[part * count][...].astype(F32)
            for ref in refs[part * count + 1 : (part + 1) * count]:
                total += ref[...].astype(F32)
            refs[-1][part * part_rows : (part + 1) * part_rows, :] = total.astype(BF16)

    return pl.pallas_call(
        kernel,
        in_specs=[pl.BlockSpec(memory_space=pltpu.VMEM)] * (parts * count),
        out_specs=pl.BlockSpec(memory_space=pltpu.VMEM),
        out_shape=jax.ShapeDtypeStruct((rows, columns), BF16),
        compiler_params=params(VMEM_SMALL),
        cost_estimate=QUICK,
        name="total_of",
    )(*[value for group in groups for value in group])


def finish(gate, text, own, arrivals):
    rows, columns = text.shape
    parts = len(arrivals)
    part_rows = rows // parts
    flat = [value for came in arrivals for value in came]
    count = len(flat) // parts

    def kernel(gate_ref, text_ref, own_ref, *refs):
        factor = jnp.tanh(gate_ref[...])
        for part in range(parts):
            place = slice(part * part_rows, (part + 1) * part_rows)
            branch = own_ref[place, :].astype(F32)
            for ref in refs[part * count : (part + 1) * count]:
                branch += ref[...].astype(F32)
            refs[-1][0, place, :] = (text_ref[place, :].astype(F32) + factor * branch).astype(
                BF16
            )

    return pl.pallas_call(
        kernel,
        in_specs=[pl.BlockSpec(memory_space=pltpu.VMEM)] * (3 + len(flat)),
        out_specs=pl.BlockSpec(memory_space=pltpu.VMEM),
        out_shape=jax.ShapeDtypeStruct((1, rows, columns), BF16),
        compiler_params=params(VMEM_SMALL),
        cost_estimate=QUICK,
        name="finish",
    )(gate.reshape(1, 1), text, own, *flat)


def project(places, feats, weight, order_len, first, blocks):
    rows, depth = feats.shape
    half = rows // 2
    wide = weight.shape[1] // order_len

    def kernel(places_ref, feats_ref, weight_ref, *out_refs):
        product = jnp.dot(
            feats_ref[...], weight_ref[...], preferred_element_type=F32
        ).astype(BF16)
        for block in range(blocks):

            @pl.when(pl.program_id(0) == block)
            def _():
                out_refs[2 * block][...] = product[:half]
                out_refs[2 * block + 1][...] = product[half:]

    halves = pl.pallas_call(
        kernel,
        grid_spec=pltpu.PrefetchScalarGridSpec(
            num_scalar_prefetch=1,
            grid=(blocks,),
            in_specs=[
                pl.BlockSpec((rows, depth), lambda i, places: (0, 0)),
                pl.BlockSpec((depth, wide), lambda i, places: (0, places[first + i])),
            ],
            out_specs=[pl.BlockSpec((half, wide), lambda i, places: (0, 0))] * (2 * blocks),
        ),
        out_shape=[jax.ShapeDtypeStruct((half, wide), BF16)] * (2 * blocks),
        compiler_params=params(),
        cost_estimate=pl.CostEstimate(
            flops=2 * rows * depth * wide * blocks,
            bytes_accessed=2 * (depth + rows) * wide * blocks,
            transcendentals=0,
        ),
        name="project",
    )(places, feats, weight)
    return [halves[2 * block : 2 * block + 2] for block in range(blocks)]


def key_values(meta, pieces, weight, order_len, section_count, sharing):
    feat_rows = pieces[0].shape[0]
    depth, width = weight.shape
    kv_rows = SLOTS // sharing
    half_width = width // 2
    count = len(pieces)

    def kernel(meta_ref, *refs):
        piece_refs, weight_ref = refs[:count], refs[count]
        out_refs, kv_ref = refs[count + 1 : -1], refs[-1]
        section = meta_ref[order_len + 1]
        slot = lax.broadcasted_iota(jnp.int32, (BLOCK, feat_rows), 0)
        packed = lax.broadcasted_iota(jnp.int32, (BLOCK, feat_rows), 1)
        for sample in range(SAMP_SECTION):
            start = meta_ref[order_len + 2 + sample]
            live = TT * meta_ref[order_len + 2 + SAMP_SECTION + sample]
            image = jnp.zeros((BLOCK, depth), F32)
            for index in range(count):
                step, swapped = index // 2, index % 2
                origin = lax.rem(section + (section_count - 2 * step), section_count)
                if swapped:
                    origin = origin + 1 - 2 * lax.rem(origin, 2)
                chosen = (slot < live) & (packed == slot + (start - origin * feat_rows))
                image += jnp.dot(
                    chosen.astype(F32).astype(BF16),
                    piece_refs[index][...],
                    preferred_element_type=F32,
                )
            kv_ref[sample * BLOCK : (sample + 1) * BLOCK, :] = jnp.dot(
                image.astype(BF16), weight_ref[...], preferred_element_type=F32
            ).astype(BF16)
        for index in range(order_len):
            target = meta_ref[index]
            row = pl.multiple_of(lax.rem(target, sharing) * kv_rows, kv_rows)
            column = pl.multiple_of(target // sharing * HD, HD)
            out_refs[index][:, :HD] = kv_ref[pl.ds(row, kv_rows), pl.ds(column, HD)]
            out_refs[index][:, HD:] = kv_ref[
                pl.ds(row, kv_rows), pl.ds(pl.multiple_of(column + half_width, HD), HD)
            ]

    whole = pl.BlockSpec(memory_space=pltpu.VMEM)
    return pl.pallas_call(
        kernel,
        in_specs=[pl.BlockSpec(memory_space=pltpu.SMEM)] + [whole] * (count + 1),
        out_specs=[whole] * order_len,
        out_shape=[jax.ShapeDtypeStruct((kv_rows, 2 * HD), BF16)] * order_len,
        scratch_shapes=[pltpu.VMEM((SLOTS, width), BF16)],
        compiler_params=params(),
        cost_estimate=QUICK,
        name="key_values",
    )(meta, *pieces, weight)


def query(chunks, weight):
    rows = sum(chunk.shape[0] for chunk in chunks)
    depth, width = weight.shape
    wide = min(2 * HD, width)
    count = len(chunks)

    def kernel(*refs):
        chunk_refs, weight_ref, out_ref = refs[:count], refs[count], refs[count + 1]
        rows_ref, scale_ref = refs[count + 2 :]

        @pl.when(pl.program_id(0) == 0)
        def _():
            first = 0
            for chunk_ref in chunk_refs:
                place = slice(first, first + chunk_ref.shape[0])
                chunk = chunk_ref[...]
                wider = chunk.astype(F32)
                rows_ref[place, :] = chunk
                scale_ref[place, :] = lax.rsqrt(
                    jnp.mean(wider * wider, axis=-1, keepdims=True) + 1e-05
                )
                first += chunk_ref.shape[0]

        projected = jnp.dot(rows_ref[...], weight_ref[...], preferred_element_type=F32)
        projected = projected * scale_ref[...]
        for head in range(wide // HD):
            one = projected[:, head * HD : (head + 1) * HD]
            one = one * lax.rsqrt(jnp.mean(one * one, axis=-1, keepdims=True) + 1e-06)
            out_ref[:, head * HD : (head + 1) * HD] = one.astype(BF16)

    return pl.pallas_call(
        kernel,
        grid=(width // wide,),
        in_specs=[pl.BlockSpec(chunk.shape, lambda i: (0, 0)) for chunk in chunks]
        + [pl.BlockSpec((depth, wide), lambda i: (0, i))],
        out_specs=pl.BlockSpec((rows, wide), lambda i: (0, i)),
        out_shape=jax.ShapeDtypeStruct((rows, width), BF16),
        scratch_shapes=[pltpu.VMEM((rows, depth), BF16), pltpu.VMEM((rows, 1), F32)],
        compiler_params=params(),
        cost_estimate=QUICK,
        name="query",
    )(*chunks, weight)


def attend(meta, queries, kv_pieces, weight, indices, sizes, order_len):
    text_rows = queries.shape[0] // len(indices)
    rows, width = queries.shape
    heads = width // HD
    sharing = len(kv_pieces)
    kv_rows = SLOTS // sharing
    columns = weight.shape[1]
    wide = min(1024, columns)

    def kernel(meta_ref, query_ref, *refs):
        kv_refs, weight_ref = refs[:sharing], refs[sharing]
        out_refs = refs[sharing + 1 : -5]
        key_ref, value_ref, attended_ref, held_ref, sems = refs[-5:]
        step = pl.program_id(0)

        def fetch(index):
            start = index * wide
            return pltpu.make_async_copy(
                weight_ref.at[:, pl.ds(pl.multiple_of(start, wide), wide)],
                held_ref.at[index],
                sems.at[index],
            )

        @pl.when(step == 0)
        def _():
            for index in range(columns // wide):
                fetch(index).start()
            mine = lax.rem(meta_ref[order_len], sharing)
            for piece in range(sharing):
                row = pl.multiple_of(
                    lax.rem(mine + sharing - piece, sharing) * kv_rows, kv_rows
                )
                keys = kv_refs[piece][:, :HD].astype(F32)
                keys = keys * lax.rsqrt(jnp.mean(keys * keys, axis=-1, keepdims=True) + 1e-06)
                key_ref[pl.ds(row, kv_rows), :] = keys.astype(BF16)
                value_ref[pl.ds(row, kv_rows), :] = kv_refs[piece][:, HD:]
            for place, index in enumerate(indices):
                sample = meta_ref[index] * text_rows // TXT
                slots = pl.ds(pl.multiple_of(sample * BLOCK, BLOCK), BLOCK)
                live = TT * meta_ref[order_len + 2 + SAMP_SECTION + sample]
                first = place * text_rows
                own = query_ref[first : first + text_rows, :]
                stacked = jnp.concatenate(
                    [own[:, h * HD : (h + 1) * HD] for h in range(heads)], axis=0
                )
                scores = lax.dot_general(
                    stacked,
                    key_ref[slots, :],
                    (((1,), (1,)), ((), ())),
                    preferred_element_type=F32,
                ) * (1.0 / math.sqrt(HD))
                slot = lax.broadcasted_iota(jnp.int32, scores.shape, 1)
                raised = jnp.where(slot < live, jnp.exp(scores), 0.0)
                weights = (raised / jnp.sum(raised, axis=-1, keepdims=True)).astype(BF16)
                result = jnp.dot(
                    weights, value_ref[slots, :], preferred_element_type=F32
                ).astype(BF16)
                for h in range(heads):
                    attended_ref[first : first + text_rows, h * HD : (h + 1) * HD] = result[
                        h * text_rows : (h + 1) * text_rows
                    ]

        fetch(step).wait()
        product = jnp.dot(
            attended_ref[...], held_ref[step], preferred_element_type=F32
        ).astype(BF16)
        first = 0
        for out_ref, size in zip(out_refs, sizes):
            out_ref[...] = product[first : first + size]
            first += size

    return pl.pallas_call(
        kernel,
        grid_spec=pltpu.PrefetchScalarGridSpec(
            num_scalar_prefetch=1,
            grid=(columns // wide,),
            in_specs=[pl.BlockSpec((rows, width), lambda i, meta: (0, 0))]
            + [pl.BlockSpec(piece.shape, lambda i, meta: (0, 0)) for piece in kv_pieces]
            + [pl.BlockSpec(memory_space=pl.ANY)],
            out_specs=[pl.BlockSpec((size, wide), lambda i, meta: (0, i)) for size in sizes],
            scratch_shapes=[
                pltpu.VMEM((SLOTS, HD), BF16),
                pltpu.VMEM((SLOTS, HD), BF16),
                pltpu.VMEM((rows, width), BF16),
                pltpu.VMEM((columns // wide, width, wide), BF16),
                pltpu.SemaphoreType.DMA((columns // wide,)),
            ],
        ),
        out_shape=[jax.ShapeDtypeStruct((size, columns), BF16) for size in sizes],
        compiler_params=params(VMEM_MOST),
        cost_estimate=QUICK,
        name="attend",
    )(meta, queries, *kv_pieces, weight)


def after(value, *others):
    return lax.optimization_barrier((value, *others))[0]


def local(
    mesh_shape,
    text_state,
    tile_feats,
    w_proj,
    w_query,
    w_kv,
    w_out,
    attn_gate,
    tile_counts,
    section_table,
):
    mp_count, section_count = mesh_shape["mp"], mesh_shape["section"]
    ring = ring_order(mp_count)
    far = mp_count // 2
    sharing = mp_count // KVH
    order = [far]
    for distance in range(far - 1, 0, -1):
        order += [-distance, distance]
    order.append(0)
    index_of = {offset: index for index, offset in enumerate(order)}
    index_of[-far] = 0
    table = np.array(
        [
            [ring[(ring.index(m) + offset) % mp_count] for offset in order] + [m, s]
            for s in range(section_count)
            for m in range(mp_count)
        ],
        np.int32,
    )
    device = lax.axis_index(("section", "mp"))
    places = lax.dynamic_slice(
        jnp.asarray(table), (device, 0), (1, mp_count + 2)
    ).reshape(-1)
    starts, counts = own_samples(tile_counts, section_table, places[mp_count + 1])
    meta = jnp.concatenate([places, starts, counts])

    up_pairs = [(ring[i], ring[(i + 1) % mp_count]) for i in range(mp_count)]
    down_pairs = [(target, source) for source, target in up_pairs]

    def up(value):
        return lax.ppermute(value, "mp", up_pairs)

    def down(value):
        return lax.ppermute(value, "mp", down_pairs)

    def across(pairs):
        return [
            (s * mp_count + a, ((s + 1) % section_count) * mp_count + b)
            for s in range(section_count)
            for a, b in pairs
        ]

    def up_across(value):
        return lax.ppermute(value, ("section", "mp"), across(up_pairs))

    def down_across(value):
        return lax.ppermute(value, ("section", "mp"), across(down_pairs))

    def to_next(value):
        return lax.ppermute(
            value, "section", [(s, (s + 1) % section_count) for s in range(section_count)]
        )

    def ring_sums(chains, hold=lambda hop, value: value, turn=None):
        running = [part(sign * distance) for part, distance, sign, _, _ in chains]
        for hop in range(far):
            for index, (part, distance, sign, move, last) in enumerate(chains):
                left = distance - hop
                if left == 1:
                    running[index] = last(hold(hop, running[index]))
                elif left > 1:
                    came = move(hold(hop, running[index]))
                    if turn is not None:
                        came = after(came, turn)
                    turn = running[index] = add(came, part(sign * (left - 1)))
        return running

    def both_ways(part, distance_up, distance_down, last_up=up, last_down=down):
        return [
            (part, distance_up, 1, up, last_up),
            (part, distance_down, -1, down, last_down),
        ]

    text_own = text_state[0]
    text_rows = text_own.shape[0]
    parts = 2 if text_rows % 32 == 0 else 1
    cut = text_rows // parts
    reach = [(far, far - 1), (far - 1, far)][:parts]
    text_next = to_next(text_own)
    gate_next = to_next(attn_gate)
    from_below, from_above = [text_own], [text_own]

    def text_round(*first):
        from_below.append(up(after(from_below[-1], *first)))
        from_above.append(down(after(from_above[-1], *first)))

    text_round()

    image_parts = project(places, tile_feats, w_proj, mp_count, 0, 1)
    image_parts += project(places, tile_feats, w_proj, mp_count, 1, mp_count - 1)
    image_chains = [
        chain
        for half, distances in enumerate(((far, far - 1), (far - 1, far)))
        for chain in both_ways(
            lambda offset, half=half: image_parts[index_of[offset]][half], *distances
        )
    ]

    def image_hold(hop, value):
        if hop == min(2, far - 1):
            return after(value, from_below[1], from_above[1])
        if hop == far - 1:
            return after(value, text_next, gate_next)
        return value

    turns = [0, 3, 1, 2]
    came = ring_sums([image_chains[turn] for turn in turns], image_hold)
    came = [came[turns.index(index)] for index in range(4)]
    image_cols = total_of(
        [[image_parts[index_of[0]][half], *came[2 * half : 2 * half + 2]] for half in range(2)]
    )

    text_round(image_cols)
    weight_query, weight_out = w_query[0], w_out[0]
    near = [-1, 1]
    near_queries = [query([from_below[1], from_above[1]], weight_query)]

    pieces = []
    moving = image_cols
    for step in range(section_count // 2):
        pieces += [
            moving,
            lax.ppermute(moving, "section", [(s, s ^ 1) for s in range(section_count)]),
        ]
        if step + 1 < section_count // 2:
            moving = lax.ppermute(
                moving,
                "section",
                [(s, (s + 2) % section_count) for s in range(section_count)],
            )
            if step == 0:
                moving = after(moving, near_queries[0])

    kv_part = key_values(meta, pieces, w_kv[0], mp_count, section_count, sharing)

    for distance in range(3, far):
        text_round(*([kv_part[0]] if distance == 3 else []))
    far_chunks = [up(from_below[-1][:cut])]
    if parts == 2:
        far_chunks.append(down(from_above[-1][cut:]))
    for distance in range(2, far):
        near += [-distance, distance]
        near_queries.append(query([from_below[distance], from_above[distance]], weight_query))

    def kv_hold(hop, value):
        if hop == min(2, far - 1):
            return after(value, *from_below[3:], *from_above[3:])
        return value

    came = ring_sums(both_ways(lambda offset: kv_part[index_of[offset]], far, far - 1), kv_hold)
    kv_own = (
        kv_part[index_of[0]].astype(F32) + came[0].astype(F32) + came[1].astype(F32)
    ).astype(BF16)
    near_queries = jnp.concatenate(near_queries, axis=0)
    kv_own = after(kv_own, *far_chunks, near_queries)
    kv_pieces = [kv_own]
    for step in range(1, sharing):
        pairs = [
            (m, m // sharing * sharing + (m % sharing + step) % sharing) for m in range(mp_count)
        ]
        kv_pieces.append(lax.ppermute(kv_own, "mp", pairs))

    far_queries = query(far_chunks + [text_own], weight_query)
    *far_part, own_part = attend(
        meta,
        far_queries,
        kv_pieces,
        weight_out,
        [index_of[far], index_of[0]],
        [cut] * parts + [text_rows],
        mp_count,
    )
    near_part = attend(
        meta,
        after(near_queries, own_part),
        kv_pieces,
        weight_out,
        [index_of[offset] for offset in near],
        [cut] * (parts * len(near)),
        mp_count,
    )
    out_parts = {offset: near_part[parts * i :][:parts] for i, offset in enumerate(near)}
    out_parts[far] = out_parts[-far] = far_part

    own_next = to_next(own_part)
    branch_chains = [
        chain
        for part, distances in enumerate(reach)
        for chain in both_ways(
            lambda offset, part=part: out_parts[offset][part],
            *distances,
            up_across,
            down_across,
        )
    ]

    turns = [0, 3, 1, 2] if parts == 2 else [0, 1]
    came = ring_sums([branch_chains[turn] for turn in turns], turn=own_next)
    came = [came[turns.index(index)] for index in range(2 * parts)]
    return finish(
        gate_next, text_next, own_next, [came[2 * part : 2 * part + 2] for part in range(parts)]
    )


def solution(mesh):
    mesh_shape = dict(mesh.shape)

    def body(*arrays):
        return local(mesh_shape, *arrays)

    return jax.shard_map(
        body,
        mesh=mesh,
        in_specs=(
            P("section", "mp", None),
            P("section", "mp"),
            P("mp", None),
            P("section", None, "mp"),
            P("section", "mp", None),
            P("section", "mp", None),
            P("section"),
            P(),
            P(),
        ),
        out_specs=P("section", "mp", None),
        check_vma=False,
    )
```

```python
import math

import jax
import jax.numpy as jnp
import numpy as np
from jax import lax
from jax.experimental import pallas as pl
from jax.experimental.pallas import tpu as pltpu
from jax.sharding import PartitionSpec as P

HD = 128
HEADS = 32
KVH = 4
SAMP_SECTION = 4
TXT = 128
TT = 32
MAXT = 4
BLOCK = MAXT * TT
SLOTS = SAMP_SECTION * BLOCK
F32 = jnp.float32
BF16 = jnp.bfloat16
VMEM_LIMIT = 24 * 1024 * 1024
QUICK = pl.CostEstimate(flops=1, bytes_accessed=1, transcendentals=0)
VMEM_SMALL = 16 * 1024 * 1024


def ring_order(count):
    wide = 2 if count <= 8 else 4
    tall = count // wide
    if count < 4 or count % wide or tall % 2:
        return list(range(count))
    order = [row * wide for row in range(tall)]
    for turn, row in enumerate(reversed(range(tall))):
        columns = range(1, wide) if turn % 2 == 0 else range(wide - 1, 0, -1)
        order += [row * wide + column for column in columns]
    return order


def own_samples(tile_counts, section_table, section_id):
    samples_all = tile_counts.shape[0]
    sample_ids = jnp.arange(samples_all, dtype=jnp.int32)
    same_section = section_table[None, :] == section_table[:, None]
    before = sample_ids[None, :] < sample_ids[:, None]
    ranking = jnp.sum((same_section & before).astype(jnp.int32), axis=1)
    picked = (section_table[None, :] == section_id) & (
        ranking[None, :] == jnp.arange(SAMP_SECTION, dtype=jnp.int32)[:, None]
    )
    first_row = TT * jnp.sum(jnp.where(before, tile_counts[None, :], 0), axis=1)
    counts_own = jnp.sum(jnp.where(picked, tile_counts[None, :], 0), axis=1)
    starts_own = jnp.sum(jnp.where(picked, first_row[None, :], 0), axis=1)
    return starts_own, counts_own


def add(one, other):
    return (one.astype(F32) + other.astype(F32)).astype(BF16)


def params(limit=VMEM_LIMIT):
    return pltpu.CompilerParams(vmem_limit_bytes=limit)


def total_of(groups):
    parts, count = len(groups), len(groups[0])
    part_rows, columns = groups[0][0].shape
    rows = parts * part_rows

    def kernel(*refs):
        for part in range(parts):
            total = refs[part * count][...].astype(F32)
            for ref in refs[part * count + 1 : (part + 1) * count]:
                total += ref[...].astype(F32)
            refs[-1][part * part_rows : (part + 1) * part_rows, :] = total.astype(BF16)

    return pl.pallas_call(
        kernel,
        in_specs=[pl.BlockSpec(memory_space=pltpu.VMEM)] * (parts * count),
        out_specs=pl.BlockSpec(memory_space=pltpu.VMEM),
        out_shape=jax.ShapeDtypeStruct((rows, columns), BF16),
        compiler_params=params(VMEM_SMALL),
        cost_estimate=QUICK,
        name="total_of",
    )(*[value for group in groups for value in group])


def finish(gate, text, own, arrivals):
    rows, columns = text.shape
    part_rows = rows // len(arrivals)
    result = jnp.zeros((1, rows, columns), BF16)
    for part, came in enumerate(arrivals):
        place = slice(part * part_rows, (part + 1) * part_rows)
        branch = own[place].astype(F32)
        for value in came:
            branch = branch + value.astype(F32)
        part_out = (text[place].astype(F32) + jnp.tanh(gate[0]) * branch).astype(BF16)
        result = lax.dynamic_update_slice(result, part_out[None], (0, part * part_rows, 0))
    return result


def project(places, feats, weight, order_len, first, blocks):
    rows, depth = feats.shape
    half = rows // 2
    wide = weight.shape[1] // order_len

    def kernel(places_ref, feats_ref, weight_ref, *out_refs):
        product = jnp.dot(
            feats_ref[...], weight_ref[...], preferred_element_type=F32
        ).astype(BF16)
        for block in range(blocks):

            @pl.when(pl.program_id(0) == block)
            def _():
                out_refs[2 * block][...] = product[:half]
                out_refs[2 * block + 1][...] = product[half:]

    halves = pl.pallas_call(
        kernel,
        grid_spec=pltpu.PrefetchScalarGridSpec(
            num_scalar_prefetch=1,
            grid=(blocks,),
            in_specs=[
                pl.BlockSpec((rows, depth), lambda i, places: (0, 0)),
                pl.BlockSpec((depth, wide), lambda i, places: (0, places[first + i])),
            ],
            out_specs=[pl.BlockSpec((half, wide), lambda i, places: (0, 0))] * (2 * blocks),
        ),
        out_shape=[jax.ShapeDtypeStruct((half, wide), BF16)] * (2 * blocks),
        compiler_params=params(56 * 1024 * 1024),
        cost_estimate=pl.CostEstimate(
            flops=2 * rows * depth * wide * blocks,
            bytes_accessed=2 * (depth + rows) * wide * blocks,
            transcendentals=0,
        ),
        name="project",
    )(places, feats, weight)
    return [halves[2 * block : 2 * block + 2] for block in range(blocks)]


def key_values(meta, pieces, weight, order_len, section_count, sharing):
    feat_rows = pieces[0].shape[0]
    depth, width = weight.shape
    kv_rows = SLOTS // sharing
    half_width = width // 2
    count = len(pieces)

    def kernel(meta_ref, *refs):
        piece_refs, weight_ref = refs[:count], refs[count]
        out_refs, kv_ref = refs[count + 1 : -1], refs[-1]
        section = meta_ref[order_len + 1]
        slot = lax.broadcasted_iota(jnp.int32, (BLOCK, feat_rows), 0)
        packed = lax.broadcasted_iota(jnp.int32, (BLOCK, feat_rows), 1)
        for sample in range(SAMP_SECTION):
            start = meta_ref[order_len + 2 + sample]
            live = TT * meta_ref[order_len + 2 + SAMP_SECTION + sample]
            image = jnp.zeros((BLOCK, depth), F32)
            for index in range(count):
                step, swapped = index // 2, index % 2
                origin = lax.rem(section + (section_count - 2 * step), section_count)
                if swapped:
                    origin = origin + 1 - 2 * lax.rem(origin, 2)
                chosen = (slot < live) & (packed == slot + (start - origin * feat_rows))
                image += jnp.dot(
                    chosen.astype(F32).astype(BF16),
                    piece_refs[index][...],
                    preferred_element_type=F32,
                )
            kv_ref[sample * BLOCK : (sample + 1) * BLOCK, :] = jnp.dot(
                image.astype(BF16), weight_ref[...], preferred_element_type=F32
            ).astype(BF16)
        for index in range(order_len):
            target = meta_ref[index]
            row = pl.multiple_of(lax.rem(target, sharing) * kv_rows, kv_rows)
            column = pl.multiple_of(target // sharing * HD, HD)
            out_refs[index][:, :HD] = kv_ref[pl.ds(row, kv_rows), pl.ds(column, HD)]
            out_refs[index][:, HD:] = kv_ref[
                pl.ds(row, kv_rows), pl.ds(pl.multiple_of(column + half_width, HD), HD)
            ]

    whole = pl.BlockSpec(memory_space=pltpu.VMEM)
    return pl.pallas_call(
        kernel,
        in_specs=[pl.BlockSpec(memory_space=pltpu.SMEM)] + [whole] * (count + 1),
        out_specs=[whole] * order_len,
        out_shape=[jax.ShapeDtypeStruct((kv_rows, 2 * HD), BF16)] * order_len,
        scratch_shapes=[pltpu.VMEM((SLOTS, width), BF16)],
        compiler_params=params(),
        cost_estimate=QUICK,
        name="key_values",
    )(meta, *pieces, weight)


def query(chunks, weight):
    rows = sum(chunk.shape[0] for chunk in chunks)
    depth, width = weight.shape
    wide = min(2 * HD, width)
    count = len(chunks)

    def kernel(*refs):
        chunk_refs, weight_ref, out_ref = refs[:count], refs[count], refs[count + 1]
        rows_ref, scale_ref = refs[count + 2 :]

        @pl.when(pl.program_id(0) == 0)
        def _():
            first = 0
            for chunk_ref in chunk_refs:
                place = slice(first, first + chunk_ref.shape[0])
                chunk = chunk_ref[...]
                wider = chunk.astype(F32)
                rows_ref[place, :] = chunk
                scale_ref[place, :] = lax.rsqrt(
                    jnp.mean(wider * wider, axis=-1, keepdims=True) + 1e-05
                )
                first += chunk_ref.shape[0]

        projected = jnp.dot(rows_ref[...], weight_ref[...], preferred_element_type=F32)
        projected = projected * scale_ref[...]
        for head in range(wide // HD):
            one = projected[:, head * HD : (head + 1) * HD]
            one = one * lax.rsqrt(jnp.mean(one * one, axis=-1, keepdims=True) + 1e-06)
            out_ref[:, head * HD : (head + 1) * HD] = one.astype(BF16)

    return pl.pallas_call(
        kernel,
        grid=(width // wide,),
        in_specs=[pl.BlockSpec(chunk.shape, lambda i: (0, 0)) for chunk in chunks]
        + [pl.BlockSpec((depth, wide), lambda i: (0, i))],
        out_specs=pl.BlockSpec((rows, wide), lambda i: (0, i)),
        out_shape=jax.ShapeDtypeStruct((rows, width), BF16),
        scratch_shapes=[pltpu.VMEM((rows, depth), BF16), pltpu.VMEM((rows, 1), F32)],
        compiler_params=params(),
        cost_estimate=QUICK,
        name="query",
    )(*chunks, weight)


def attend(meta, queries, kv_pieces, weight, indices, sizes, order_len):
    text_rows = queries.shape[0] // len(indices)
    rows, width = queries.shape
    heads = width // HD
    sharing = len(kv_pieces)
    kv_rows = SLOTS // sharing
    columns = weight.shape[1]
    wide = min(1024, columns)
    tall = min(64, width)

    def kernel(meta_ref, query_ref, *refs):
        kv_refs, weight_ref = refs[:sharing], refs[sharing]
        out_refs = refs[sharing + 1 : -5]
        key_ref, value_ref, attended_ref, held_ref, sems = refs[-5:]
        step = pl.program_id(0)

        def fetch(index):
            place = pl.ds(index * tall, tall)
            return pltpu.make_async_copy(
                weight_ref.at[place, :], held_ref.at[place, :], sems.at[index]
            )

        @pl.when(step == 0)
        def _():
            for index in range(width // tall):
                fetch(index).start()
            mine = lax.rem(meta_ref[order_len], sharing)
            for piece in range(sharing):
                row = pl.multiple_of(
                    lax.rem(mine + sharing - piece, sharing) * kv_rows, kv_rows
                )
                keys = kv_refs[piece][:, :HD].astype(F32)
                keys = keys * lax.rsqrt(jnp.mean(keys * keys, axis=-1, keepdims=True) + 1e-06)
                key_ref[pl.ds(row, kv_rows), :] = keys.astype(BF16)
                value_ref[pl.ds(row, kv_rows), :] = kv_refs[piece][:, HD:]
            for place, index in enumerate(indices):
                sample = meta_ref[index] * text_rows // TXT
                slots = pl.ds(pl.multiple_of(sample * BLOCK, BLOCK), BLOCK)
                live = TT * meta_ref[order_len + 2 + SAMP_SECTION + sample]
                first = place * text_rows
                own = query_ref[first : first + text_rows, :]
                stacked = jnp.concatenate(
                    [own[:, h * HD : (h + 1) * HD] for h in range(heads)], axis=0
                )
                scores = lax.dot_general(
                    stacked,
                    key_ref[slots, :],
                    (((1,), (1,)), ((), ())),
                    preferred_element_type=F32,
                ) * (1.0 / math.sqrt(HD))
                slot = lax.broadcasted_iota(jnp.int32, scores.shape, 1)
                raised = jnp.where(slot < live, jnp.exp(scores), 0.0)
                weights = (raised / jnp.sum(raised, axis=-1, keepdims=True)).astype(BF16)
                result = jnp.dot(
                    weights, value_ref[slots, :], preferred_element_type=F32
                ).astype(BF16)
                for h in range(heads):
                    attended_ref[first : first + text_rows, h * HD : (h + 1) * HD] = result[
                        h * text_rows : (h + 1) * text_rows
                    ]
            for index in range(width // tall):
                fetch(index).wait()

        product = jnp.dot(
            attended_ref[...],
            held_ref[:, pl.ds(pl.multiple_of(step * wide, wide), wide)],
            preferred_element_type=F32,
        ).astype(BF16)
        first = 0
        for out_ref, size in zip(out_refs, sizes):
            out_ref[...] = product[first : first + size]
            first += size

    return pl.pallas_call(
        kernel,
        grid_spec=pltpu.PrefetchScalarGridSpec(
            num_scalar_prefetch=1,
            grid=(columns // wide,),
            in_specs=[pl.BlockSpec((rows, width), lambda i, meta: (0, 0))]
            + [pl.BlockSpec(piece.shape, lambda i, meta: (0, 0)) for piece in kv_pieces]
            + [pl.BlockSpec(memory_space=pl.ANY)],
            out_specs=[pl.BlockSpec((size, wide), lambda i, meta: (0, i)) for size in sizes],
            scratch_shapes=[
                pltpu.VMEM((SLOTS, HD), BF16),
                pltpu.VMEM((SLOTS, HD), BF16),
                pltpu.VMEM((rows, width), BF16),
                pltpu.VMEM((width, columns), BF16),
                pltpu.SemaphoreType.DMA((width // tall,)),
            ],
        ),
        out_shape=[jax.ShapeDtypeStruct((size, columns), BF16) for size in sizes],
        compiler_params=params(),
        cost_estimate=pl.CostEstimate(
            flops=8 * rows * width * columns,
            bytes_accessed=8 * width * columns,
            transcendentals=rows * heads * BLOCK,
        ),
        name="attend",
    )(meta, queries, *kv_pieces, weight)


def after(value, *others):
    return lax.optimization_barrier((value, *others))[0]


def local(
    mesh_shape,
    text_state,
    tile_feats,
    w_proj,
    w_query,
    w_kv,
    w_out,
    attn_gate,
    tile_counts,
    section_table,
):
    mp_count, section_count = mesh_shape["mp"], mesh_shape["section"]
    ring = ring_order(mp_count)
    far = mp_count // 2
    sharing = mp_count // KVH
    order = [far]
    for distance in range(far - 1, 0, -1):
        order += [-distance, distance]
    order.append(0)
    index_of = {offset: index for index, offset in enumerate(order)}
    index_of[-far] = 0
    table = np.array(
        [
            [ring[(ring.index(m) + offset) % mp_count] for offset in order] + [m, s]
            for s in range(section_count)
            for m in range(mp_count)
        ],
        np.int32,
    )
    device = lax.axis_index(("section", "mp"))
    places = lax.dynamic_slice(
        jnp.asarray(table), (device, 0), (1, mp_count + 2)
    ).reshape(-1)
    starts, counts = own_samples(tile_counts, section_table, places[mp_count + 1])
    meta = jnp.concatenate([places, starts, counts])

    up_pairs = [(ring[i], ring[(i + 1) % mp_count]) for i in range(mp_count)]
    down_pairs = [(target, source) for source, target in up_pairs]

    def up(value):
        return lax.ppermute(value, "mp", up_pairs)

    def down(value):
        return lax.ppermute(value, "mp", down_pairs)

    def across(pairs):
        return [
            (s * mp_count + a, ((s + 1) % section_count) * mp_count + b)
            for s in range(section_count)
            for a, b in pairs
        ]

    def up_across(value):
        return lax.ppermute(value, ("section", "mp"), across(up_pairs))

    def down_across(value):
        return lax.ppermute(value, ("section", "mp"), across(down_pairs))

    def to_next(value):
        return lax.ppermute(
            value, "section", [(s, (s + 1) % section_count) for s in range(section_count)]
        )

    def ring_sums(chains, hold=lambda hop, value: value, turn=None):
        running = [part(sign * distance) for part, distance, sign, _, _ in chains]
        for hop in range(far):
            for index, (part, distance, sign, move, last) in enumerate(chains):
                left = distance - hop
                if left == 1:
                    running[index] = last(hold(hop, running[index]))
                elif left > 1:
                    came = move(hold(hop, running[index]))
                    if turn is not None:
                        came = after(came, turn)
                    turn = running[index] = add(came, part(sign * (left - 1)))
        return running

    def both_ways(part, distance_up, distance_down, last_up=up, last_down=down):
        return [
            (part, distance_up, 1, up, last_up),
            (part, distance_down, -1, down, last_down),
        ]

    text_own = text_state[0]
    text_rows = text_own.shape[0]
    parts = 2 if text_rows % 32 == 0 else 1
    cut = text_rows // parts
    reach = [(far, far - 1), (far - 1, far)][:parts]
    text_next = to_next(text_own)
    gate_next = to_next(attn_gate)
    from_below, from_above = [text_own], [text_own]

    def text_round(*first):
        from_below.append(up(after(from_below[-1], *first)))
        from_above.append(down(after(from_above[-1], *first)))

    text_round()

    image_parts = project(places, tile_feats, w_proj, mp_count, 0, 1)
    image_parts += project(places, tile_feats, w_proj, mp_count, 1, mp_count - 1)
    image_chains = [
        chain
        for half, distances in enumerate(((far, far - 1), (far - 1, far)))
        for chain in both_ways(
            lambda offset, half=half: image_parts[index_of[offset]][half], *distances
        )
    ]

    def image_hold(hop, value):
        if hop == 1:
            return after(value, from_below[1], from_above[1], text_next)
        return value

    turns = [0, 3, 1, 2]
    came = ring_sums([image_chains[turn] for turn in turns], image_hold)
    came = [came[turns.index(index)] for index in range(4)]
    image_cols = total_of(
        [[image_parts[index_of[0]][half], *came[2 * half : 2 * half + 2]] for half in range(2)]
    )

    text_round(image_cols)
    weight_query, weight_out = w_query[0], w_out[0]
    near = [-1, 1]
    near_queries = [query([from_below[1], from_above[1]], weight_query)]

    pieces = []
    moving = image_cols
    for step in range(section_count // 2):
        pieces += [
            moving,
            lax.ppermute(moving, "section", [(s, s ^ 1) for s in range(section_count)]),
        ]
        if step + 1 < section_count // 2:
            moving = lax.ppermute(
                moving,
                "section",
                [(s, (s + 2) % section_count) for s in range(section_count)],
            )
            if step == 0:
                moving = after(moving, near_queries[0])

    kv_part = key_values(meta, pieces, w_kv[0], mp_count, section_count, sharing)

    for distance in range(3, far):
        text_round(*([kv_part[0]] if distance == 3 else []))
    for distance in range(2, far):
        near += [-distance, distance]
        near_queries.append(query([from_below[distance], from_above[distance]], weight_query))

    def kv_hold(hop, value):
        if hop == far - 1:
            return after(value, *from_below[3:], *from_above[3:])
        return value

    came = ring_sums(both_ways(lambda offset: kv_part[index_of[offset]], far, far - 1), kv_hold)
    kv_own = (
        kv_part[index_of[0]].astype(F32) + came[0].astype(F32) + came[1].astype(F32)
    ).astype(BF16)
    kv_own = after(kv_own, gate_next, *near_queries)
    kv_pieces = [kv_own]
    for step in range(1, sharing):
        pairs = [
            (m, m // sharing * sharing + (m % sharing + step) % sharing) for m in range(mp_count)
        ]
        kv_pieces.append(lax.ppermute(kv_own, "mp", pairs))

    far_chunks = [up(after(from_below[-1], kv_own)[:cut])]
    if parts == 2:
        far_chunks.append(down(after(from_above[-1], kv_own)[cut:]))

    def attend_to(offsets, queries, sizes):
        return attend(
            meta,
            queries,
            kv_pieces,
            weight_out,
            [index_of[offset] for offset in offsets],
            sizes,
            mp_count,
        )

    first, first_queries = near[-2:] + [0], [near_queries[-1], query([text_own], weight_query)]
    rest, rest_queries = near[:-2], near_queries[:-1]
    *first_part, own_part = attend_to(
        first,
        jnp.concatenate(first_queries, axis=0),
        [cut] * (parts * (len(first) - 1)) + [text_rows],
    )
    far_part = attend_to(
        [far], after(query(far_chunks, weight_query), own_part), [cut] * parts
    )
    rest_part = attend_to(
        rest,
        after(jnp.concatenate(rest_queries, axis=0), far_part[0]),
        [cut] * (parts * len(rest)),
    )
    near_part = list(first_part) + list(rest_part)
    out_parts = {
        offset: near_part[parts * i :][:parts] for i, offset in enumerate(first[:-1] + rest)
    }
    out_parts[far] = out_parts[-far] = far_part

    own_next = to_next(own_part)
    branch_chains = [
        chain
        for part, distances in enumerate(reach)
        for chain in both_ways(
            lambda offset, part=part: out_parts[offset][part],
            *distances,
            up_across,
            down_across,
        )
    ]

    turns = [1, 2, 0, 3] if parts == 2 else [0, 1]
    came = ring_sums([branch_chains[turn] for turn in turns], turn=own_next)
    came = [came[turns.index(index)] for index in range(2 * parts)]
    return finish(
        gate_next, text_next, own_next, [came[2 * part : 2 * part + 2] for part in range(parts)]
    )


def solution(mesh):
    mesh_shape = dict(mesh.shape)

    def body(*arrays):
        return local(mesh_shape, *arrays)

    return jax.shard_map(
        body,
        mesh=mesh,
        in_specs=(
            P("section", "mp", None),
            P("section", "mp"),
            P("mp", None),
            P("section", None, "mp"),
            P("section", "mp", None),
            P("section", "mp", None),
            P("section"),
            P(),
            P(),
        ),
        out_specs=P("section", "mp", None),
        check_vma=False,
    )
```

```python
import math

import jax
import jax.numpy as jnp
import numpy as np
from jax import lax
from jax.experimental import pallas as pl
from jax.experimental.pallas import tpu as pltpu
from jax.sharding import PartitionSpec as P

HD = 128
HEADS = 32
KVH = 4
SAMP_SECTION = 4
TXT = 128
TT = 32
MAXT = 4
BLOCK = MAXT * TT
SLOTS = SAMP_SECTION * BLOCK
F32 = jnp.float32
BF16 = jnp.bfloat16
VMEM_LIMIT = 24 * 1024 * 1024
QUICK = pl.CostEstimate(flops=1, bytes_accessed=1, transcendentals=0)
VMEM_SMALL = 16 * 1024 * 1024


def ring_order(count):
    wide = 2 if count <= 8 else 4
    tall = count // wide
    if count < 4 or count % wide or tall % 2:
        return list(range(count))
    order = [row * wide for row in range(tall)]
    for turn, row in enumerate(reversed(range(tall))):
        columns = range(1, wide) if turn % 2 == 0 else range(wide - 1, 0, -1)
        order += [row * wide + column for column in columns]
    return order


def own_samples(tile_counts, section_table, section_id):
    samples_all = tile_counts.shape[0]
    sample_ids = jnp.arange(samples_all, dtype=jnp.int32)
    same_section = section_table[None, :] == section_table[:, None]
    before = sample_ids[None, :] < sample_ids[:, None]
    ranking = jnp.sum((same_section & before).astype(jnp.int32), axis=1)
    picked = (section_table[None, :] == section_id) & (
        ranking[None, :] == jnp.arange(SAMP_SECTION, dtype=jnp.int32)[:, None]
    )
    first_row = TT * jnp.sum(jnp.where(before, tile_counts[None, :], 0), axis=1)
    counts_own = jnp.sum(jnp.where(picked, tile_counts[None, :], 0), axis=1)
    starts_own = jnp.sum(jnp.where(picked, first_row[None, :], 0), axis=1)
    return starts_own, counts_own


def add(one, other):
    return (one.astype(F32) + other.astype(F32)).astype(BF16)


def params(limit=VMEM_LIMIT):
    return pltpu.CompilerParams(vmem_limit_bytes=limit)


def total_of(groups):
    parts, count = len(groups), len(groups[0])
    part_rows, columns = groups[0][0].shape
    rows = parts * part_rows

    def kernel(*refs):
        for part in range(parts):
            total = refs[part * count][...].astype(F32)
            for ref in refs[part * count + 1 : (part + 1) * count]:
                total += ref[...].astype(F32)
            refs[-1][part * part_rows : (part + 1) * part_rows, :] = total.astype(BF16)

    return pl.pallas_call(
        kernel,
        in_specs=[pl.BlockSpec(memory_space=pltpu.VMEM)] * (parts * count),
        out_specs=pl.BlockSpec(memory_space=pltpu.VMEM),
        out_shape=jax.ShapeDtypeStruct((rows, columns), BF16),
        compiler_params=params(VMEM_SMALL),
        cost_estimate=QUICK,
        name="total_of",
    )(*[value for group in groups for value in group])


def finish(gate, text, own, arrivals):
    part_rows = text.shape[0] // len(arrivals)
    results = []
    for part, came in enumerate(arrivals):
        pieces = max(len(values) for values in came)
        piece_rows = part_rows // pieces
        for piece in range(pieces):
            first = part * part_rows + piece * piece_rows
            place = slice(first, first + piece_rows)
            branch = own[place].astype(F32)
            for values in came:
                if len(values) == pieces:
                    value = values[piece]
                else:
                    value = values[0][piece * piece_rows : (piece + 1) * piece_rows]
                branch = branch + value.astype(F32)
            results.append((text[place].astype(F32) + jnp.tanh(gate[0]) * branch).astype(BF16))
    return jnp.concatenate(results, axis=0)[None]


def project(places, feats, weight, order_len, first, blocks):
    rows, depth = feats.shape
    half = rows // 2
    wide = weight.shape[1] // order_len

    def kernel(places_ref, feats_ref, weight_ref, *out_refs):
        product = jnp.dot(
            feats_ref[...], weight_ref[...], preferred_element_type=F32
        ).astype(BF16)
        for block in range(blocks):

            @pl.when(pl.program_id(0) == block)
            def _():
                out_refs[2 * block][...] = product[:half]
                out_refs[2 * block + 1][...] = product[half:]

    halves = pl.pallas_call(
        kernel,
        grid_spec=pltpu.PrefetchScalarGridSpec(
            num_scalar_prefetch=1,
            grid=(blocks,),
            in_specs=[
                pl.BlockSpec((rows, depth), lambda i, places: (0, 0)),
                pl.BlockSpec((depth, wide), lambda i, places: (0, places[first + i])),
            ],
            out_specs=[pl.BlockSpec((half, wide), lambda i, places: (0, 0))] * (2 * blocks),
        ),
        out_shape=[jax.ShapeDtypeStruct((half, wide), BF16)] * (2 * blocks),
        compiler_params=params(56 * 1024 * 1024),
        cost_estimate=pl.CostEstimate(
            flops=2 * rows * depth * wide * blocks,
            bytes_accessed=2 * (depth + rows) * wide * blocks,
            transcendentals=0,
        ),
        name="project",
    )(places, feats, weight)
    return [halves[2 * block : 2 * block + 2] for block in range(blocks)]


def key_values(meta, pieces, weight, order_len, section_count, sharing):
    feat_rows = pieces[0].shape[0]
    depth, width = weight.shape
    kv_rows = SLOTS // sharing
    half_width = width // 2
    count = len(pieces)

    def kernel(meta_ref, *refs):
        piece_refs, weight_ref = refs[:count], refs[count]
        out_refs, kv_ref = refs[count + 1 : -1], refs[-1]
        section = meta_ref[order_len + 1]
        slot = lax.broadcasted_iota(jnp.int32, (BLOCK, feat_rows), 0)
        packed = lax.broadcasted_iota(jnp.int32, (BLOCK, feat_rows), 1)
        for sample in range(SAMP_SECTION):
            start = meta_ref[order_len + 2 + sample]
            live = TT * meta_ref[order_len + 2 + SAMP_SECTION + sample]
            image = jnp.zeros((BLOCK, depth), F32)
            for index in range(count):
                step, swapped = index // 2, index % 2
                origin = lax.rem(section + (section_count - 2 * step), section_count)
                if swapped:
                    origin = origin + 1 - 2 * lax.rem(origin, 2)
                chosen = (slot < live) & (packed == slot + (start - origin * feat_rows))
                image += jnp.dot(
                    chosen.astype(F32).astype(BF16),
                    piece_refs[index][...],
                    preferred_element_type=F32,
                )
            kv_ref[sample * BLOCK : (sample + 1) * BLOCK, :] = jnp.dot(
                image.astype(BF16), weight_ref[...], preferred_element_type=F32
            ).astype(BF16)
        for index in range(order_len):
            target = meta_ref[index]
            row = pl.multiple_of(lax.rem(target, sharing) * kv_rows, kv_rows)
            column = pl.multiple_of(target // sharing * HD, HD)
            out_refs[index][:, :HD] = kv_ref[pl.ds(row, kv_rows), pl.ds(column, HD)]
            out_refs[index][:, HD:] = kv_ref[
                pl.ds(row, kv_rows), pl.ds(pl.multiple_of(column + half_width, HD), HD)
            ]

    whole = pl.BlockSpec(memory_space=pltpu.VMEM)
    return pl.pallas_call(
        kernel,
        in_specs=[pl.BlockSpec(memory_space=pltpu.SMEM)] + [whole] * (count + 1),
        out_specs=[whole] * order_len,
        out_shape=[jax.ShapeDtypeStruct((kv_rows, 2 * HD), BF16)] * order_len,
        scratch_shapes=[pltpu.VMEM((SLOTS, width), BF16)],
        compiler_params=params(),
        cost_estimate=QUICK,
        name="key_values",
    )(meta, *pieces, weight)


def query(chunks, weight):
    rows = sum(chunk.shape[0] for chunk in chunks)
    depth, width = weight.shape
    wide = min(2 * HD, width)
    count = len(chunks)

    def kernel(*refs):
        chunk_refs, weight_ref, out_ref = refs[:count], refs[count], refs[count + 1]
        rows_ref, scale_ref = refs[count + 2 :]

        @pl.when(pl.program_id(0) == 0)
        def _():
            first = 0
            for chunk_ref in chunk_refs:
                place = slice(first, first + chunk_ref.shape[0])
                chunk = chunk_ref[...]
                wider = chunk.astype(F32)
                rows_ref[place, :] = chunk
                scale_ref[place, :] = lax.rsqrt(
                    jnp.mean(wider * wider, axis=-1, keepdims=True) + 1e-05
                )
                first += chunk_ref.shape[0]

        projected = jnp.dot(rows_ref[...], weight_ref[...], preferred_element_type=F32)
        projected = projected * scale_ref[...]
        for head in range(wide // HD):
            one = projected[:, head * HD : (head + 1) * HD]
            one = one * lax.rsqrt(jnp.mean(one * one, axis=-1, keepdims=True) + 1e-06)
            out_ref[:, head * HD : (head + 1) * HD] = one.astype(BF16)

    return pl.pallas_call(
        kernel,
        grid=(width // wide,),
        in_specs=[pl.BlockSpec(chunk.shape, lambda i: (0, 0)) for chunk in chunks]
        + [pl.BlockSpec((depth, wide), lambda i: (0, i))],
        out_specs=pl.BlockSpec((rows, wide), lambda i: (0, i)),
        out_shape=jax.ShapeDtypeStruct((rows, width), BF16),
        scratch_shapes=[pltpu.VMEM((rows, depth), BF16), pltpu.VMEM((rows, 1), F32)],
        compiler_params=params(),
        cost_estimate=pl.CostEstimate(
            flops=2 * rows * depth * width,
            bytes_accessed=2 * depth * (width + rows),
            transcendentals=0,
        ),
        name="query",
    )(*chunks, weight)


def attend(meta, queries, kv_pieces, weight, indices, sizes, order_len):
    text_rows = queries.shape[0] // len(indices)
    rows, width = queries.shape
    heads = width // HD
    sharing = len(kv_pieces)
    kv_rows = SLOTS // sharing
    columns = weight.shape[1]
    wide = min(1024, columns)
    tall = min(64, width)

    def kernel(meta_ref, query_ref, *refs):
        kv_refs, weight_ref = refs[:sharing], refs[sharing]
        out_refs = refs[sharing + 1 : -5]
        key_ref, value_ref, attended_ref, held_ref, sems = refs[-5:]
        step = pl.program_id(0)

        def fetch(index):
            place = pl.ds(index * tall, tall)
            return pltpu.make_async_copy(
                weight_ref.at[place, :], held_ref.at[place, :], sems.at[index]
            )

        @pl.when(step == 0)
        def _():
            for index in range(width // tall):
                fetch(index).start()
            mine = lax.rem(meta_ref[order_len], sharing)
            for piece in range(sharing):
                row = pl.multiple_of(
                    lax.rem(mine + sharing - piece, sharing) * kv_rows, kv_rows
                )
                keys = kv_refs[piece][:, :HD].astype(F32)
                keys = keys * lax.rsqrt(jnp.mean(keys * keys, axis=-1, keepdims=True) + 1e-06)
                key_ref[pl.ds(row, kv_rows), :] = keys.astype(BF16)
                value_ref[pl.ds(row, kv_rows), :] = kv_refs[piece][:, HD:]
            for place, index in enumerate(indices):
                sample = meta_ref[index] * text_rows // TXT
                slots = pl.ds(pl.multiple_of(sample * BLOCK, BLOCK), BLOCK)
                live = TT * meta_ref[order_len + 2 + SAMP_SECTION + sample]
                first = place * text_rows
                own = query_ref[first : first + text_rows, :]
                stacked = jnp.concatenate(
                    [own[:, h * HD : (h + 1) * HD] for h in range(heads)], axis=0
                )
                scores = lax.dot_general(
                    stacked,
                    key_ref[slots, :],
                    (((1,), (1,)), ((), ())),
                    preferred_element_type=F32,
                ) * (1.0 / math.sqrt(HD))
                slot = lax.broadcasted_iota(jnp.int32, scores.shape, 1)
                raised = jnp.where(slot < live, jnp.exp(scores), 0.0)
                weights = (raised / jnp.sum(raised, axis=-1, keepdims=True)).astype(BF16)
                result = jnp.dot(
                    weights, value_ref[slots, :], preferred_element_type=F32
                ).astype(BF16)
                for h in range(heads):
                    attended_ref[first : first + text_rows, h * HD : (h + 1) * HD] = result[
                        h * text_rows : (h + 1) * text_rows
                    ]
            for index in range(width // tall):
                fetch(index).wait()

        product = jnp.dot(
            attended_ref[...],
            held_ref[:, pl.ds(pl.multiple_of(step * wide, wide), wide)],
            preferred_element_type=F32,
        ).astype(BF16)
        first = 0
        for out_ref, size in zip(out_refs, sizes):
            out_ref[...] = product[first : first + size]
            first += size

    return pl.pallas_call(
        kernel,
        grid_spec=pltpu.PrefetchScalarGridSpec(
            num_scalar_prefetch=1,
            grid=(columns // wide,),
            in_specs=[pl.BlockSpec((rows, width), lambda i, meta: (0, 0))]
            + [pl.BlockSpec(piece.shape, lambda i, meta: (0, 0)) for piece in kv_pieces]
            + [pl.BlockSpec(memory_space=pl.ANY)],
            out_specs=[pl.BlockSpec((size, wide), lambda i, meta: (0, i)) for size in sizes],
            scratch_shapes=[
                pltpu.VMEM((SLOTS, HD), BF16),
                pltpu.VMEM((SLOTS, HD), BF16),
                pltpu.VMEM((rows, width), BF16),
                pltpu.VMEM((width, columns), BF16),
                pltpu.SemaphoreType.DMA((width // tall,)),
            ],
        ),
        out_shape=[jax.ShapeDtypeStruct((size, columns), BF16) for size in sizes],
        compiler_params=params(),
        cost_estimate=pl.CostEstimate(
            flops=8 * rows * width * columns,
            bytes_accessed=8 * width * columns,
            transcendentals=rows * heads * BLOCK,
        ),
        name="attend",
    )(meta, queries, *kv_pieces, weight)


def after(value, *others):
    if not others:
        return value
    return lax.optimization_barrier((value, *others))[0]


def local(
    mesh_shape,
    text_state,
    tile_feats,
    w_proj,
    w_query,
    w_kv,
    w_out,
    attn_gate,
    tile_counts,
    section_table,
):
    mp_count, section_count = mesh_shape["mp"], mesh_shape["section"]
    ring = ring_order(mp_count)
    far = mp_count // 2
    sharing = mp_count // KVH
    order = [far]
    for distance in range(far - 1, 0, -1):
        order += [-distance, distance]
    order.append(0)
    index_of = {offset: index for index, offset in enumerate(order)}
    index_of[-far] = 0
    table = np.array(
        [
            [ring[(ring.index(m) + offset) % mp_count] for offset in order] + [m, s]
            for s in range(section_count)
            for m in range(mp_count)
        ],
        np.int32,
    )
    device = lax.axis_index(("section", "mp"))
    places = lax.dynamic_slice(
        jnp.asarray(table), (device, 0), (1, mp_count + 2)
    ).reshape(-1)
    starts, counts = own_samples(tile_counts, section_table, places[mp_count + 1])
    meta = jnp.concatenate([places, starts, counts])

    up_pairs = [(ring[i], ring[(i + 1) % mp_count]) for i in range(mp_count)]
    down_pairs = [(target, source) for source, target in up_pairs]

    def up(value):
        return lax.ppermute(value, "mp", up_pairs)

    def down(value):
        return lax.ppermute(value, "mp", down_pairs)

    def across(pairs):
        return [
            (s * mp_count + a, ((s + 1) % section_count) * mp_count + b)
            for s in range(section_count)
            for a, b in pairs
        ]

    def up_across(value):
        return lax.ppermute(value, ("section", "mp"), across(up_pairs))

    def down_across(value):
        return lax.ppermute(value, ("section", "mp"), across(down_pairs))

    def to_next(value):
        return lax.ppermute(
            value, "section", [(s, (s + 1) % section_count) for s in range(section_count)]
        )

    def ring_sums(chains, hold=lambda left, value: value, turn=(), fine=False):
        running = [[part(sign * distance)] for part, distance, sign, _, _ in chains]
        ended = []
        for hop in range(far):
            moved = [[] for _ in chains]
            for index, (part, distance, sign, move, last) in enumerate(chains):
                left = distance - hop
                sent = [hold(left, value) for value in running[index]]
                if left == 1:
                    running[index] = [last(value) for value in sent]
                    if fine and distance < far:
                        ended.append(running[index][0])
                elif left > 1:
                    plus = [part(sign * (left - 1))]
                    if left == 2 and fine and distance == far > 2:
                        rows = plus[0].shape[0] // 2
                        sent, plus = (
                            [value[0][:rows], value[0][rows:]]
                            for value in ([after(sent[0], *ended)], plus)
                        )
                    moved[index] = list(zip([move(value) for value in sent], plus))
                    running[index] = []
            for piece in range(max(len(values) for values in moved)):
                for index, values in enumerate(moved):
                    if piece < len(values):
                        came, own = values[piece]
                        turn = [add(after(came, *turn), own)]
                        running[index] += turn
        return running

    def both_ways(part, distance_up, distance_down, last_up=up, last_down=down):
        return [
            (part, distance_up, 1, up, last_up),
            (part, distance_down, -1, down, last_down),
        ]

    text_own = text_state[0]
    text_rows = text_own.shape[0]
    parts = 2 if text_rows % 32 == 0 else 1
    cut = text_rows // parts
    reach = [(far, far - 1), (far - 1, far)][:parts]
    text_next = to_next(text_own)
    gate_next = to_next(attn_gate)
    from_below, from_above = [text_own], [text_own]

    def text_round(*first):
        from_below.append(up(after(from_below[-1], *first)))
        from_above.append(down(after(from_above[-1], *first)))

    text_round()

    image_parts = project(places, tile_feats, w_proj, mp_count, 0, 1)
    image_parts += project(places, tile_feats, w_proj, mp_count, 1, mp_count - 1)
    image_chains = [
        chain
        for half, distances in enumerate(((far, far - 1), (far - 1, far)))
        for chain in both_ways(
            lambda offset, half=half: image_parts[index_of[offset]][half], *distances
        )
    ]

    def image_hold(left, value):
        return after(value, text_next) if left == 1 else value

    turns = [0, 3, 1, 2]
    came = ring_sums(
        [image_chains[turn] for turn in turns],
        image_hold,
        turn=[gate_next, from_below[1], from_above[1]],
    )
    came = [came[turns.index(index)][0] for index in range(4)]
    image_cols = total_of(
        [[image_parts[index_of[0]][half], *came[2 * half : 2 * half + 2]] for half in range(2)]
    )

    text_round(image_cols)
    weight_query, weight_out = w_query[0], w_out[0]
    queries = {
        0: query([text_own], weight_query),
        1: query([from_below[1], from_above[1]], weight_query),
    }

    pieces = []
    moving = image_cols
    for step in range(section_count // 2):
        pieces += [
            moving,
            lax.ppermute(moving, "section", [(s, s ^ 1) for s in range(section_count)]),
        ]
        if step + 1 < section_count // 2:
            moving = lax.ppermute(
                moving,
                "section",
                [(s, (s + 2) % section_count) for s in range(section_count)],
            )
            if step == 0:
                moving = after(moving, queries[0], queries[1])

    kv_part = key_values(meta, pieces, w_kv[0], mp_count, section_count, sharing)

    for distance in range(3, far):
        text_round(*([kv_part[0]] if distance == 3 else []))
    if far > 2:
        queries[far - 1] = query([from_below[far - 1], from_above[far - 1]], weight_query)

    def kv_hold(left, value):
        if left == 1:
            return after(value, *from_below[3:], *from_above[3:])
        return value

    def within(step):
        return [
            (m, m // sharing * sharing + (m % sharing + step) % sharing) for m in range(mp_count)
        ]

    def last_to_both(move, pairs):
        partner = dict(within(1))
        other = [(source, partner[target]) for source, target in pairs]
        if sharing != 2:
            return lambda value: [move(value)]
        return lambda value: [move(value), lax.ppermute(value, "mp", other)]

    own_kv = [kv_part[index_of[0]]]
    if sharing == 2:
        own_kv.append(lax.ppermute(own_kv[0], "mp", within(1)))
    came = ring_sums(
        both_ways(
            lambda offset: kv_part[index_of[offset]],
            far,
            far - 1,
            last_to_both(up, up_pairs),
            last_to_both(down, down_pairs),
        ),
        kv_hold,
    )
    kv_pieces = [
        (own.astype(F32) + above.astype(F32) + below.astype(F32)).astype(BF16)
        for own, above, below in zip(own_kv, came[0][0], came[1][0])
    ]
    kv_own = kv_pieces[0] = after(kv_pieces[0], queries[far - 1])
    if sharing != 2:
        for step in range(1, sharing):
            kv_pieces.append(lax.ppermute(kv_own, "mp", within(step)))

    far_chunks = [up(after(from_below[-1], kv_own)[:cut])]
    if parts == 2:
        far_chunks.append(down(after(from_above[-1], kv_own)[cut:]))

    def attend_to(offsets, queries, sizes):
        return attend(
            meta,
            queries,
            kv_pieces,
            weight_out,
            [index_of[offset] for offset in offsets],
            sizes,
            mp_count,
        )

    first = [1 - far, far - 1, 0]
    *first_part, own_part = attend_to(
        first,
        jnp.concatenate([queries[far - 1], queries[0]], axis=0),
        [cut] * (2 * parts) + [text_rows],
    )
    rest = [sign * distance for distance in range(1, far - 1) for sign in (-1, 1)]
    for distance in range(2, far - 1):
        below = after(from_below[distance], own_part)
        queries[distance] = query([below, from_above[distance]], weight_query)
    rest_queries = jnp.concatenate([queries[distance] for distance in range(1, far - 1)], axis=0)
    far_queries = query(far_chunks, weight_query)
    far_part = attend_to([far], after(far_queries, rest_queries, own_part), [cut] * parts)
    rest_part = attend_to(
        rest, after(rest_queries, far_part[0]), [cut] * (parts * len(rest))
    )
    near_part = list(first_part) + list(rest_part)
    out_parts = {
        offset: near_part[parts * i :][:parts] for i, offset in enumerate(first[:-1] + rest)
    }
    out_parts[far] = out_parts[-far] = far_part

    own_next = to_next(own_part)
    branch_chains = [
        chain
        for part, distances in enumerate(reach)
        for chain in both_ways(
            lambda offset, part=part: out_parts[offset][part],
            *distances,
            up_across,
            down_across,
        )
    ]

    turns = [1, 2, 0, 3] if parts == 2 else [0, 1]
    came = ring_sums([branch_chains[turn] for turn in turns], turn=[own_next], fine=parts == 2)
    came = [came[turns.index(index)] for index in range(2 * parts)]
    return finish(
        gate_next, text_next, own_next, [came[2 * part : 2 * part + 2] for part in range(parts)]
    )


def solution(mesh):
    mesh_shape = dict(mesh.shape)

    def body(*arrays):
        return local(mesh_shape, *arrays)

    return jax.shard_map(
        body,
        mesh=mesh,
        in_specs=(
            P("section", "mp", None),
            P("section", "mp"),
            P("mp", None),
            P("section", None, "mp"),
            P("section", "mp", None),
            P("section", "mp", None),
            P("section"),
            P(),
            P(),
        ),
        out_specs=P("section", "mp", None),
        check_vma=False,
    )
```

```python
import math

import jax
import jax.numpy as jnp
import numpy as np
from jax import lax
from jax.experimental import pallas as pl
from jax.experimental.pallas import tpu as pltpu
from jax.sharding import PartitionSpec as P

HD = 128
HEADS = 32
KVH = 4
SAMP_SECTION = 4
TXT = 128
TT = 32
MAXT = 4
BLOCK = MAXT * TT
SLOTS = SAMP_SECTION * BLOCK
F32 = jnp.float32
BF16 = jnp.bfloat16
VMEM_LIMIT = 24 * 1024 * 1024
QUICK = pl.CostEstimate(flops=1, bytes_accessed=1, transcendentals=0)
VMEM_SMALL = 16 * 1024 * 1024


def ring_order(count):
    wide = 2 if count <= 8 else 4
    tall = count // wide
    if count < 4 or count % wide or tall % 2:
        return list(range(count))
    order = [row * wide for row in range(tall)]
    for turn, row in enumerate(reversed(range(tall))):
        columns = range(1, wide) if turn % 2 == 0 else range(wide - 1, 0, -1)
        order += [row * wide + column for column in columns]
    return order


def own_samples(tile_counts, section_table, section_id):
    samples_all = tile_counts.shape[0]
    sample_ids = jnp.arange(samples_all, dtype=jnp.int32)
    same_section = section_table[None, :] == section_table[:, None]
    before = sample_ids[None, :] < sample_ids[:, None]
    ranking = jnp.sum((same_section & before).astype(jnp.int32), axis=1)
    picked = (section_table[None, :] == section_id) & (
        ranking[None, :] == jnp.arange(SAMP_SECTION, dtype=jnp.int32)[:, None]
    )
    first_row = TT * jnp.sum(jnp.where(before, tile_counts[None, :], 0), axis=1)
    counts_own = jnp.sum(jnp.where(picked, tile_counts[None, :], 0), axis=1)
    starts_own = jnp.sum(jnp.where(picked, first_row[None, :], 0), axis=1)
    return starts_own, counts_own


def add(one, other):
    return (one.astype(F32) + other.astype(F32)).astype(BF16)


def params(limit=VMEM_LIMIT):
    return pltpu.CompilerParams(vmem_limit_bytes=limit)


def total_of(groups):
    parts, count = len(groups), len(groups[0])
    part_rows, columns = groups[0][0].shape
    rows = parts * part_rows

    def kernel(*refs):
        for part in range(parts):
            total = refs[part * count][...].astype(F32)
            for ref in refs[part * count + 1 : (part + 1) * count]:
                total += ref[...].astype(F32)
            refs[-1][part * part_rows : (part + 1) * part_rows, :] = total.astype(BF16)

    return pl.pallas_call(
        kernel,
        in_specs=[pl.BlockSpec(memory_space=pltpu.VMEM)] * (parts * count),
        out_specs=pl.BlockSpec(memory_space=pltpu.VMEM),
        out_shape=jax.ShapeDtypeStruct((rows, columns), BF16),
        compiler_params=params(VMEM_SMALL),
        cost_estimate=QUICK,
        name="total_of",
    )(*[value for group in groups for value in group])


def project(places, feats, weight, order_len, first, blocks):
    rows, depth = feats.shape
    half = rows // 2
    wide = weight.shape[1] // order_len

    def kernel(places_ref, feats_ref, weight_ref, *out_refs):
        product = jnp.dot(
            feats_ref[...], weight_ref[...], preferred_element_type=F32
        ).astype(BF16)
        for block in range(blocks):

            @pl.when(pl.program_id(0) == block)
            def _():
                out_refs[2 * block][...] = product[:half]
                out_refs[2 * block + 1][...] = product[half:]

    halves = pl.pallas_call(
        kernel,
        grid_spec=pltpu.PrefetchScalarGridSpec(
            num_scalar_prefetch=1,
            grid=(blocks,),
            in_specs=[
                pl.BlockSpec((rows, depth), lambda i, places: (0, 0)),
                pl.BlockSpec((depth, wide), lambda i, places: (0, places[first + i])),
            ],
            out_specs=[pl.BlockSpec((half, wide), lambda i, places: (0, 0))] * (2 * blocks),
        ),
        out_shape=[jax.ShapeDtypeStruct((half, wide), BF16)] * (2 * blocks),
        compiler_params=params(56 * 1024 * 1024),
        cost_estimate=pl.CostEstimate(
            flops=2 * rows * depth * wide * blocks,
            bytes_accessed=2 * (depth + rows) * wide * blocks,
            transcendentals=0,
        ),
        name="project",
    )(places, feats, weight)
    return [halves[2 * block : 2 * block + 2] for block in range(blocks)]


def key_values(meta, pieces, weight, order_len, section_count, sharing):
    feat_rows = pieces[0].shape[0]
    depth, width = weight.shape
    kv_rows = SLOTS // sharing
    half_width = width // 2
    count = len(pieces)

    def kernel(meta_ref, *refs):
        piece_refs, weight_ref = refs[:count], refs[count]
        out_refs, kv_ref = refs[count + 1 : -1], refs[-1]
        section = meta_ref[order_len + 1]
        slot = lax.broadcasted_iota(jnp.int32, (BLOCK, feat_rows), 0)
        packed = lax.broadcasted_iota(jnp.int32, (BLOCK, feat_rows), 1)
        for sample in range(SAMP_SECTION):
            start = meta_ref[order_len + 2 + sample]
            live = TT * meta_ref[order_len + 2 + SAMP_SECTION + sample]
            image = jnp.zeros((BLOCK, depth), F32)
            for index in range(count):
                step, swapped = index // 2, index % 2
                origin = lax.rem(section + (section_count - 2 * step), section_count)
                if swapped:
                    origin = origin + 1 - 2 * lax.rem(origin, 2)
                chosen = (slot < live) & (packed == slot + (start - origin * feat_rows))
                image += jnp.dot(
                    chosen.astype(F32).astype(BF16),
                    piece_refs[index][...],
                    preferred_element_type=F32,
                )
            kv_ref[sample * BLOCK : (sample + 1) * BLOCK, :] = jnp.dot(
                image.astype(BF16), weight_ref[...], preferred_element_type=F32
            ).astype(BF16)
        for index in range(order_len):
            target = meta_ref[index]
            row = pl.multiple_of(lax.rem(target, sharing) * kv_rows, kv_rows)
            column = pl.multiple_of(target // sharing * HD, HD)
            out_refs[index][:, :HD] = kv_ref[pl.ds(row, kv_rows), pl.ds(column, HD)]
            out_refs[index][:, HD:] = kv_ref[
                pl.ds(row, kv_rows), pl.ds(pl.multiple_of(column + half_width, HD), HD)
            ]

    whole = pl.BlockSpec(memory_space=pltpu.VMEM)
    return pl.pallas_call(
        kernel,
        in_specs=[pl.BlockSpec(memory_space=pltpu.SMEM)] + [whole] * (count + 1),
        out_specs=[whole] * order_len,
        out_shape=[jax.ShapeDtypeStruct((kv_rows, 2 * HD), BF16)] * order_len,
        scratch_shapes=[pltpu.VMEM((SLOTS, width), BF16)],
        compiler_params=params(),
        cost_estimate=QUICK,
        name="key_values",
    )(meta, *pieces, weight)


def query(chunks, weight):
    rows = sum(chunk.shape[0] for chunk in chunks)
    depth, width = weight.shape
    wide = min(2 * HD, width)
    count = len(chunks)

    def kernel(*refs):
        chunk_refs, weight_ref, out_ref = refs[:count], refs[count], refs[count + 1]
        rows_ref, scale_ref = refs[count + 2 :]

        @pl.when(pl.program_id(0) == 0)
        def _():
            first = 0
            for chunk_ref in chunk_refs:
                place = slice(first, first + chunk_ref.shape[0])
                chunk = chunk_ref[...]
                wider = chunk.astype(F32)
                rows_ref[place, :] = chunk
                scale_ref[place, :] = lax.rsqrt(
                    jnp.mean(wider * wider, axis=-1, keepdims=True) + 1e-05
                )
                first += chunk_ref.shape[0]

        projected = jnp.dot(rows_ref[...], weight_ref[...], preferred_element_type=F32)
        projected = projected * scale_ref[...]
        for head in range(wide // HD):
            one = projected[:, head * HD : (head + 1) * HD]
            one = one * lax.rsqrt(jnp.mean(one * one, axis=-1, keepdims=True) + 1e-06)
            out_ref[:, head * HD : (head + 1) * HD] = one.astype(BF16)

    return pl.pallas_call(
        kernel,
        grid=(width // wide,),
        in_specs=[pl.BlockSpec(chunk.shape, lambda i: (0, 0)) for chunk in chunks]
        + [pl.BlockSpec((depth, wide), lambda i: (0, i))],
        out_specs=pl.BlockSpec((rows, wide), lambda i: (0, i)),
        out_shape=jax.ShapeDtypeStruct((rows, width), BF16),
        scratch_shapes=[pltpu.VMEM((rows, depth), BF16), pltpu.VMEM((rows, 1), F32)],
        compiler_params=params(),
        cost_estimate=pl.CostEstimate(
            flops=2 * rows * depth * width,
            bytes_accessed=2 * depth * (width + rows),
            transcendentals=0,
        ),
        name="query",
    )(*chunks, weight)


def attend(meta, queries, kv_pieces, weight, indices, sizes, order_len):
    text_rows = queries.shape[0] // len(indices)
    rows, width = queries.shape
    heads = width // HD
    sharing = len(kv_pieces)
    kv_rows = SLOTS // sharing
    columns = weight.shape[1]
    wide = min(1024, columns)
    tall = min(64, width)

    def kernel(meta_ref, query_ref, *refs):
        kv_refs, weight_ref = refs[:sharing], refs[sharing]
        out_refs = refs[sharing + 1 : -5]
        key_ref, value_ref, attended_ref, held_ref, sems = refs[-5:]
        step = pl.program_id(0)

        def fetch(index):
            place = pl.ds(index * tall, tall)
            return pltpu.make_async_copy(
                weight_ref.at[place, :], held_ref.at[place, :], sems.at[index]
            )

        @pl.when(step == 0)
        def _():
            for index in range(width // tall):
                fetch(index).start()
            mine = lax.rem(meta_ref[order_len], sharing)
            for piece in range(sharing):
                row = pl.multiple_of(
                    lax.rem(mine + sharing - piece, sharing) * kv_rows, kv_rows
                )
                keys = kv_refs[piece][:, :HD].astype(F32)
                keys = keys * lax.rsqrt(jnp.mean(keys * keys, axis=-1, keepdims=True) + 1e-06)
                key_ref[pl.ds(row, kv_rows), :] = keys.astype(BF16)
                value_ref[pl.ds(row, kv_rows), :] = kv_refs[piece][:, HD:]
            for place, index in enumerate(indices):
                sample = meta_ref[index] * text_rows // TXT
                slots = pl.ds(pl.multiple_of(sample * BLOCK, BLOCK), BLOCK)
                live = TT * meta_ref[order_len + 2 + SAMP_SECTION + sample]
                first = place * text_rows
                own = query_ref[first : first + text_rows, :]
                stacked = jnp.concatenate(
                    [own[:, h * HD : (h + 1) * HD] for h in range(heads)], axis=0
                )
                scores = lax.dot_general(
                    stacked,
                    key_ref[slots, :],
                    (((1,), (1,)), ((), ())),
                    preferred_element_type=F32,
                ) * (1.0 / math.sqrt(HD))
                slot = lax.broadcasted_iota(jnp.int32, scores.shape, 1)
                raised = jnp.where(slot < live, jnp.exp(scores), 0.0)
                weights = (raised / jnp.sum(raised, axis=-1, keepdims=True)).astype(BF16)
                result = jnp.dot(
                    weights, value_ref[slots, :], preferred_element_type=F32
                ).astype(BF16)
                for h in range(heads):
                    attended_ref[first : first + text_rows, h * HD : (h + 1) * HD] = result[
                        h * text_rows : (h + 1) * text_rows
                    ]
            for index in range(width // tall):
                fetch(index).wait()

        product = jnp.dot(
            attended_ref[...],
            held_ref[:, pl.ds(pl.multiple_of(step * wide, wide), wide)],
            preferred_element_type=F32,
        ).astype(BF16)
        first = 0
        for out_ref, size in zip(out_refs, sizes):
            out_ref[...] = product[first : first + size]
            first += size

    return pl.pallas_call(
        kernel,
        grid_spec=pltpu.PrefetchScalarGridSpec(
            num_scalar_prefetch=1,
            grid=(columns // wide,),
            in_specs=[pl.BlockSpec((rows, width), lambda i, meta: (0, 0))]
            + [pl.BlockSpec(piece.shape, lambda i, meta: (0, 0)) for piece in kv_pieces]
            + [pl.BlockSpec(memory_space=pl.ANY)],
            out_specs=[pl.BlockSpec((size, wide), lambda i, meta: (0, i)) for size in sizes],
            scratch_shapes=[
                pltpu.VMEM((SLOTS, HD), BF16),
                pltpu.VMEM((SLOTS, HD), BF16),
                pltpu.VMEM((rows, width), BF16),
                pltpu.VMEM((width, columns), BF16),
                pltpu.SemaphoreType.DMA((width // tall,)),
            ],
        ),
        out_shape=[jax.ShapeDtypeStruct((size, columns), BF16) for size in sizes],
        compiler_params=params(),
        cost_estimate=pl.CostEstimate(
            flops=8 * rows * width * columns,
            bytes_accessed=8 * width * columns,
            transcendentals=rows * heads * BLOCK,
        ),
        name="attend",
    )(meta, queries, *kv_pieces, weight)


def after(value, *others):
    if not others:
        return value
    return lax.optimization_barrier((value, *others))[0]


def local(
    mesh_shape,
    text_state,
    tile_feats,
    w_proj,
    w_query,
    w_kv,
    w_out,
    attn_gate,
    tile_counts,
    section_table,
):
    mp_count, section_count = mesh_shape["mp"], mesh_shape["section"]
    ring = ring_order(mp_count)
    far = mp_count // 2
    sharing = mp_count // KVH
    order = [far]
    for distance in range(far - 1, 0, -1):
        order += [-distance, distance]
    order.append(0)
    index_of = {offset: index for index, offset in enumerate(order)}
    index_of[-far] = 0
    table = np.array(
        [
            [ring[(ring.index(m) + offset) % mp_count] for offset in order] + [m, s]
            for s in range(section_count)
            for m in range(mp_count)
        ],
        np.int32,
    )
    device = lax.axis_index(("section", "mp"))
    places = lax.dynamic_slice(
        jnp.asarray(table), (device, 0), (1, mp_count + 2)
    ).reshape(-1)
    starts, counts = own_samples(tile_counts, section_table, places[mp_count + 1])
    meta = jnp.concatenate([places, starts, counts])

    up_pairs = [(ring[i], ring[(i + 1) % mp_count]) for i in range(mp_count)]
    down_pairs = [(target, source) for source, target in up_pairs]

    def up(value):
        return lax.ppermute(value, "mp", up_pairs)

    def down(value):
        return lax.ppermute(value, "mp", down_pairs)

    def across(pairs):
        return [
            (s * mp_count + a, ((s + 1) % section_count) * mp_count + b)
            for s in range(section_count)
            for a, b in pairs
        ]

    def up_across(value):
        return lax.ppermute(value, ("section", "mp"), across(up_pairs))

    def down_across(value):
        return lax.ppermute(value, ("section", "mp"), across(down_pairs))

    def to_next(value):
        return lax.ppermute(
            value, "section", [(s, (s + 1) % section_count) for s in range(section_count)]
        )

    def ring_sums(chains, hold=lambda left, value: value, turn=()):
        running = [part(sign * distance) for part, distance, sign, _, _ in chains]
        for hop in range(far):
            for index, (part, distance, sign, move, last) in enumerate(chains):
                left = distance - hop
                if left == 1:
                    running[index] = last(hold(left, running[index]))
                elif left > 1:
                    came = after(move(hold(left, running[index])), *turn)
                    running[index] = add(came, part(sign * (left - 1)))
                    turn = [running[index]]
        return running

    def both_ways(part, distance_up, distance_down, last_up=up, last_down=down):
        return [
            (part, distance_up, 1, up, last_up if distance_up == far else up),
            (part, distance_down, -1, down, last_down if distance_down == far else down),
        ]

    text_own = text_state[0]
    text_rows = text_own.shape[0]
    parts = 2 if text_rows % 32 == 0 else 1
    cut = text_rows // parts
    reach = [(far, far - 1), (far - 1, far)][:parts]
    text_next = to_next(text_own)
    gate_next = to_next(attn_gate)
    from_below, from_above = [text_own], [text_own]

    def text_round(*first):
        from_below.append(up(after(from_below[-1], *first)))
        from_above.append(down(after(from_above[-1], *first)))

    text_round()

    image_parts = project(places, tile_feats, w_proj, mp_count, 0, 1)
    image_parts += project(places, tile_feats, w_proj, mp_count, 1, mp_count - 1)
    image_chains = [
        chain
        for half, distances in enumerate(((far, far - 1), (far - 1, far)))
        for chain in both_ways(
            lambda offset, half=half: image_parts[index_of[offset]][half], *distances
        )
    ]

    def image_hold(left, value):
        return after(value, text_next) if left == 1 else value

    turns = [0, 3, 1, 2]
    came = ring_sums(
        [image_chains[turn] for turn in turns],
        image_hold,
        turn=[gate_next, from_below[1], from_above[1]],
    )
    came = [came[turns.index(index)] for index in range(4)]
    image_cols = total_of(
        [[image_parts[index_of[0]][half], *came[2 * half : 2 * half + 2]] for half in range(2)]
    )

    text_round(image_cols)
    weight_query, weight_out = w_query[0], w_out[0]
    queries = {
        0: query([text_own], weight_query),
        1: query([from_below[1], from_above[1]], weight_query),
    }

    pieces = []
    moving = image_cols
    for step in range(section_count // 2):
        pieces += [
            moving,
            lax.ppermute(moving, "section", [(s, s ^ 1) for s in range(section_count)]),
        ]
        if step + 1 < section_count // 2:
            moving = lax.ppermute(
                moving,
                "section",
                [(s, (s + 2) % section_count) for s in range(section_count)],
            )
            if step == 0:
                moving = after(moving, queries[0], queries[1])

    kv_part = key_values(meta, pieces, w_kv[0], mp_count, section_count, sharing)

    for distance in range(3, far - 1):
        text_round(*([kv_part[0]] if distance == 3 else []))
    below, above = (after(value[-1], kv_part[0]) for value in (from_below, from_above))
    low = slice(text_rows - cut, text_rows)
    onward = [up(below[:cut]), down(above[low])]
    sent, behind = [], []

    def kv_hold(left, value):
        sent.append(value)
        if len(sent) == 4 and parts == 2:
            behind.append(up(after(below[cut:], sent[2])))
            behind.append(down(after(above[: text_rows - cut], sent[3])))
        if left == min(2, far - 1):
            return after(value, *onward)
        return after(value, *behind) if left == 1 else value

    came = ring_sums(both_ways(lambda offset: kv_part[index_of[offset]], far, far - 1), kv_hold)
    kv_own = (
        kv_part[index_of[0]].astype(F32) + came[0].astype(F32) + came[1].astype(F32)
    ).astype(BF16)
    if far > 2:
        last_chunks = [onward[0], *behind, onward[1]]
        queries[far - 1] = query(last_chunks, weight_query)
        kv_own = after(kv_own, queries[far - 1])
    kv_pieces = [kv_own]
    for step in range(1, sharing):
        pairs = [
            (m, m // sharing * sharing + (m % sharing + step) % sharing) for m in range(mp_count)
        ]
        kv_pieces.append(lax.ppermute(kv_own, "mp", pairs))

    far_chunks = [up(after(onward[0], kv_own))]
    if parts == 2:
        far_chunks.append(down(after(onward[1], kv_own)))

    def attend_to(offsets, rows):
        indices = [index_of[offset] for offset in offsets]
        sizes = [cut] * (parts * len(offsets))
        return attend(meta, rows, kv_pieces, weight_out, indices, sizes, mp_count)

    first = [1 - far, far - 1]
    first_part = attend_to(first, queries[far - 1])
    rest = [0] + [sign * distance for distance in range(1, far - 1) for sign in (-1, 1)]
    for distance in range(2, far - 1):
        below = after(from_below[distance], first_part[0])
        queries[distance] = query([below, from_above[distance]], weight_query)
    rest_queries = jnp.concatenate([queries[distance] for distance in range(far - 1)], axis=0)
    far_queries = after(query(far_chunks, weight_query), rest_queries, first_part[0])
    far_part = attend_to([far], far_queries)
    rest_part = attend_to(rest, after(rest_queries, far_part[0]))
    near_part = list(first_part) + list(rest_part)
    out_parts = {
        offset: near_part[parts * i :][:parts] for i, offset in enumerate(first + rest)
    }
    out_parts[far] = out_parts[-far] = far_part

    branch_chains = [
        chain
        for part, distances in enumerate(reach)
        for chain in both_ways(
            lambda offset, part=part: out_parts[offset][part],
            *distances,
            up_across,
            down_across,
        )
    ]
    turns = [1, 2, 0, 3] if parts == 2 else [1, 0]
    came = ring_sums([branch_chains[turn] for turn in turns])
    came = [came[turns.index(index)] for index in range(2 * parts)]
    near_came = [came[1], came[2]] if parts == 2 else [came[1]]
    far_came = [came[0], came[3]] if parts == 2 else [came[0]]
    own_next = to_next(
        jnp.concatenate(
            [add(out_parts[0][part], near_came[part]) for part in range(parts)], axis=0
        )
    )
    results = []
    for part in range(parts):
        place = slice(part * cut, (part + 1) * cut)
        branch = own_next[place].astype(F32) + far_came[part].astype(F32)
        results.append(
            (text_next[place].astype(F32) + jnp.tanh(gate_next[0]) * branch).astype(BF16)
        )
    return jnp.concatenate(results, axis=0)[None]


def solution(mesh):
    mesh_shape = dict(mesh.shape)

    def body(*arrays):
        return local(mesh_shape, *arrays)

    return jax.shard_map(
        body,
        mesh=mesh,
        in_specs=(
            P("section", "mp", None),
            P("section", "mp"),
            P("mp", None),
            P("section", None, "mp"),
            P("section", "mp", None),
            P("section", "mp", None),
            P("section"),
            P(),
            P(),
        ),
        out_specs=P("section", "mp", None),
        check_vma=False,
    )
```

```python
import math

import jax
import jax.numpy as jnp
import numpy as np
from jax import lax
from jax.experimental import pallas as pl
from jax.experimental.pallas import tpu as pltpu
from jax.sharding import PartitionSpec as P

HD = 128
HEADS = 32
KVH = 4
SAMP_SECTION = 4
TXT = 128
TT = 32
MAXT = 4
BLOCK = MAXT * TT
SLOTS = SAMP_SECTION * BLOCK
F32 = jnp.float32
BF16 = jnp.bfloat16
VMEM_LIMIT = 24 * 1024 * 1024
QUICK = pl.CostEstimate(flops=1, bytes_accessed=1, transcendentals=0)
VMEM_SMALL = 16 * 1024 * 1024


def ring_order(count):
    wide = 2 if count <= 8 else 4
    tall = count // wide
    if count < 4 or count % wide or tall % 2:
        return list(range(count))
    order = [row * wide for row in range(tall)]
    for turn, row in enumerate(reversed(range(tall))):
        columns = range(1, wide) if turn % 2 == 0 else range(wide - 1, 0, -1)
        order += [row * wide + column for column in columns]
    return order


def own_samples(tile_counts, section_table, section_id):
    samples_all = tile_counts.shape[0]
    sample_ids = jnp.arange(samples_all, dtype=jnp.int32)
    same_section = section_table[None, :] == section_table[:, None]
    before = sample_ids[None, :] < sample_ids[:, None]
    ranking = jnp.sum((same_section & before).astype(jnp.int32), axis=1)
    picked = (section_table[None, :] == section_id) & (
        ranking[None, :] == jnp.arange(SAMP_SECTION, dtype=jnp.int32)[:, None]
    )
    first_row = TT * jnp.sum(jnp.where(before, tile_counts[None, :], 0), axis=1)
    counts_own = jnp.sum(jnp.where(picked, tile_counts[None, :], 0), axis=1)
    starts_own = jnp.sum(jnp.where(picked, first_row[None, :], 0), axis=1)
    return starts_own, counts_own


def add(one, other):
    return (one.astype(F32) + other.astype(F32)).astype(BF16)


def params(limit=VMEM_LIMIT):
    return pltpu.CompilerParams(vmem_limit_bytes=limit)


def total_of(groups):
    parts, count = len(groups), len(groups[0])
    part_rows, columns = groups[0][0].shape
    rows = parts * part_rows

    def kernel(*refs):
        for part in range(parts):
            total = refs[part * count][...].astype(F32)
            for ref in refs[part * count + 1 : (part + 1) * count]:
                total += ref[...].astype(F32)
            refs[-1][part * part_rows : (part + 1) * part_rows, :] = total.astype(BF16)

    return pl.pallas_call(
        kernel,
        in_specs=[pl.BlockSpec(memory_space=pltpu.VMEM)] * (parts * count),
        out_specs=pl.BlockSpec(memory_space=pltpu.VMEM),
        out_shape=jax.ShapeDtypeStruct((rows, columns), BF16),
        compiler_params=params(VMEM_SMALL),
        cost_estimate=QUICK,
        name="total_of",
    )(*[value for group in groups for value in group])


def project(places, feats, weight, order_len, first, blocks):
    rows, depth = feats.shape
    half = rows // 2
    wide = weight.shape[1] // order_len

    def kernel(places_ref, feats_ref, weight_ref, *out_refs):
        product = jnp.dot(
            feats_ref[...], weight_ref[...], preferred_element_type=F32
        ).astype(BF16)
        for block in range(blocks):

            @pl.when(pl.program_id(0) == block)
            def _():
                out_refs[2 * block][...] = product[:half]
                out_refs[2 * block + 1][...] = product[half:]

    halves = pl.pallas_call(
        kernel,
        grid_spec=pltpu.PrefetchScalarGridSpec(
            num_scalar_prefetch=1,
            grid=(blocks,),
            in_specs=[
                pl.BlockSpec((rows, depth), lambda i, places: (0, 0)),
                pl.BlockSpec((depth, wide), lambda i, places: (0, places[first + i])),
            ],
            out_specs=[pl.BlockSpec((half, wide), lambda i, places: (0, 0))] * (2 * blocks),
        ),
        out_shape=[jax.ShapeDtypeStruct((half, wide), BF16)] * (2 * blocks),
        compiler_params=params(56 * 1024 * 1024),
        cost_estimate=pl.CostEstimate(
            flops=2 * rows * depth * wide * blocks,
            bytes_accessed=2 * (depth + rows) * wide * blocks,
            transcendentals=0,
        ),
        name="project",
    )(places, feats, weight)
    return [halves[2 * block : 2 * block + 2] for block in range(blocks)]


def key_values(meta, pieces, weight, order_len, section_count, sharing):
    feat_rows = pieces[0].shape[0]
    depth, width = weight.shape
    kv_rows = SLOTS // sharing
    half_width = width // 2
    count = len(pieces)

    def kernel(meta_ref, *refs):
        piece_refs, weight_ref = refs[:count], refs[count]
        out_refs, kv_ref = refs[count + 1 : -1], refs[-1]
        section = meta_ref[order_len + 1]
        slot = lax.broadcasted_iota(jnp.int32, (BLOCK, feat_rows), 0)
        packed = lax.broadcasted_iota(jnp.int32, (BLOCK, feat_rows), 1)
        for sample in range(SAMP_SECTION):
            start = meta_ref[order_len + 2 + sample]
            live = TT * meta_ref[order_len + 2 + SAMP_SECTION + sample]
            image = jnp.zeros((BLOCK, depth), F32)
            for index in range(count):
                step, swapped = index // 2, index % 2
                origin = lax.rem(section + (section_count - 2 * step), section_count)
                if swapped:
                    origin = origin + 1 - 2 * lax.rem(origin, 2)
                chosen = (slot < live) & (packed == slot + (start - origin * feat_rows))
                image += jnp.dot(
                    chosen.astype(F32).astype(BF16),
                    piece_refs[index][...],
                    preferred_element_type=F32,
                )
            kv_ref[sample * BLOCK : (sample + 1) * BLOCK, :] = jnp.dot(
                image.astype(BF16), weight_ref[...], preferred_element_type=F32
            ).astype(BF16)
        for index in range(order_len):
            target = meta_ref[index]
            row = pl.multiple_of(lax.rem(target, sharing) * kv_rows, kv_rows)
            column = pl.multiple_of(target // sharing * HD, HD)
            out_refs[index][:, :HD] = kv_ref[pl.ds(row, kv_rows), pl.ds(column, HD)]
            out_refs[index][:, HD:] = kv_ref[
                pl.ds(row, kv_rows), pl.ds(pl.multiple_of(column + half_width, HD), HD)
            ]

    whole = pl.BlockSpec(memory_space=pltpu.VMEM)
    return pl.pallas_call(
        kernel,
        in_specs=[pl.BlockSpec(memory_space=pltpu.SMEM)] + [whole] * (count + 1),
        out_specs=[whole] * order_len,
        out_shape=[jax.ShapeDtypeStruct((kv_rows, 2 * HD), BF16)] * order_len,
        scratch_shapes=[pltpu.VMEM((SLOTS, width), BF16)],
        compiler_params=params(),
        cost_estimate=QUICK,
        name="key_values",
    )(meta, *pieces, weight)


def query(chunks, weight):
    rows = sum(chunk.shape[0] for chunk in chunks)
    depth, width = weight.shape
    wide = min(2 * HD, width)
    count = len(chunks)

    def kernel(*refs):
        chunk_refs, weight_ref, out_ref = refs[:count], refs[count], refs[count + 1]
        rows_ref, scale_ref = refs[count + 2 :]

        @pl.when(pl.program_id(0) == 0)
        def _():
            first = 0
            for chunk_ref in chunk_refs:
                place = slice(first, first + chunk_ref.shape[0])
                chunk = chunk_ref[...]
                wider = chunk.astype(F32)
                rows_ref[place, :] = chunk
                scale_ref[place, :] = lax.rsqrt(
                    jnp.mean(wider * wider, axis=-1, keepdims=True) + 1e-05
                )
                first += chunk_ref.shape[0]

        projected = jnp.dot(rows_ref[...], weight_ref[...], preferred_element_type=F32)
        projected = projected * scale_ref[...]
        for head in range(wide // HD):
            one = projected[:, head * HD : (head + 1) * HD]
            one = one * lax.rsqrt(jnp.mean(one * one, axis=-1, keepdims=True) + 1e-06)
            out_ref[:, head * HD : (head + 1) * HD] = one.astype(BF16)

    return pl.pallas_call(
        kernel,
        grid=(width // wide,),
        in_specs=[pl.BlockSpec(chunk.shape, lambda i: (0, 0)) for chunk in chunks]
        + [pl.BlockSpec((depth, wide), lambda i: (0, i))],
        out_specs=pl.BlockSpec((rows, wide), lambda i: (0, i)),
        out_shape=jax.ShapeDtypeStruct((rows, width), BF16),
        scratch_shapes=[pltpu.VMEM((rows, depth), BF16), pltpu.VMEM((rows, 1), F32)],
        compiler_params=params(),
        cost_estimate=pl.CostEstimate(
            flops=2 * rows * depth * width,
            bytes_accessed=2 * depth * (width + rows),
            transcendentals=0,
        ),
        name="query",
    )(*chunks, weight)


def attend(meta, queries, kv_pieces, weight, indices, sizes, shard_rows, order_len):
    text_rows = queries.shape[0] // len(indices)
    rows, width = queries.shape
    heads = width // HD
    sharing = len(kv_pieces)
    kv_rows = SLOTS // sharing
    columns = weight.shape[1]
    wide = min(1024, columns)
    tall = min(64, width)

    def kernel(meta_ref, query_ref, *refs):
        kv_refs, weight_ref = refs[:sharing], refs[sharing]
        out_refs = refs[sharing + 1 : -5]
        key_ref, value_ref, attended_ref, held_ref, sems = refs[-5:]
        step = pl.program_id(0)

        def fetch(index):
            place = pl.ds(index * tall, tall)
            return pltpu.make_async_copy(
                weight_ref.at[place, :], held_ref.at[place, :], sems.at[index]
            )

        @pl.when(step == 0)
        def _():
            for index in range(width // tall):
                fetch(index).start()
            mine = lax.rem(meta_ref[order_len], sharing)
            for piece in range(sharing):
                row = pl.multiple_of(
                    lax.rem(mine + sharing - piece, sharing) * kv_rows, kv_rows
                )
                keys = kv_refs[piece][:, :HD].astype(F32)
                keys = keys * lax.rsqrt(jnp.mean(keys * keys, axis=-1, keepdims=True) + 1e-06)
                key_ref[pl.ds(row, kv_rows), :] = keys.astype(BF16)
                value_ref[pl.ds(row, kv_rows), :] = kv_refs[piece][:, HD:]
            for place, index in enumerate(indices):
                sample = meta_ref[index] * shard_rows // TXT
                slots = pl.ds(pl.multiple_of(sample * BLOCK, BLOCK), BLOCK)
                live = TT * meta_ref[order_len + 2 + SAMP_SECTION + sample]
                first = place * text_rows
                own = query_ref[first : first + text_rows, :]
                stacked = jnp.concatenate(
                    [own[:, h * HD : (h + 1) * HD] for h in range(heads)], axis=0
                )
                scores = lax.dot_general(
                    stacked,
                    key_ref[slots, :],
                    (((1,), (1,)), ((), ())),
                    preferred_element_type=F32,
                ) * (1.0 / math.sqrt(HD))
                slot = lax.broadcasted_iota(jnp.int32, scores.shape, 1)
                raised = jnp.where(slot < live, jnp.exp(scores), 0.0)
                weights = (raised / jnp.sum(raised, axis=-1, keepdims=True)).astype(BF16)
                result = jnp.dot(
                    weights, value_ref[slots, :], preferred_element_type=F32
                ).astype(BF16)
                for h in range(heads):
                    attended_ref[first : first + text_rows, h * HD : (h + 1) * HD] = result[
                        h * text_rows : (h + 1) * text_rows
                    ]
            for index in range(width // tall):
                fetch(index).wait()

        product = jnp.dot(
            attended_ref[...],
            held_ref[:, pl.ds(pl.multiple_of(step * wide, wide), wide)],
            preferred_element_type=F32,
        ).astype(BF16)
        first = 0
        for out_ref, size in zip(out_refs, sizes):
            out_ref[...] = product[first : first + size]
            first += size

    return pl.pallas_call(
        kernel,
        grid_spec=pltpu.PrefetchScalarGridSpec(
            num_scalar_prefetch=1,
            grid=(columns // wide,),
            in_specs=[pl.BlockSpec((rows, width), lambda i, meta: (0, 0))]
            + [pl.BlockSpec(piece.shape, lambda i, meta: (0, 0)) for piece in kv_pieces]
            + [pl.BlockSpec(memory_space=pl.ANY)],
            out_specs=[pl.BlockSpec((size, wide), lambda i, meta: (0, i)) for size in sizes],
            scratch_shapes=[
                pltpu.VMEM((SLOTS, HD), BF16),
                pltpu.VMEM((SLOTS, HD), BF16),
                pltpu.VMEM((rows, width), BF16),
                pltpu.VMEM((width, columns), BF16),
                pltpu.SemaphoreType.DMA((width // tall,)),
            ],
        ),
        out_shape=[jax.ShapeDtypeStruct((size, columns), BF16) for size in sizes],
        compiler_params=params(),
        cost_estimate=pl.CostEstimate(
            flops=8 * rows * width * columns,
            bytes_accessed=8 * width * columns,
            transcendentals=rows * heads * BLOCK,
        ),
        name="attend",
    )(meta, queries, *kv_pieces, weight)


def after(value, *others):
    if not others:
        return value
    return lax.optimization_barrier((value, *others))[0]


def local(
    mesh_shape,
    text_state,
    tile_feats,
    w_proj,
    w_query,
    w_kv,
    w_out,
    attn_gate,
    tile_counts,
    section_table,
):
    mp_count, section_count = mesh_shape["mp"], mesh_shape["section"]
    ring = ring_order(mp_count)
    far = mp_count // 2
    sharing = mp_count // KVH
    order = [far]
    for distance in range(far - 1, 0, -1):
        order += [-distance, distance]
    order.append(0)
    index_of = {offset: index for index, offset in enumerate(order)}
    index_of[-far] = 0
    table = np.array(
        [
            [ring[(ring.index(m) + offset) % mp_count] for offset in order] + [m, s]
            for s in range(section_count)
            for m in range(mp_count)
        ],
        np.int32,
    )
    device = lax.axis_index(("section", "mp"))
    places = lax.dynamic_slice(
        jnp.asarray(table), (device, 0), (1, mp_count + 2)
    ).reshape(-1)
    starts, counts = own_samples(tile_counts, section_table, places[mp_count + 1])
    meta = jnp.concatenate([places, starts, counts])

    up_pairs = [(ring[i], ring[(i + 1) % mp_count]) for i in range(mp_count)]
    down_pairs = [(target, source) for source, target in up_pairs]

    def up(value):
        return lax.ppermute(value, "mp", up_pairs)

    def down(value):
        return lax.ppermute(value, "mp", down_pairs)

    def across(pairs):
        return [
            (s * mp_count + a, ((s + 1) % section_count) * mp_count + b)
            for s in range(section_count)
            for a, b in pairs
        ]

    def up_across(value):
        return lax.ppermute(value, ("section", "mp"), across(up_pairs))

    def down_across(value):
        return lax.ppermute(value, ("section", "mp"), across(down_pairs))

    def to_next(value):
        return lax.ppermute(
            value, "section", [(s, (s + 1) % section_count) for s in range(section_count)]
        )

    def ring_sums(chains, hold=lambda left, value: value, turn=()):
        running = [part(sign * distance) for part, distance, sign, _, _ in chains]
        for hop in range(far):
            for index, (part, distance, sign, move, last) in enumerate(chains):
                left = distance - hop
                if left == 1:
                    running[index] = last(hold(left, running[index]))
                elif left > 1:
                    came = after(move(hold(left, running[index])), *turn)
                    running[index] = add(came, part(sign * (left - 1)))
                    turn = [running[index]]
        return running

    def both_ways(part, distance_up, distance_down, last_up=up, last_down=down):
        return [
            (part, distance_up, 1, up, last_up),
            (part, distance_down, -1, down, last_down),
        ]

    text_own = text_state[0]
    text_rows = text_own.shape[0]
    parts = 2 if text_rows % 32 == 0 else 1
    cut = text_rows // parts
    reach = [(far, far - 1), (far - 1, far)][:parts]
    text_next = to_next(text_own)
    gate_next = to_next(attn_gate)
    from_below, from_above = [text_own], [text_own]

    def text_round(*first):
        from_below.append(up(after(from_below[-1], *first)))
        from_above.append(down(after(from_above[-1], *first)))

    text_round()

    image_parts = project(places, tile_feats, w_proj, mp_count, 0, 1)
    image_parts += project(places, tile_feats, w_proj, mp_count, 1, mp_count - 1)
    image_chains = [
        chain
        for half, distances in enumerate(((far, far - 1), (far - 1, far)))
        for chain in both_ways(
            lambda offset, half=half: image_parts[index_of[offset]][half], *distances
        )
    ]

    def image_hold(left, value):
        return after(value, text_next) if left == 1 else value

    turns = [0, 3, 1, 2]
    came = ring_sums(
        [image_chains[turn] for turn in turns],
        image_hold,
        turn=[gate_next, from_below[1], from_above[1]],
    )
    came = [came[turns.index(index)] for index in range(4)]
    image_cols = total_of(
        [[image_parts[index_of[0]][half], *came[2 * half : 2 * half + 2]] for half in range(2)]
    )

    text_round(image_cols)
    weight_query, weight_out = w_query[0], w_out[0]
    queries = {
        0: query([text_own], weight_query),
        1: query([from_below[1], from_above[1]], weight_query),
    }

    pieces = []
    moving = image_cols
    for step in range(section_count // 2):
        pieces += [
            moving,
            lax.ppermute(moving, "section", [(s, s ^ 1) for s in range(section_count)]),
        ]
        if step + 1 < section_count // 2:
            moving = lax.ppermute(
                moving,
                "section",
                [(s, (s + 2) % section_count) for s in range(section_count)],
            )
            if step == 0:
                moving = after(moving, queries[0], queries[1])

    kv_part = key_values(meta, pieces, w_kv[0], mp_count, section_count, sharing)

    for distance in range(3, far - 1):
        text_round(*([kv_part[0]] if distance == 3 else []))
    below, above = (after(value[-1], kv_part[0]) for value in (from_below, from_above))
    low = slice(text_rows - cut, text_rows)
    onward = [up(below[:cut]), down(above[low])]
    far_chunks = [up(onward[0])]
    if parts == 2:
        far_chunks.append(down(onward[1]))

    def kv_hold(left, value):
        return after(value, *onward) if left == min(2, far - 1) else value

    came = ring_sums(
        both_ways(lambda offset: kv_part[index_of[offset]], far, far - 1),
        kv_hold,
        turn=[from_below[2], from_above[2]] if far > 2 else [],
    )
    kv_own = (
        kv_part[index_of[0]].astype(F32) + came[0].astype(F32) + came[1].astype(F32)
    ).astype(BF16)
    kv_own = after(kv_own, *far_chunks)
    kv_pieces = [kv_own]
    for step in range(1, sharing):
        pairs = [
            (m, m // sharing * sharing + (m % sharing + step) % sharing) for m in range(mp_count)
        ]
        kv_pieces.append(lax.ppermute(kv_own, "mp", pairs))

    behind = []
    if parts == 2:
        behind = [up(after(below, kv_own)[cut:]), down(after(above, kv_own)[:cut])]

    def attend_to(offsets, rows, sizes):
        indices = [index_of[offset] for offset in offsets]
        return attend(meta, rows, kv_pieces, weight_out, indices, sizes, text_rows, mp_count)

    last = far - 1
    near = [sign * distance for distance in range(1, last) for sign in (-1, 1)]
    out_parts = {offset: [None] * parts for offset in [last, -last]}
    first = [far] * parts + [-last, last]
    first_queries = query(far_chunks + onward, weight_query)
    first_part = attend_to(first, first_queries, [cut] * len(first))
    out_parts[far] = out_parts[-far] = first_part[:parts]
    out_parts[-last][0], out_parts[last][parts - 1] = first_part[parts:]
    ready = first_part[0]
    for distance in range(2, last):
        rows = [after(from_below[distance], ready), from_above[distance]]
        queries[distance] = query(rows, weight_query)
    rest_queries = jnp.concatenate([queries[distance] for distance in range(last)], axis=0)
    if parts == 2:
        behind_queries = after(query(behind, weight_query), rest_queries, ready)
        behind_part = attend_to([-last, last], behind_queries, [cut] * 2)
        out_parts[-last][1], out_parts[last][0] = behind_part
        ready = behind_part[0]
    sizes = [text_rows] + [cut] * (parts * len(near))
    own_part, *near_part = attend_to([0] + near, after(rest_queries, ready), sizes)
    for index, offset in enumerate(near):
        out_parts[offset] = near_part[parts * index :][:parts]
    own_next = to_next(own_part)

    branch_chains = [
        chain
        for part, distances in enumerate(reach)
        for chain in both_ways(
            lambda offset, part=part: out_parts[offset][part],
            *distances,
            up_across,
            down_across,
        )
    ]

    def branch_hold(left, value):
        if left == 1:
            return after(value, own_next)
        return after(value, *behind) if left == last else value

    turns = [0, 3, 1, 2] if parts == 2 else [0, 1]
    came = ring_sums([branch_chains[turn] for turn in turns], branch_hold)
    came = [came[turns.index(index)] for index in range(2 * parts)]
    results = []
    for part in range(parts):
        place = slice(part * cut, (part + 1) * cut)
        branch = own_next[place].astype(F32)
        for value in came[2 * part : 2 * part + 2]:
            branch = branch + value.astype(F32)
        results.append(
            (text_next[place].astype(F32) + jnp.tanh(gate_next[0]) * branch).astype(BF16)
        )
    return jnp.concatenate(results, axis=0)[None]


def solution(mesh):
    mesh_shape = dict(mesh.shape)

    def body(*arrays):
        return local(mesh_shape, *arrays)

    return jax.shard_map(
        body,
        mesh=mesh,
        in_specs=(
            P("section", "mp", None),
            P("section", "mp"),
            P("mp", None),
            P("section", None, "mp"),
            P("section", "mp", None),
            P("section", "mp", None),
            P("section"),
            P(),
            P(),
        ),
        out_specs=P("section", "mp", None),
        check_vma=False,
    )
```

```python
import math

import jax
import jax.numpy as jnp
import numpy as np
from jax import lax
from jax.experimental import pallas as pl
from jax.experimental.pallas import tpu as pltpu
from jax.sharding import PartitionSpec as P

HD = 128
HEADS = 32
KVH = 4
SAMP_SECTION = 4
TXT = 128
TT = 32
MAXT = 4
BLOCK = MAXT * TT
SLOTS = SAMP_SECTION * BLOCK
F32 = jnp.float32
BF16 = jnp.bfloat16
VMEM_LIMIT = 24 * 1024 * 1024
QUICK = pl.CostEstimate(flops=1, bytes_accessed=1, transcendentals=0)
VMEM_SMALL = 16 * 1024 * 1024


def ring_order(count):
    wide = 2 if count <= 8 else 4
    tall = count // wide
    if count < 4 or count % wide or tall % 2:
        return list(range(count))
    order = [row * wide for row in range(tall)]
    for turn, row in enumerate(reversed(range(tall))):
        columns = range(1, wide) if turn % 2 == 0 else range(wide - 1, 0, -1)
        order += [row * wide + column for column in columns]
    return order


def own_samples(tile_counts, section_table, section_id):
    samples_all = tile_counts.shape[0]
    sample_ids = jnp.arange(samples_all, dtype=jnp.int32)
    same_section = section_table[None, :] == section_table[:, None]
    before = sample_ids[None, :] < sample_ids[:, None]
    ranking = jnp.sum((same_section & before).astype(jnp.int32), axis=1)
    picked = (section_table[None, :] == section_id) & (
        ranking[None, :] == jnp.arange(SAMP_SECTION, dtype=jnp.int32)[:, None]
    )
    first_row = TT * jnp.sum(jnp.where(before, tile_counts[None, :], 0), axis=1)
    counts_own = jnp.sum(jnp.where(picked, tile_counts[None, :], 0), axis=1)
    starts_own = jnp.sum(jnp.where(picked, first_row[None, :], 0), axis=1)
    return starts_own, counts_own


def add(one, other):
    return (one.astype(F32) + other.astype(F32)).astype(BF16)


def params(limit=VMEM_LIMIT):
    return pltpu.CompilerParams(vmem_limit_bytes=limit)


def total_of(groups):
    parts, count = len(groups), len(groups[0])
    part_rows, columns = groups[0][0].shape
    rows = parts * part_rows

    def kernel(*refs):
        for part in range(parts):
            total = refs[part * count][...].astype(F32)
            for ref in refs[part * count + 1 : (part + 1) * count]:
                total += ref[...].astype(F32)
            refs[-1][part * part_rows : (part + 1) * part_rows, :] = total.astype(BF16)

    return pl.pallas_call(
        kernel,
        in_specs=[pl.BlockSpec(memory_space=pltpu.VMEM)] * (parts * count),
        out_specs=pl.BlockSpec(memory_space=pltpu.VMEM),
        out_shape=jax.ShapeDtypeStruct((rows, columns), BF16),
        compiler_params=params(VMEM_SMALL),
        cost_estimate=QUICK,
        name="total_of",
    )(*[value for group in groups for value in group])


def project(places, feats, weight, order_len, first, blocks):
    rows, depth = feats.shape
    half = rows // 2
    wide = weight.shape[1] // order_len

    def kernel(places_ref, feats_ref, weight_ref, *out_refs):
        product = jnp.dot(
            feats_ref[...], weight_ref[...], preferred_element_type=F32
        ).astype(BF16)
        for block in range(blocks):

            @pl.when(pl.program_id(0) == block)
            def _():
                out_refs[2 * block][...] = product[:half]
                out_refs[2 * block + 1][...] = product[half:]

    halves = pl.pallas_call(
        kernel,
        grid_spec=pltpu.PrefetchScalarGridSpec(
            num_scalar_prefetch=1,
            grid=(blocks,),
            in_specs=[
                pl.BlockSpec((rows, depth), lambda i, places: (0, 0)),
                pl.BlockSpec((depth, wide), lambda i, places: (0, places[first + i])),
            ],
            out_specs=[pl.BlockSpec((half, wide), lambda i, places: (0, 0))] * (2 * blocks),
        ),
        out_shape=[jax.ShapeDtypeStruct((half, wide), BF16)] * (2 * blocks),
        compiler_params=params(56 * 1024 * 1024),
        cost_estimate=pl.CostEstimate(
            flops=2 * rows * depth * wide * blocks,
            bytes_accessed=2 * (depth + rows) * wide * blocks,
            transcendentals=0,
        ),
        name="project",
    )(places, feats, weight)
    return [halves[2 * block : 2 * block + 2] for block in range(blocks)]


def key_values(meta, pieces, weight, order_len, section_count, sharing):
    feat_rows = pieces[0].shape[0]
    depth, width = weight.shape
    kv_rows = SLOTS // sharing
    half_width = width // 2
    count = len(pieces)

    def kernel(meta_ref, *refs):
        piece_refs, weight_ref = refs[:count], refs[count]
        out_refs, kv_ref = refs[count + 1 : -1], refs[-1]
        section = meta_ref[order_len + 1]
        slot = lax.broadcasted_iota(jnp.int32, (BLOCK, feat_rows), 0)
        packed = lax.broadcasted_iota(jnp.int32, (BLOCK, feat_rows), 1)
        for sample in range(SAMP_SECTION):
            start = meta_ref[order_len + 2 + sample]
            live = TT * meta_ref[order_len + 2 + SAMP_SECTION + sample]
            image = jnp.zeros((BLOCK, depth), F32)
            for index in range(count):
                step, swapped = index // 2, index % 2
                origin = lax.rem(section + (section_count - 2 * step), section_count)
                if swapped:
                    origin = origin + 1 - 2 * lax.rem(origin, 2)
                chosen = (slot < live) & (packed == slot + (start - origin * feat_rows))
                image += jnp.dot(
                    chosen.astype(F32).astype(BF16),
                    piece_refs[index][...],
                    preferred_element_type=F32,
                )
            kv_ref[sample * BLOCK : (sample + 1) * BLOCK, :] = jnp.dot(
                image.astype(BF16), weight_ref[...], preferred_element_type=F32
            ).astype(BF16)
        for index in range(order_len):
            target = meta_ref[index]
            row = pl.multiple_of(lax.rem(target, sharing) * kv_rows, kv_rows)
            column = pl.multiple_of(target // sharing * HD, HD)
            out_refs[index][:, :HD] = kv_ref[pl.ds(row, kv_rows), pl.ds(column, HD)]
            out_refs[index][:, HD:] = kv_ref[
                pl.ds(row, kv_rows), pl.ds(pl.multiple_of(column + half_width, HD), HD)
            ]

    whole = pl.BlockSpec(memory_space=pltpu.VMEM)
    return pl.pallas_call(
        kernel,
        in_specs=[pl.BlockSpec(memory_space=pltpu.SMEM)] + [whole] * (count + 1),
        out_specs=[whole] * order_len,
        out_shape=[jax.ShapeDtypeStruct((kv_rows, 2 * HD), BF16)] * order_len,
        scratch_shapes=[pltpu.VMEM((SLOTS, width), BF16)],
        compiler_params=params(),
        cost_estimate=QUICK,
        name="key_values",
    )(meta, *pieces, weight)


def query(chunks, weight):
    rows = sum(chunk.shape[0] for chunk in chunks)
    depth, width = weight.shape
    wide = min(2 * HD, width)
    count = len(chunks)

    def kernel(*refs):
        chunk_refs, weight_ref, out_ref = refs[:count], refs[count], refs[count + 1]
        rows_ref, scale_ref = refs[count + 2 :]

        @pl.when(pl.program_id(0) == 0)
        def _():
            first = 0
            for chunk_ref in chunk_refs:
                place = slice(first, first + chunk_ref.shape[0])
                chunk = chunk_ref[...]
                wider = chunk.astype(F32)
                rows_ref[place, :] = chunk
                scale_ref[place, :] = lax.rsqrt(
                    jnp.mean(wider * wider, axis=-1, keepdims=True) + 1e-05
                )
                first += chunk_ref.shape[0]

        projected = jnp.dot(rows_ref[...], weight_ref[...], preferred_element_type=F32)
        projected = projected * scale_ref[...]
        for head in range(wide // HD):
            one = projected[:, head * HD : (head + 1) * HD]
            one = one * lax.rsqrt(jnp.mean(one * one, axis=-1, keepdims=True) + 1e-06)
            out_ref[:, head * HD : (head + 1) * HD] = one.astype(BF16)

    return pl.pallas_call(
        kernel,
        grid=(width // wide,),
        in_specs=[pl.BlockSpec(chunk.shape, lambda i: (0, 0)) for chunk in chunks]
        + [pl.BlockSpec((depth, wide), lambda i: (0, i))],
        out_specs=pl.BlockSpec((rows, wide), lambda i: (0, i)),
        out_shape=jax.ShapeDtypeStruct((rows, width), BF16),
        scratch_shapes=[pltpu.VMEM((rows, depth), BF16), pltpu.VMEM((rows, 1), F32)],
        compiler_params=params(),
        cost_estimate=pl.CostEstimate(
            flops=2 * rows * depth * width,
            bytes_accessed=2 * depth * (width + rows),
            transcendentals=0,
        ),
        name="query",
    )(*chunks, weight)


def attend(meta, queries, kv_pieces, weight, indices, sizes, shard_rows, order_len):
    text_rows = queries.shape[0] // len(indices)
    rows, width = queries.shape
    heads = width // HD
    sharing = len(kv_pieces)
    kv_rows = SLOTS // sharing
    columns = weight.shape[1]
    wide = min(1024, columns)
    tall = min(64, width)

    def kernel(meta_ref, query_ref, *refs):
        kv_refs, weight_ref = refs[:sharing], refs[sharing]
        out_refs = refs[sharing + 1 : -5]
        key_ref, value_ref, attended_ref, held_ref, sems = refs[-5:]
        step = pl.program_id(0)

        def fetch(index):
            place = pl.ds(index * tall, tall)
            return pltpu.make_async_copy(
                weight_ref.at[place, :], held_ref.at[place, :], sems.at[index]
            )

        @pl.when(step == 0)
        def _():
            for index in range(width // tall):
                fetch(index).start()
            mine = lax.rem(meta_ref[order_len], sharing)
            for piece in range(sharing):
                row = pl.multiple_of(
                    lax.rem(mine + sharing - piece, sharing) * kv_rows, kv_rows
                )
                keys = kv_refs[piece][:, :HD].astype(F32)
                keys = keys * lax.rsqrt(jnp.mean(keys * keys, axis=-1, keepdims=True) + 1e-06)
                key_ref[pl.ds(row, kv_rows), :] = keys.astype(BF16)
                value_ref[pl.ds(row, kv_rows), :] = kv_refs[piece][:, HD:]
            for place, index in enumerate(indices):
                sample = meta_ref[index] * shard_rows // TXT
                slots = pl.ds(pl.multiple_of(sample * BLOCK, BLOCK), BLOCK)
                live = TT * meta_ref[order_len + 2 + SAMP_SECTION + sample]
                first = place * text_rows
                own = query_ref[first : first + text_rows, :]
                stacked = jnp.concatenate(
                    [own[:, h * HD : (h + 1) * HD] for h in range(heads)], axis=0
                )
                scores = lax.dot_general(
                    stacked,
                    key_ref[slots, :],
                    (((1,), (1,)), ((), ())),
                    preferred_element_type=F32,
                ) * (1.0 / math.sqrt(HD))
                slot = lax.broadcasted_iota(jnp.int32, scores.shape, 1)
                raised = jnp.where(slot < live, jnp.exp(scores), 0.0)
                weights = (raised / jnp.sum(raised, axis=-1, keepdims=True)).astype(BF16)
                result = jnp.dot(
                    weights, value_ref[slots, :], preferred_element_type=F32
                ).astype(BF16)
                for h in range(heads):
                    attended_ref[first : first + text_rows, h * HD : (h + 1) * HD] = result[
                        h * text_rows : (h + 1) * text_rows
                    ]
            for index in range(width // tall):
                fetch(index).wait()

        product = jnp.dot(
            attended_ref[...],
            held_ref[:, pl.ds(pl.multiple_of(step * wide, wide), wide)],
            preferred_element_type=F32,
        ).astype(BF16)
        first = 0
        for out_ref, size in zip(out_refs, sizes):
            out_ref[...] = product[first : first + size]
            first += size

    return pl.pallas_call(
        kernel,
        grid_spec=pltpu.PrefetchScalarGridSpec(
            num_scalar_prefetch=1,
            grid=(columns // wide,),
            in_specs=[pl.BlockSpec((rows, width), lambda i, meta: (0, 0))]
            + [pl.BlockSpec(piece.shape, lambda i, meta: (0, 0)) for piece in kv_pieces]
            + [pl.BlockSpec(memory_space=pl.ANY)],
            out_specs=[pl.BlockSpec((size, wide), lambda i, meta: (0, i)) for size in sizes],
            scratch_shapes=[
                pltpu.VMEM((SLOTS, HD), BF16),
                pltpu.VMEM((SLOTS, HD), BF16),
                pltpu.VMEM((rows, width), BF16),
                pltpu.VMEM((width, columns), BF16),
                pltpu.SemaphoreType.DMA((width // tall,)),
            ],
        ),
        out_shape=[jax.ShapeDtypeStruct((size, columns), BF16) for size in sizes],
        compiler_params=params(),
        cost_estimate=pl.CostEstimate(
            flops=8 * rows * width * columns,
            bytes_accessed=8 * width * columns,
            transcendentals=rows * heads * BLOCK,
        ),
        name="attend",
    )(meta, queries, *kv_pieces, weight)


def after(value, *others):
    if not others:
        return value
    return lax.optimization_barrier((value, *others))[0]


def local(
    mesh_shape,
    text_state,
    tile_feats,
    w_proj,
    w_query,
    w_kv,
    w_out,
    attn_gate,
    tile_counts,
    section_table,
):
    mp_count, section_count = mesh_shape["mp"], mesh_shape["section"]
    ring = ring_order(mp_count)
    far = mp_count // 2
    sharing = mp_count // KVH
    order = [far]
    for distance in range(far - 1, 0, -1):
        order += [-distance, distance]
    order.append(0)
    index_of = {offset: index for index, offset in enumerate(order)}
    index_of[-far] = 0
    table = np.array(
        [
            [ring[(ring.index(m) + offset) % mp_count] for offset in order] + [m, s]
            for s in range(section_count)
            for m in range(mp_count)
        ],
        np.int32,
    )
    device = lax.axis_index(("section", "mp"))
    places = lax.dynamic_slice(
        jnp.asarray(table), (device, 0), (1, mp_count + 2)
    ).reshape(-1)
    starts, counts = own_samples(tile_counts, section_table, places[mp_count + 1])
    meta = jnp.concatenate([places, starts, counts])

    up_pairs = [(ring[i], ring[(i + 1) % mp_count]) for i in range(mp_count)]
    down_pairs = [(target, source) for source, target in up_pairs]

    def up(value):
        return lax.ppermute(value, "mp", up_pairs)

    def down(value):
        return lax.ppermute(value, "mp", down_pairs)

    def across(pairs):
        return [
            (s * mp_count + a, ((s + 1) % section_count) * mp_count + b)
            for s in range(section_count)
            for a, b in pairs
        ]

    def up_across(value):
        return lax.ppermute(value, ("section", "mp"), across(up_pairs))

    def down_across(value):
        return lax.ppermute(value, ("section", "mp"), across(down_pairs))

    def to_next(value):
        return lax.ppermute(
            value, "section", [(s, (s + 1) % section_count) for s in range(section_count)]
        )

    def ring_sums(chains, hold=lambda left, value: value, turn=()):
        running = [part(sign * distance) for part, distance, sign, _, _ in chains]
        for hop in range(far):
            for index, (part, distance, sign, move, last) in enumerate(chains):
                left = distance - hop
                if left == 1:
                    running[index] = last(hold(left, running[index]))
                elif left > 1:
                    came = after(move(hold(left, running[index])), *turn)
                    running[index] = add(came, part(sign * (left - 1)))
                    turn = [running[index]]
        return running

    def both_ways(part, distance_up, distance_down, last_up=up, last_down=down):
        return [
            (part, distance_up, 1, up, last_up),
            (part, distance_down, -1, down, last_down),
        ]

    text_own = text_state[0]
    text_rows = text_own.shape[0]
    parts = 2 if text_rows % 32 == 0 else 1
    cut = text_rows // parts
    reach = [(far, far - 1), (far - 1, far)][:parts]
    text_next = to_next(text_own)
    gate_next = to_next(attn_gate)
    from_below, from_above = [text_own], [text_own]

    def text_round(*first):
        from_below.append(up(after(from_below[-1], *first)))
        from_above.append(down(after(from_above[-1], *first)))

    text_round()

    image_parts = project(places, tile_feats, w_proj, mp_count, 0, 1)
    image_parts += project(places, tile_feats, w_proj, mp_count, 1, mp_count - 1)
    image_chains = [
        chain
        for half, distances in enumerate(((far, far - 1), (far - 1, far)))
        for chain in both_ways(
            lambda offset, half=half: image_parts[index_of[offset]][half], *distances
        )
    ]

    weight_query, weight_out = w_query[0], w_out[0]
    queries = [query([text_own, from_below[1], from_above[1]], weight_query)]

    turns = [0, 3, 1, 2]
    came = ring_sums(
        [image_chains[turn] for turn in turns], turn=[gate_next, queries[0]]
    )
    came = [came[turns.index(index)] for index in range(4)]
    image_cols = total_of(
        [[image_parts[index_of[0]][half], *came[2 * half : 2 * half + 2]] for half in range(2)]
    )

    text_round(image_cols)
    pieces = []
    moving = image_cols
    for step in range(section_count // 2):
        pieces += [
            moving,
            lax.ppermute(moving, "section", [(s, s ^ 1) for s in range(section_count)]),
        ]
        if step + 1 < section_count // 2:
            moving = lax.ppermute(
                moving,
                "section",
                [(s, (s + 2) % section_count) for s in range(section_count)],
            )

    kv_part = key_values(meta, pieces, w_kv[0], mp_count, section_count, sharing)

    for distance in range(3, far - 1):
        text_round(*([kv_part[0]] if distance == 3 else []))
    below, above = (after(value[-1], kv_part[0]) for value in (from_below, from_above))
    low = slice(text_rows - cut, text_rows)
    onward = [up(below[:cut]), down(above[low])]
    far_chunks = [up(onward[0])]
    if parts == 2:
        far_chunks.append(down(onward[1]))

    def kv_hold(left, value):
        return after(value, *onward) if left == min(2, far - 1) else value

    came = ring_sums(
        both_ways(lambda offset: kv_part[index_of[offset]], far, far - 1),
        kv_hold,
        turn=[from_below[2], from_above[2]] if far > 2 else [],
    )
    kv_own = (
        kv_part[index_of[0]].astype(F32) + came[0].astype(F32) + came[1].astype(F32)
    ).astype(BF16)
    kv_own = after(kv_own, *far_chunks)
    kv_pieces = [kv_own]
    for step in range(1, sharing):
        pairs = [
            (m, m // sharing * sharing + (m % sharing + step) % sharing) for m in range(mp_count)
        ]
        kv_pieces.append(lax.ppermute(kv_own, "mp", pairs))

    behind = []
    if parts == 2:
        behind = [up(after(below, kv_own)[cut:]), down(after(above, kv_own)[:cut])]

    def attend_to(offsets, rows, sizes):
        indices = [index_of[offset] for offset in offsets]
        return attend(meta, rows, kv_pieces, weight_out, indices, sizes, text_rows, mp_count)

    last = far - 1
    near = [sign * distance for distance in range(1, last) for sign in (-1, 1)]
    out_parts = {offset: [None] * parts for offset in [last, -last]}
    first = [far] * parts + [-last, last]
    first_queries = query(far_chunks + onward, weight_query)
    first_part = attend_to(first, first_queries, [cut] * len(first))
    out_parts[far] = out_parts[-far] = first_part[:parts]
    out_parts[-last][0], out_parts[last][parts - 1] = first_part[parts:]
    ready = first_part[0]
    for distance in range(2, last):
        rows = [after(from_below[distance], ready), from_above[distance]]
        queries.append(query(rows, weight_query))
    rest_queries = jnp.concatenate(queries, axis=0)
    if parts == 2:
        behind_queries = after(query(behind, weight_query), rest_queries, ready)
        behind_part = attend_to([-last, last], behind_queries, [cut] * 2)
        out_parts[-last][1], out_parts[last][0] = behind_part
        ready = behind_part[0]
    sizes = [text_rows] + [cut] * (parts * len(near))
    own_part, *near_part = attend_to([0] + near, after(rest_queries, ready, text_next), sizes)
    for index, offset in enumerate(near):
        out_parts[offset] = near_part[parts * index :][:parts]
    own_next = to_next(own_part)

    branch_chains = [
        chain
        for part, distances in enumerate(reach)
        for chain in both_ways(
            lambda offset, part=part: out_parts[offset][part],
            *distances,
            up_across,
            down_across,
        )
    ]

    def branch_hold(left, value):
        if left == 1:
            return after(value, own_next)
        return after(value, *behind) if left == last else value

    turns = [0, 3, 1, 2] if parts == 2 else [0, 1]
    came = ring_sums([branch_chains[turn] for turn in turns], branch_hold)
    came = [came[turns.index(index)] for index in range(2 * parts)]
    results = []
    for part in range(parts):
        place = slice(part * cut, (part + 1) * cut)
        branch = own_next[place].astype(F32)
        for value in came[2 * part : 2 * part + 2]:
            branch = branch + value.astype(F32)
        results.append(
            (text_next[place].astype(F32) + jnp.tanh(gate_next[0]) * branch).astype(BF16)
        )
    return jnp.concatenate(results, axis=0)[None]


def solution(mesh):
    mesh_shape = dict(mesh.shape)

    def body(*arrays):
        return local(mesh_shape, *arrays)

    return jax.shard_map(
        body,
        mesh=mesh,
        in_specs=(
            P("section", "mp", None),
            P("section", "mp"),
            P("mp", None),
            P("section", None, "mp"),
            P("section", "mp", None),
            P("section", "mp", None),
            P("section"),
            P(),
            P(),
        ),
        out_specs=P("section", "mp", None),
        check_vma=False,
    )
```

```python
import math

import jax
import jax.numpy as jnp
import numpy as np
from jax import lax
from jax.experimental import pallas as pl
from jax.experimental.pallas import tpu as pltpu
from jax.sharding import PartitionSpec as P

HD = 128
HEADS = 32
KVH = 4
SAMP_SECTION = 4
TXT = 128
TT = 32
MAXT = 4
BLOCK = MAXT * TT
SLOTS = SAMP_SECTION * BLOCK
F32 = jnp.float32
BF16 = jnp.bfloat16
VMEM_LIMIT = 24 * 1024 * 1024
VMEM_MOST = 56 * 1024 * 1024
QUICK = pl.CostEstimate(flops=1, bytes_accessed=1, transcendentals=0)
VMEM_SMALL = 16 * 1024 * 1024


def ring_order(count):
    wide = 2 if count <= 8 else 4
    tall = count // wide
    if count < 4 or count % wide or tall % 2:
        return list(range(count))
    order = [row * wide for row in range(tall)]
    for turn, row in enumerate(reversed(range(tall))):
        columns = range(1, wide) if turn % 2 == 0 else range(wide - 1, 0, -1)
        order += [row * wide + column for column in columns]
    return order


def own_samples(tile_counts, section_table, section_id):
    samples_all = tile_counts.shape[0]
    sample_ids = jnp.arange(samples_all, dtype=jnp.int32)
    same_section = section_table[None, :] == section_table[:, None]
    before = sample_ids[None, :] < sample_ids[:, None]
    ranking = jnp.sum((same_section & before).astype(jnp.int32), axis=1)
    picked = (section_table[None, :] == section_id) & (
        ranking[None, :] == jnp.arange(SAMP_SECTION, dtype=jnp.int32)[:, None]
    )
    first_row = TT * jnp.sum(jnp.where(before, tile_counts[None, :], 0), axis=1)
    counts_own = jnp.sum(jnp.where(picked, tile_counts[None, :], 0), axis=1)
    starts_own = jnp.sum(jnp.where(picked, first_row[None, :], 0), axis=1)
    return starts_own, counts_own


def add(one, other):
    return (one.astype(F32) + other.astype(F32)).astype(BF16)


def params(limit=VMEM_LIMIT):
    return pltpu.CompilerParams(vmem_limit_bytes=limit)


def total_of(groups):
    parts, count = len(groups), len(groups[0])
    part_rows, columns = groups[0][0].shape
    rows = parts * part_rows

    def kernel(*refs):
        for part in range(parts):
            total = refs[part * count][...].astype(F32)
            for ref in refs[part * count + 1 : (part + 1) * count]:
                total += ref[...].astype(F32)
            refs[-1][part * part_rows : (part + 1) * part_rows, :] = total.astype(BF16)

    return pl.pallas_call(
        kernel,
        in_specs=[pl.BlockSpec(memory_space=pltpu.VMEM)] * (parts * count),
        out_specs=pl.BlockSpec(memory_space=pltpu.VMEM),
        out_shape=jax.ShapeDtypeStruct((rows, columns), BF16),
        compiler_params=params(VMEM_SMALL),
        cost_estimate=QUICK,
        name="total_of",
    )(*[value for group in groups for value in group])


def project(places, feats, weight, order_len, first, blocks):
    rows, depth = feats.shape
    half = rows // 2
    wide = weight.shape[1] // order_len

    def kernel(places_ref, feats_ref, weight_ref, *out_refs):
        product = jnp.dot(
            feats_ref[...], weight_ref[...], preferred_element_type=F32
        ).astype(BF16)
        for block in range(blocks):

            @pl.when(pl.program_id(0) == block)
            def _():
                out_refs[2 * block][...] = product[:half]
                out_refs[2 * block + 1][...] = product[half:]

    halves = pl.pallas_call(
        kernel,
        grid_spec=pltpu.PrefetchScalarGridSpec(
            num_scalar_prefetch=1,
            grid=(blocks,),
            in_specs=[
                pl.BlockSpec((rows, depth), lambda i, places: (0, 0)),
                pl.BlockSpec((depth, wide), lambda i, places: (0, places[first + i])),
            ],
            out_specs=[pl.BlockSpec((half, wide), lambda i, places: (0, 0))] * (2 * blocks),
        ),
        out_shape=[jax.ShapeDtypeStruct((half, wide), BF16)] * (2 * blocks),
        compiler_params=params(VMEM_MOST),
        cost_estimate=pl.CostEstimate(
            flops=2 * rows * depth * wide * blocks,
            bytes_accessed=2 * (depth + rows) * wide * blocks,
            transcendentals=0,
        ),
        name="project",
    )(places, feats, weight)
    return [halves[2 * block : 2 * block + 2] for block in range(blocks)]


def key_values(meta, pieces, weight, order_len, section_count, sharing):
    feat_rows = pieces[0].shape[0]
    depth, width = weight.shape
    kv_rows = SLOTS // sharing
    half_width = width // 2
    count = len(pieces)

    def kernel(meta_ref, *refs):
        piece_refs, weight_ref = refs[:count], refs[count]
        out_refs, kv_ref = refs[count + 1 : -1], refs[-1]
        section = meta_ref[order_len + 1]
        slot = lax.broadcasted_iota(jnp.int32, (BLOCK, feat_rows), 0)
        packed = lax.broadcasted_iota(jnp.int32, (BLOCK, feat_rows), 1)
        for sample in range(SAMP_SECTION):
            start = meta_ref[order_len + 2 + sample]
            live = TT * meta_ref[order_len + 2 + SAMP_SECTION + sample]
            image = jnp.zeros((BLOCK, depth), F32)
            for index in range(count):
                step, swapped = index // 2, index % 2
                origin = lax.rem(section + (section_count - 2 * step), section_count)
                if swapped:
                    origin = origin + 1 - 2 * lax.rem(origin, 2)
                chosen = (slot < live) & (packed == slot + (start - origin * feat_rows))
                image += jnp.dot(
                    chosen.astype(F32).astype(BF16),
                    piece_refs[index][...],
                    preferred_element_type=F32,
                )
            kv_ref[sample * BLOCK : (sample + 1) * BLOCK, :] = jnp.dot(
                image.astype(BF16), weight_ref[...], preferred_element_type=F32
            ).astype(BF16)
        for index in range(order_len):
            target = meta_ref[index]
            row = pl.multiple_of(lax.rem(target, sharing) * kv_rows, kv_rows)
            column = pl.multiple_of(target // sharing * HD, HD)
            out_refs[index][:, :HD] = kv_ref[pl.ds(row, kv_rows), pl.ds(column, HD)]
            out_refs[index][:, HD:] = kv_ref[
                pl.ds(row, kv_rows), pl.ds(pl.multiple_of(column + half_width, HD), HD)
            ]

    whole = pl.BlockSpec(memory_space=pltpu.VMEM)
    return pl.pallas_call(
        kernel,
        in_specs=[pl.BlockSpec(memory_space=pltpu.SMEM)] + [whole] * (count + 1),
        out_specs=[whole] * order_len,
        out_shape=[jax.ShapeDtypeStruct((kv_rows, 2 * HD), BF16)] * order_len,
        scratch_shapes=[pltpu.VMEM((SLOTS, width), BF16)],
        compiler_params=params(),
        cost_estimate=QUICK,
        name="key_values",
    )(meta, *pieces, weight)


def query(chunks, weight, limit=VMEM_LIMIT):
    rows = sum(chunk.shape[0] for chunk in chunks)
    depth, width = weight.shape
    wide = min(2 * HD, width)
    count = len(chunks)

    def kernel(*refs):
        chunk_refs, weight_ref, out_ref = refs[:count], refs[count], refs[count + 1]
        rows_ref, scale_ref = refs[count + 2 :]

        @pl.when(pl.program_id(0) == 0)
        def _():
            first = 0
            for chunk_ref in chunk_refs:
                place = slice(first, first + chunk_ref.shape[0])
                chunk = chunk_ref[...]
                wider = chunk.astype(F32)
                rows_ref[place, :] = chunk
                scale_ref[place, :] = lax.rsqrt(
                    jnp.mean(wider * wider, axis=-1, keepdims=True) + 1e-05
                )
                first += chunk_ref.shape[0]

        projected = jnp.dot(rows_ref[...], weight_ref[...], preferred_element_type=F32)
        projected = projected * scale_ref[...]
        for head in range(wide // HD):
            one = projected[:, head * HD : (head + 1) * HD]
            one = one * lax.rsqrt(jnp.mean(one * one, axis=-1, keepdims=True) + 1e-06)
            out_ref[:, head * HD : (head + 1) * HD] = one.astype(BF16)

    return pl.pallas_call(
        kernel,
        grid=(width // wide,),
        in_specs=[pl.BlockSpec(chunk.shape, lambda i: (0, 0)) for chunk in chunks]
        + [pl.BlockSpec((depth, wide), lambda i: (0, i))],
        out_specs=pl.BlockSpec((rows, wide), lambda i: (0, i)),
        out_shape=jax.ShapeDtypeStruct((rows, width), BF16),
        scratch_shapes=[pltpu.VMEM((rows, depth), BF16), pltpu.VMEM((rows, 1), F32)],
        compiler_params=params(limit),
        cost_estimate=pl.CostEstimate(
            flops=2 * rows * depth * width,
            bytes_accessed=2 * depth * (width + rows),
            transcendentals=0,
        ),
        name="query",
    )(*chunks, weight)


def attend(meta, queries, kv_pieces, weight, indices, sizes, shard_rows, order_len):
    text_rows = queries.shape[0] // len(indices)
    rows, width = queries.shape
    heads = width // HD
    sharing = len(kv_pieces)
    kv_rows = SLOTS // sharing
    columns = weight.shape[1]
    wide = min(1024, columns)
    tall = min(64, width)

    def kernel(meta_ref, query_ref, *refs):
        kv_refs, weight_ref = refs[:sharing], refs[sharing]
        out_refs = refs[sharing + 1 : -5]
        key_ref, value_ref, attended_ref, held_ref, sems = refs[-5:]
        step = pl.program_id(0)

        def fetch(index):
            place = pl.ds(index * tall, tall)
            return pltpu.make_async_copy(
                weight_ref.at[place, :], held_ref.at[place, :], sems.at[index]
            )

        @pl.when(step == 0)
        def _():
            for index in range(width // tall):
                fetch(index).start()
            mine = lax.rem(meta_ref[order_len], sharing)
            for piece in range(sharing):
                row = pl.multiple_of(
                    lax.rem(mine + sharing - piece, sharing) * kv_rows, kv_rows
                )
                keys = kv_refs[piece][:, :HD].astype(F32)
                keys = keys * lax.rsqrt(jnp.mean(keys * keys, axis=-1, keepdims=True) + 1e-06)
                key_ref[pl.ds(row, kv_rows), :] = keys.astype(BF16)
                value_ref[pl.ds(row, kv_rows), :] = kv_refs[piece][:, HD:]
            for place, index in enumerate(indices):
                sample = meta_ref[index] * shard_rows // TXT
                slots = pl.ds(pl.multiple_of(sample * BLOCK, BLOCK), BLOCK)
                live = TT * meta_ref[order_len + 2 + SAMP_SECTION + sample]
                first = place * text_rows
                own = query_ref[first : first + text_rows, :]
                stacked = jnp.concatenate(
                    [own[:, h * HD : (h + 1) * HD] for h in range(heads)], axis=0
                )
                scores = lax.dot_general(
                    stacked,
                    key_ref[slots, :],
                    (((1,), (1,)), ((), ())),
                    preferred_element_type=F32,
                ) * (1.0 / math.sqrt(HD))
                slot = lax.broadcasted_iota(jnp.int32, scores.shape, 1)
                raised = jnp.where(slot < live, jnp.exp(scores), 0.0)
                weights = (raised / jnp.sum(raised, axis=-1, keepdims=True)).astype(BF16)
                result = jnp.dot(
                    weights, value_ref[slots, :], preferred_element_type=F32
                ).astype(BF16)
                for h in range(heads):
                    attended_ref[first : first + text_rows, h * HD : (h + 1) * HD] = result[
                        h * text_rows : (h + 1) * text_rows
                    ]
            for index in range(width // tall):
                fetch(index).wait()

        product = jnp.dot(
            attended_ref[...],
            held_ref[:, pl.ds(pl.multiple_of(step * wide, wide), wide)],
            preferred_element_type=F32,
        ).astype(BF16)
        first = 0
        for out_ref, size in zip(out_refs, sizes):
            out_ref[...] = product[first : first + size]
            first += size

    return pl.pallas_call(
        kernel,
        grid_spec=pltpu.PrefetchScalarGridSpec(
            num_scalar_prefetch=1,
            grid=(columns // wide,),
            in_specs=[pl.BlockSpec((rows, width), lambda i, meta: (0, 0))]
            + [pl.BlockSpec(piece.shape, lambda i, meta: (0, 0)) for piece in kv_pieces]
            + [pl.BlockSpec(memory_space=pl.ANY)],
            out_specs=[pl.BlockSpec((size, wide), lambda i, meta: (0, i)) for size in sizes],
            scratch_shapes=[
                pltpu.VMEM((SLOTS, HD), BF16),
                pltpu.VMEM((SLOTS, HD), BF16),
                pltpu.VMEM((rows, width), BF16),
                pltpu.VMEM((width, columns), BF16),
                pltpu.SemaphoreType.DMA((width // tall,)),
            ],
        ),
        out_shape=[jax.ShapeDtypeStruct((size, columns), BF16) for size in sizes],
        compiler_params=params(),
        cost_estimate=pl.CostEstimate(
            flops=8 * rows * width * columns,
            bytes_accessed=8 * width * columns,
            transcendentals=rows * heads * BLOCK,
        ),
        name="attend",
    )(meta, queries, *kv_pieces, weight)


def after(value, *others):
    if not others:
        return value
    return lax.optimization_barrier((value, *others))[0]


def local(
    mesh_shape,
    text_state,
    tile_feats,
    w_proj,
    w_query,
    w_kv,
    w_out,
    attn_gate,
    tile_counts,
    section_table,
):
    mp_count, section_count = mesh_shape["mp"], mesh_shape["section"]
    ring = ring_order(mp_count)
    far = mp_count // 2
    sharing = mp_count // KVH
    order = [far]
    for distance in range(far - 1, 0, -1):
        order += [-distance, distance]
    order.append(0)
    index_of = {offset: index for index, offset in enumerate(order)}
    index_of[-far] = 0
    table = np.array(
        [
            [ring[(ring.index(m) + offset) % mp_count] for offset in order] + [m, s]
            for s in range(section_count)
            for m in range(mp_count)
        ],
        np.int32,
    )
    device = lax.axis_index(("section", "mp"))
    places = lax.dynamic_slice(
        jnp.asarray(table), (device, 0), (1, mp_count + 2)
    ).reshape(-1)
    starts, counts = own_samples(tile_counts, section_table, places[mp_count + 1])
    meta = jnp.concatenate([places, starts, counts])

    up_pairs = [(ring[i], ring[(i + 1) % mp_count]) for i in range(mp_count)]
    down_pairs = [(target, source) for source, target in up_pairs]

    def up(value):
        return lax.ppermute(value, "mp", up_pairs)

    def down(value):
        return lax.ppermute(value, "mp", down_pairs)

    def across(pairs):
        return [
            (s * mp_count + a, ((s + 1) % section_count) * mp_count + b)
            for s in range(section_count)
            for a, b in pairs
        ]

    def up_across(value):
        return lax.ppermute(value, ("section", "mp"), across(up_pairs))

    def down_across(value):
        return lax.ppermute(value, ("section", "mp"), across(down_pairs))

    def to_next(value):
        return lax.ppermute(
            value, "section", [(s, (s + 1) % section_count) for s in range(section_count)]
        )

    def ring_sums(chains, hold=lambda left, value: value, turn=()):
        running = [part(sign * distance) for part, distance, sign, _, _ in chains]
        for hop in range(far):
            for index, (part, distance, sign, move, last) in enumerate(chains):
                left = distance - hop
                if left == 1:
                    running[index] = last(hold(left, running[index]))
                elif left > 1:
                    came = after(move(hold(left, running[index])), *turn)
                    running[index] = add(came, part(sign * (left - 1)))
                    turn = [running[index]]
        return running

    def both_ways(part, distance_up, distance_down, last_up=up, last_down=down):
        return [
            (part, distance_up, 1, up, last_up),
            (part, distance_down, -1, down, last_down),
        ]

    text_own = text_state[0]
    text_rows = text_own.shape[0]
    parts = 2 if text_rows % 32 == 0 else 1
    cut = text_rows // parts
    reach = [(far, far - 1), (far - 1, far)][:parts]
    text_next = to_next(text_own)
    gate_next = to_next(attn_gate)
    from_below, from_above = [text_own], [text_own]

    def text_round(*first):
        from_below.append(up(after(from_below[-1], *first)))
        from_above.append(down(after(from_above[-1], *first)))

    text_round()

    image_parts = project(places, tile_feats, w_proj, mp_count, 0, 1)
    image_parts += project(places, tile_feats, w_proj, mp_count, 1, mp_count - 1)
    image_chains = [
        chain
        for half, distances in enumerate(((far, far - 1), (far - 1, far)))
        for chain in both_ways(
            lambda offset, half=half: image_parts[index_of[offset]][half], *distances
        )
    ]

    weight_query, weight_out = w_query[0], w_out[0]
    queries = [query([text_own, from_below[1], from_above[1]], weight_query, VMEM_MOST)]

    turns = [0, 3, 1, 2]
    came = ring_sums(
        [image_chains[turn] for turn in turns], turn=[gate_next, queries[0]]
    )
    came = [came[turns.index(index)] for index in range(4)]
    image_cols = total_of(
        [[image_parts[index_of[0]][half], *came[2 * half : 2 * half + 2]] for half in range(2)]
    )

    text_round(image_cols)
    pieces = []
    moving = image_cols
    for step in range(section_count // 2):
        pieces += [
            moving,
            lax.ppermute(moving, "section", [(s, s ^ 1) for s in range(section_count)]),
        ]
        if step + 1 < section_count // 2:
            moving = lax.ppermute(
                moving,
                "section",
                [(s, (s + 2) % section_count) for s in range(section_count)],
            )

    kv_part = key_values(meta, pieces, w_kv[0], mp_count, section_count, sharing)

    for distance in range(3, far - 1):
        text_round(*([kv_part[0]] if distance == 3 else []))
    below, above = (after(value[-1], kv_part[0]) for value in (from_below, from_above))
    low = slice(text_rows - cut, text_rows)
    onward = [up(below[:cut]), down(above[low])]
    far_chunks = [up(onward[0])]
    if parts == 2:
        far_chunks.append(down(onward[1]))

    def kv_hold(left, value):
        return after(value, *onward) if left == min(2, far - 1) else value

    came = ring_sums(
        both_ways(lambda offset: kv_part[index_of[offset]], far, far - 1),
        kv_hold,
        turn=[from_below[2], from_above[2]] if far > 2 else [],
    )
    kv_own = (
        kv_part[index_of[0]].astype(F32) + came[0].astype(F32) + came[1].astype(F32)
    ).astype(BF16)
    kv_own = after(kv_own, *far_chunks)
    kv_pieces = [kv_own]
    for step in range(1, sharing):
        pairs = [
            (m, m // sharing * sharing + (m % sharing + step) % sharing) for m in range(mp_count)
        ]
        kv_pieces.append(lax.ppermute(kv_own, "mp", pairs))

    behind = []
    if parts == 2:
        behind = [up(after(below, kv_own)[cut:]), down(after(above, kv_own)[:cut])]

    def attend_to(offsets, rows, sizes):
        indices = [index_of[offset] for offset in offsets]
        return attend(meta, rows, kv_pieces, weight_out, indices, sizes, text_rows, mp_count)

    last = far - 1
    near = [sign * distance for distance in range(1, last) for sign in (-1, 1)]
    out_parts = {offset: [None] * parts for offset in [last, -last]}
    first = [far] * parts + [-last, last]
    first_queries = query(far_chunks + onward, weight_query)
    first_part = attend_to(first, first_queries, [cut] * len(first))
    out_parts[far] = out_parts[-far] = first_part[:parts]
    out_parts[-last][0], out_parts[last][parts - 1] = first_part[parts:]
    ready = first_part[0]
    for distance in range(2, last):
        rows = [after(from_below[distance], ready), from_above[distance]]
        queries.append(query(rows, weight_query))
    rest_queries = jnp.concatenate(queries, axis=0)
    if parts == 2:
        behind_queries = after(query(behind, weight_query), rest_queries, ready)
        behind_part = attend_to([-last, last], behind_queries, [cut] * 2)
        out_parts[-last][1], out_parts[last][0] = behind_part
        ready = behind_part[0]
    sizes = [text_rows] + [cut] * (parts * len(near))
    own_part, *near_part = attend_to([0] + near, after(rest_queries, ready, text_next), sizes)
    for index, offset in enumerate(near):
        out_parts[offset] = near_part[parts * index :][:parts]
    own_next = to_next(own_part)

    branch_chains = [
        chain
        for part, distances in enumerate(reach)
        for chain in both_ways(
            lambda offset, part=part: out_parts[offset][part],
            *distances,
            up_across,
            down_across,
        )
    ]

    def branch_hold(left, value):
        if left == 1:
            return after(value, own_next)
        return after(value, *behind) if left == last else value

    turns = [0, 3, 1, 2] if parts == 2 else [0, 1]
    came = ring_sums([branch_chains[turn] for turn in turns], branch_hold)
    came = [came[turns.index(index)] for index in range(2 * parts)]
    results = []
    for part in range(parts):
        place = slice(part * cut, (part + 1) * cut)
        branch = own_next[place].astype(F32)
        for value in came[2 * part : 2 * part + 2]:
            branch = branch + value.astype(F32)
        results.append(
            (text_next[place].astype(F32) + jnp.tanh(gate_next[0]) * branch).astype(BF16)
        )
    return jnp.concatenate(results, axis=0)[None]


def solution(mesh):
    mesh_shape = dict(mesh.shape)

    def body(*arrays):
        return local(mesh_shape, *arrays)

    return jax.shard_map(
        body,
        mesh=mesh,
        in_specs=(
            P("section", "mp", None),
            P("section", "mp"),
            P("mp", None),
            P("section", None, "mp"),
            P("section", "mp", None),
            P("section", "mp", None),
            P("section"),
            P(),
            P(),
        ),
        out_specs=P("section", "mp", None),
        check_vma=False,
    )
```

```python
import math

import jax
import jax.numpy as jnp
import numpy as np
from jax import lax
from jax.experimental import pallas as pl
from jax.experimental.pallas import tpu as pltpu
from jax.sharding import PartitionSpec as P

HD = 128
HEADS = 32
KVH = 4
SAMP_SECTION = 4
TXT = 128
TT = 32
MAXT = 4
BLOCK = MAXT * TT
SLOTS = SAMP_SECTION * BLOCK
F32 = jnp.float32
BF16 = jnp.bfloat16
VMEM_LIMIT = 24 * 1024 * 1024
VMEM_MOST = 56 * 1024 * 1024
QUICK = pl.CostEstimate(flops=1, bytes_accessed=1, transcendentals=0)
VMEM_SMALL = 16 * 1024 * 1024


def ring_order(count):
    wide = 2 if count <= 8 else 4
    tall = count // wide
    if count < 4 or count % wide or tall % 2:
        return list(range(count))
    order = [row * wide for row in range(tall)]
    for turn, row in enumerate(reversed(range(tall))):
        columns = range(1, wide) if turn % 2 == 0 else range(wide - 1, 0, -1)
        order += [row * wide + column for column in columns]
    return order


def own_samples(tile_counts, section_table, section_id):
    samples_all = tile_counts.shape[0]
    sample_ids = jnp.arange(samples_all, dtype=jnp.int32)
    same_section = section_table[None, :] == section_table[:, None]
    before = sample_ids[None, :] < sample_ids[:, None]
    ranking = jnp.sum((same_section & before).astype(jnp.int32), axis=1)
    picked = (section_table[None, :] == section_id) & (
        ranking[None, :] == jnp.arange(SAMP_SECTION, dtype=jnp.int32)[:, None]
    )
    first_row = TT * jnp.sum(jnp.where(before, tile_counts[None, :], 0), axis=1)
    counts_own = jnp.sum(jnp.where(picked, tile_counts[None, :], 0), axis=1)
    starts_own = jnp.sum(jnp.where(picked, first_row[None, :], 0), axis=1)
    return starts_own, counts_own


def add(one, other):
    return (one.astype(F32) + other.astype(F32)).astype(BF16)


def params(limit=VMEM_LIMIT):
    return pltpu.CompilerParams(vmem_limit_bytes=limit)


def total_of(groups):
    parts, count = len(groups), len(groups[0])
    part_rows, columns = groups[0][0].shape
    rows = parts * part_rows

    def kernel(*refs):
        for part in range(parts):
            total = refs[part * count][...].astype(F32)
            for ref in refs[part * count + 1 : (part + 1) * count]:
                total += ref[...].astype(F32)
            refs[-1][part * part_rows : (part + 1) * part_rows, :] = total.astype(BF16)

    return pl.pallas_call(
        kernel,
        in_specs=[pl.BlockSpec(memory_space=pltpu.VMEM)] * (parts * count),
        out_specs=pl.BlockSpec(memory_space=pltpu.VMEM),
        out_shape=jax.ShapeDtypeStruct((rows, columns), BF16),
        compiler_params=params(VMEM_SMALL),
        cost_estimate=QUICK,
        name="total_of",
    )(*[value for group in groups for value in group])


def project(places, feats, weight, order_len, first, blocks):
    rows, depth = feats.shape
    half = rows // 2
    wide = weight.shape[1] // order_len

    def kernel(places_ref, feats_ref, weight_ref, *out_refs):
        product = jnp.dot(
            feats_ref[...], weight_ref[...], preferred_element_type=F32
        ).astype(BF16)
        for block in range(blocks):

            @pl.when(pl.program_id(0) == block)
            def _():
                out_refs[2 * block][...] = product[:half]
                out_refs[2 * block + 1][...] = product[half:]

    halves = pl.pallas_call(
        kernel,
        grid_spec=pltpu.PrefetchScalarGridSpec(
            num_scalar_prefetch=1,
            grid=(blocks,),
            in_specs=[
                pl.BlockSpec((rows, depth), lambda i, places: (0, 0)),
                pl.BlockSpec((depth, wide), lambda i, places: (0, places[first + i])),
            ],
            out_specs=[pl.BlockSpec((half, wide), lambda i, places: (0, 0))] * (2 * blocks),
        ),
        out_shape=[jax.ShapeDtypeStruct((half, wide), BF16)] * (2 * blocks),
        compiler_params=params(VMEM_MOST),
        cost_estimate=pl.CostEstimate(
            flops=2 * rows * depth * wide * blocks,
            bytes_accessed=2 * (depth + rows) * wide * blocks,
            transcendentals=0,
        ),
        name="project",
    )(places, feats, weight)
    return [halves[2 * block : 2 * block + 2] for block in range(blocks)]


def key_values(meta, pieces, weight, order_len, section_count, sharing):
    feat_rows = pieces[0].shape[0]
    depth, width = weight.shape
    kv_rows = SLOTS // sharing
    half_width = width // 2
    count = len(pieces)

    def kernel(meta_ref, *refs):
        piece_refs, weight_ref = refs[:count], refs[count]
        out_refs, kv_ref = refs[count + 1 : -1], refs[-1]
        section = meta_ref[order_len + 1]
        slot = lax.broadcasted_iota(jnp.int32, (BLOCK, feat_rows), 0)
        packed = lax.broadcasted_iota(jnp.int32, (BLOCK, feat_rows), 1)
        for sample in range(SAMP_SECTION):
            start = meta_ref[order_len + 2 + sample]
            live = TT * meta_ref[order_len + 2 + SAMP_SECTION + sample]
            image = jnp.zeros((BLOCK, depth), F32)
            for index in range(count):
                step, swapped = index // 2, index % 2
                origin = lax.rem(section + (section_count - 2 * step), section_count)
                if swapped:
                    origin = origin + 1 - 2 * lax.rem(origin, 2)
                chosen = (slot < live) & (packed == slot + (start - origin * feat_rows))
                image += jnp.dot(
                    chosen.astype(F32).astype(BF16),
                    piece_refs[index][...],
                    preferred_element_type=F32,
                )
            kv_ref[sample * BLOCK : (sample + 1) * BLOCK, :] = jnp.dot(
                image.astype(BF16), weight_ref[...], preferred_element_type=F32
            ).astype(BF16)
        for index in range(order_len):
            target = meta_ref[index]
            row = pl.multiple_of(lax.rem(target, sharing) * kv_rows, kv_rows)
            column = pl.multiple_of(target // sharing * HD, HD)
            out_refs[index][:, :HD] = kv_ref[pl.ds(row, kv_rows), pl.ds(column, HD)]
            out_refs[index][:, HD:] = kv_ref[
                pl.ds(row, kv_rows), pl.ds(pl.multiple_of(column + half_width, HD), HD)
            ]

    whole = pl.BlockSpec(memory_space=pltpu.VMEM)
    return pl.pallas_call(
        kernel,
        in_specs=[pl.BlockSpec(memory_space=pltpu.SMEM)] + [whole] * (count + 1),
        out_specs=[whole] * order_len,
        out_shape=[jax.ShapeDtypeStruct((kv_rows, 2 * HD), BF16)] * order_len,
        scratch_shapes=[pltpu.VMEM((SLOTS, width), BF16)],
        compiler_params=params(),
        cost_estimate=QUICK,
        name="key_values",
    )(meta, *pieces, weight)


def row_scale(rows):
    wider = rows.astype(F32)
    return lax.rsqrt(jnp.mean(wider * wider, axis=-1, keepdims=True) + 1e-05)


def row_scales(chunks):
    rows = sum(chunk.shape[0] for chunk in chunks)
    depth = chunks[0].shape[1]

    def kernel(*refs):
        first = 0
        for chunk_ref in refs[:-1]:
            size = chunk_ref.shape[0]
            refs[-1][first : first + size, :] = jnp.broadcast_to(
                row_scale(chunk_ref[...]), (size, HD)
            )
            first += size

    return pl.pallas_call(
        kernel,
        in_specs=[pl.BlockSpec(memory_space=pltpu.VMEM)] * len(chunks),
        out_specs=pl.BlockSpec(memory_space=pltpu.VMEM),
        out_shape=jax.ShapeDtypeStruct((rows, HD), F32),
        compiler_params=params(VMEM_SMALL),
        cost_estimate=pl.CostEstimate(
            flops=4 * rows * depth, bytes_accessed=8 * rows * depth, transcendentals=0
        ),
        name="row_scales",
    )(*chunks)


def query(chunks, weight, scales=None):
    rows = sum(chunk.shape[0] for chunk in chunks)
    depth, width = weight.shape
    wide = min(2 * HD, width)
    count = len(chunks)
    given = [] if scales is None else [scales]

    def kernel(*refs):
        chunk_refs, weight_ref, out_ref = refs[:count], refs[count], refs[-3]
        rows_ref, scale_ref = refs[-2:]

        @pl.when(pl.program_id(0) == 0)
        def _():
            first = 0
            for chunk_ref in chunk_refs:
                place = slice(first, first + chunk_ref.shape[0])
                chunk = chunk_ref[...]
                rows_ref[place, :] = chunk
                if scales is None:
                    scale_ref[place, :] = row_scale(chunk)
                first += chunk_ref.shape[0]
            if scales is not None:
                scale_ref[...] = refs[count + 1][:, :1]

        projected = jnp.dot(rows_ref[...], weight_ref[...], preferred_element_type=F32)
        projected = projected * scale_ref[...]
        for head in range(wide // HD):
            one = projected[:, head * HD : (head + 1) * HD]
            one = one * lax.rsqrt(jnp.mean(one * one, axis=-1, keepdims=True) + 1e-06)
            out_ref[:, head * HD : (head + 1) * HD] = one.astype(BF16)

    return pl.pallas_call(
        kernel,
        grid=(width // wide,),
        in_specs=[pl.BlockSpec(chunk.shape, lambda i: (0, 0)) for chunk in chunks]
        + [pl.BlockSpec((depth, wide), lambda i: (0, i))]
        + [pl.BlockSpec((rows, HD), lambda i: (0, 0)) for _ in given],
        out_specs=pl.BlockSpec((rows, wide), lambda i: (0, i)),
        out_shape=jax.ShapeDtypeStruct((rows, width), BF16),
        scratch_shapes=[pltpu.VMEM((rows, depth), BF16), pltpu.VMEM((rows, 1), F32)],
        compiler_params=params(),
        cost_estimate=pl.CostEstimate(
            flops=2 * rows * depth * width,
            bytes_accessed=2 * depth * (width + rows),
            transcendentals=0,
        ),
        name="query",
    )(*chunks, weight, *given)


def attend(meta, queries, kv_pieces, weight, indices, sizes, shard_rows, order_len):
    text_rows = queries.shape[0] // len(indices)
    rows, width = queries.shape
    heads = width // HD
    sharing = len(kv_pieces)
    kv_rows = SLOTS // sharing
    columns = weight.shape[1]
    wide = min(1024, columns)
    tall = min(64, width)

    def kernel(meta_ref, query_ref, *refs):
        kv_refs, weight_ref = refs[:sharing], refs[sharing]
        out_refs = refs[sharing + 1 : -5]
        key_ref, value_ref, attended_ref, held_ref, sems = refs[-5:]
        step = pl.program_id(0)

        def fetch(index):
            place = pl.ds(index * tall, tall)
            return pltpu.make_async_copy(
                weight_ref.at[place, :], held_ref.at[place, :], sems.at[index]
            )

        @pl.when(step == 0)
        def _():
            for index in range(width // tall):
                fetch(index).start()
            mine = lax.rem(meta_ref[order_len], sharing)
            for piece in range(sharing):
                row = pl.multiple_of(
                    lax.rem(mine + sharing - piece, sharing) * kv_rows, kv_rows
                )
                keys = kv_refs[piece][:, :HD].astype(F32)
                keys = keys * lax.rsqrt(jnp.mean(keys * keys, axis=-1, keepdims=True) + 1e-06)
                key_ref[pl.ds(row, kv_rows), :] = keys.astype(BF16)
                value_ref[pl.ds(row, kv_rows), :] = kv_refs[piece][:, HD:]
            for place, index in enumerate(indices):
                sample = meta_ref[index] * shard_rows // TXT
                slots = pl.ds(pl.multiple_of(sample * BLOCK, BLOCK), BLOCK)
                live = TT * meta_ref[order_len + 2 + SAMP_SECTION + sample]
                first = place * text_rows
                own = query_ref[first : first + text_rows, :]
                stacked = jnp.concatenate(
                    [own[:, h * HD : (h + 1) * HD] for h in range(heads)], axis=0
                )
                scores = lax.dot_general(
                    stacked,
                    key_ref[slots, :],
                    (((1,), (1,)), ((), ())),
                    preferred_element_type=F32,
                ) * (1.0 / math.sqrt(HD))
                slot = lax.broadcasted_iota(jnp.int32, scores.shape, 1)
                raised = jnp.where(slot < live, jnp.exp(scores), 0.0)
                weights = (raised / jnp.sum(raised, axis=-1, keepdims=True)).astype(BF16)
                result = jnp.dot(
                    weights, value_ref[slots, :], preferred_element_type=F32
                ).astype(BF16)
                for h in range(heads):
                    attended_ref[first : first + text_rows, h * HD : (h + 1) * HD] = result[
                        h * text_rows : (h + 1) * text_rows
                    ]
            for index in range(width // tall):
                fetch(index).wait()

        product = jnp.dot(
            attended_ref[...],
            held_ref[:, pl.ds(pl.multiple_of(step * wide, wide), wide)],
            preferred_element_type=F32,
        ).astype(BF16)
        first = 0
        for out_ref, size in zip(out_refs, sizes):
            out_ref[...] = product[first : first + size]
            first += size

    return pl.pallas_call(
        kernel,
        grid_spec=pltpu.PrefetchScalarGridSpec(
            num_scalar_prefetch=1,
            grid=(columns // wide,),
            in_specs=[pl.BlockSpec((rows, width), lambda i, meta: (0, 0))]
            + [pl.BlockSpec(piece.shape, lambda i, meta: (0, 0)) for piece in kv_pieces]
            + [pl.BlockSpec(memory_space=pl.ANY)],
            out_specs=[pl.BlockSpec((size, wide), lambda i, meta: (0, i)) for size in sizes],
            scratch_shapes=[
                pltpu.VMEM((SLOTS, HD), BF16),
                pltpu.VMEM((SLOTS, HD), BF16),
                pltpu.VMEM((rows, width), BF16),
                pltpu.VMEM((width, columns), BF16),
                pltpu.SemaphoreType.DMA((width // tall,)),
            ],
        ),
        out_shape=[jax.ShapeDtypeStruct((size, columns), BF16) for size in sizes],
        compiler_params=params(),
        cost_estimate=pl.CostEstimate(
            flops=8 * rows * width * columns,
            bytes_accessed=8 * width * columns,
            transcendentals=rows * heads * BLOCK,
        ),
        name="attend",
    )(meta, queries, *kv_pieces, weight)


def after(value, *others):
    if not others:
        return value
    return lax.optimization_barrier((value, *others))[0]


def local(
    mesh_shape,
    text_state,
    tile_feats,
    w_proj,
    w_query,
    w_kv,
    w_out,
    attn_gate,
    tile_counts,
    section_table,
):
    mp_count, section_count = mesh_shape["mp"], mesh_shape["section"]
    ring = ring_order(mp_count)
    far = mp_count // 2
    sharing = mp_count // KVH
    order = [far]
    for distance in range(far - 1, 0, -1):
        order += [-distance, distance]
    order.append(0)
    index_of = {offset: index for index, offset in enumerate(order)}
    index_of[-far] = 0
    table = np.array(
        [
            [ring[(ring.index(m) + offset) % mp_count] for offset in order] + [m, s]
            for s in range(section_count)
            for m in range(mp_count)
        ],
        np.int32,
    )
    device = lax.axis_index(("section", "mp"))
    places = lax.dynamic_slice(
        jnp.asarray(table), (device, 0), (1, mp_count + 2)
    ).reshape(-1)
    starts, counts = own_samples(tile_counts, section_table, places[mp_count + 1])
    meta = jnp.concatenate([places, starts, counts])

    up_pairs = [(ring[i], ring[(i + 1) % mp_count]) for i in range(mp_count)]
    down_pairs = [(target, source) for source, target in up_pairs]

    def up(value):
        return lax.ppermute(value, "mp", up_pairs)

    def down(value):
        return lax.ppermute(value, "mp", down_pairs)

    def across(pairs):
        return [
            (s * mp_count + a, ((s + 1) % section_count) * mp_count + b)
            for s in range(section_count)
            for a, b in pairs
        ]

    def up_across(value):
        return lax.ppermute(value, ("section", "mp"), across(up_pairs))

    def down_across(value):
        return lax.ppermute(value, ("section", "mp"), across(down_pairs))

    def to_next(value):
        return lax.ppermute(
            value, "section", [(s, (s + 1) % section_count) for s in range(section_count)]
        )

    def ring_sums(chains, hold=lambda left, value: value, turn=()):
        running = [part(sign * distance) for part, distance, sign, _, _ in chains]
        for hop in range(far):
            for index, (part, distance, sign, move, last) in enumerate(chains):
                left = distance - hop
                if left == 1:
                    running[index] = last(hold(left, running[index]))
                elif left > 1:
                    came = after(move(hold(left, running[index])), *turn)
                    running[index] = add(came, part(sign * (left - 1)))
                    turn = [running[index]]
        return running

    def both_ways(part, distance_up, distance_down, last_up=up, last_down=down):
        return [
            (part, distance_up, 1, up, last_up),
            (part, distance_down, -1, down, last_down),
        ]

    text_own = text_state[0]
    text_rows = text_own.shape[0]
    parts = 2 if text_rows % 32 == 0 else 1
    cut = text_rows // parts
    reach = [(far, far - 1), (far - 1, far)][:parts]
    text_next = to_next(text_own)
    gate_next = to_next(attn_gate)
    from_below, from_above = [text_own], [text_own]

    def text_round(*first):
        from_below.append(up(after(from_below[-1], *first)))
        from_above.append(down(after(from_above[-1], *first)))

    text_round()

    image_parts = project(places, tile_feats, w_proj, mp_count, 0, 1)
    image_parts += project(places, tile_feats, w_proj, mp_count, 1, mp_count - 1)
    image_chains = [
        chain
        for half, distances in enumerate(((far, far - 1), (far - 1, far)))
        for chain in both_ways(
            lambda offset, half=half: image_parts[index_of[offset]][half], *distances
        )
    ]

    text_scales = row_scales([text_own, from_below[1], from_above[1]])

    turns = [0, 3, 1, 2]
    came = ring_sums(
        [image_chains[turn] for turn in turns], turn=[gate_next, text_scales]
    )
    came = [came[turns.index(index)] for index in range(4)]
    image_cols = total_of(
        [[image_parts[index_of[0]][half], *came[2 * half : 2 * half + 2]] for half in range(2)]
    )

    text_round(image_cols)
    pieces = []
    moving = image_cols
    for step in range(section_count // 2):
        pieces += [
            moving,
            lax.ppermute(moving, "section", [(s, s ^ 1) for s in range(section_count)]),
        ]
        if step + 1 < section_count // 2:
            moving = lax.ppermute(
                moving,
                "section",
                [(s, (s + 2) % section_count) for s in range(section_count)],
            )

    kv_part = key_values(meta, pieces, w_kv[0], mp_count, section_count, sharing)

    for distance in range(3, far - 1):
        text_round(*([kv_part[0]] if distance == 3 else []))
    below, above = (after(value[-1], kv_part[0]) for value in (from_below, from_above))
    low = slice(text_rows - cut, text_rows)
    onward = [up(below[:cut]), down(above[low])]
    far_chunks = [up(onward[0])]
    if parts == 2:
        far_chunks.append(down(onward[1]))

    def kv_hold(left, value):
        return after(value, *onward) if left == min(2, far - 1) else value

    came = ring_sums(
        both_ways(lambda offset: kv_part[index_of[offset]], far, far - 1),
        kv_hold,
        turn=[from_below[2], from_above[2]] if far > 2 else [],
    )
    kv_own = (
        kv_part[index_of[0]].astype(F32) + came[0].astype(F32) + came[1].astype(F32)
    ).astype(BF16)
    weight_query, weight_out = w_query[0], w_out[0]
    queries = [query([text_own, from_below[1], from_above[1]], weight_query, text_scales)]
    kv_own = after(kv_own, queries[0], *far_chunks)
    kv_pieces = [kv_own]
    for step in range(1, sharing):
        pairs = [
            (m, m // sharing * sharing + (m % sharing + step) % sharing) for m in range(mp_count)
        ]
        kv_pieces.append(lax.ppermute(kv_own, "mp", pairs))

    behind = []
    if parts == 2:
        behind = [up(after(below, kv_own)[cut:]), down(after(above, kv_own)[:cut])]

    def attend_to(offsets, rows, sizes):
        indices = [index_of[offset] for offset in offsets]
        return attend(meta, rows, kv_pieces, weight_out, indices, sizes, text_rows, mp_count)

    last = far - 1
    near = [sign * distance for distance in range(1, last) for sign in (-1, 1)]
    out_parts = {offset: [None] * parts for offset in [last, -last]}
    first = [far] * parts + [-last, last]
    first_queries = query(far_chunks + onward, weight_query)
    first_part = attend_to(first, first_queries, [cut] * len(first))
    out_parts[far] = out_parts[-far] = first_part[:parts]
    out_parts[-last][0], out_parts[last][parts - 1] = first_part[parts:]
    ready = first_part[0]
    for distance in range(2, last):
        rows = [after(from_below[distance], ready), from_above[distance]]
        queries.append(query(rows, weight_query))
    rest_queries = jnp.concatenate(queries, axis=0)
    if parts == 2:
        behind_queries = after(query(behind, weight_query), rest_queries, ready)
        behind_part = attend_to([-last, last], behind_queries, [cut] * 2)
        out_parts[-last][1], out_parts[last][0] = behind_part
        ready = behind_part[0]
    sizes = [text_rows] + [cut] * (parts * len(near))
    own_part, *near_part = attend_to([0] + near, after(rest_queries, ready, text_next), sizes)
    for index, offset in enumerate(near):
        out_parts[offset] = near_part[parts * index :][:parts]
    own_next = to_next(own_part)

    branch_chains = [
        chain
        for part, distances in enumerate(reach)
        for chain in both_ways(
            lambda offset, part=part: out_parts[offset][part],
            *distances,
            up_across,
            down_across,
        )
    ]

    def branch_hold(left, value):
        if left == 1:
            return after(value, own_next)
        return after(value, *behind) if left == last else value

    turns = [0, 3, 1, 2] if parts == 2 else [0, 1]
    came = ring_sums([branch_chains[turn] for turn in turns], branch_hold)
    came = [came[turns.index(index)] for index in range(2 * parts)]
    result = text_next
    for part in range(parts):
        place = slice(part * cut, (part + 1) * cut)
        branch = own_next[place].astype(F32)
        for value in came[2 * part : 2 * part + 2]:
            branch = branch + value.astype(F32)
        rows = (text_next[place].astype(F32) + jnp.tanh(gate_next[0]) * branch).astype(BF16)
        result = lax.dynamic_update_slice(result, rows, (part * cut, 0))
    return result[None]


def solution(mesh):
    mesh_shape = dict(mesh.shape)

    def body(*arrays):
        return local(mesh_shape, *arrays)

    return jax.shard_map(
        body,
        mesh=mesh,
        in_specs=(
            P("section", "mp", None),
            P("section", "mp"),
            P("mp", None),
            P("section", None, "mp"),
            P("section", "mp", None),
            P("section", "mp", None),
            P("section"),
            P(),
            P(),
        ),
        out_specs=P("section", "mp", None),
        check_vma=False,
    )
```

```python
import math

import jax
import jax.numpy as jnp
import numpy as np
from jax import lax
from jax.experimental import pallas as pl
from jax.experimental.pallas import tpu as pltpu
from jax.sharding import PartitionSpec as P

HD = 128
HEADS = 32
KVH = 4
SAMP_SECTION = 4
TXT = 128
TT = 32
MAXT = 4
BLOCK = MAXT * TT
SLOTS = SAMP_SECTION * BLOCK
F32 = jnp.float32
BF16 = jnp.bfloat16
VMEM_LIMIT = 24 * 1024 * 1024
VMEM_MOST = 50 * 1024 * 1024
QUICK = pl.CostEstimate(flops=1, bytes_accessed=1, transcendentals=0)
VMEM_SMALL = 16 * 1024 * 1024


def ring_order(count):
    wide = 2 if count <= 8 else 4
    tall = count // wide
    if count < 4 or count % wide or tall % 2:
        return list(range(count))
    order = [row * wide for row in range(tall)]
    for turn, row in enumerate(reversed(range(tall))):
        columns = range(1, wide) if turn % 2 == 0 else range(wide - 1, 0, -1)
        order += [row * wide + column for column in columns]
    return order


def own_samples(tile_counts, section_table, section_id):
    samples_all = tile_counts.shape[0]
    sample_ids = jnp.arange(samples_all, dtype=jnp.int32)
    same_section = section_table[None, :] == section_table[:, None]
    before = sample_ids[None, :] < sample_ids[:, None]
    ranking = jnp.sum((same_section & before).astype(jnp.int32), axis=1)
    picked = (section_table[None, :] == section_id) & (
        ranking[None, :] == jnp.arange(SAMP_SECTION, dtype=jnp.int32)[:, None]
    )
    first_row = TT * jnp.sum(jnp.where(before, tile_counts[None, :], 0), axis=1)
    counts_own = jnp.sum(jnp.where(picked, tile_counts[None, :], 0), axis=1)
    starts_own = jnp.sum(jnp.where(picked, first_row[None, :], 0), axis=1)
    return starts_own, counts_own


def add(one, other):
    return (one.astype(F32) + other.astype(F32)).astype(BF16)


def params(limit=VMEM_LIMIT):
    return pltpu.CompilerParams(vmem_limit_bytes=limit)


def total_of(groups):
    parts, count = len(groups), len(groups[0])
    part_rows, columns = groups[0][0].shape
    rows = parts * part_rows

    def kernel(*refs):
        for part in range(parts):
            total = refs[part * count][...].astype(F32)
            for ref in refs[part * count + 1 : (part + 1) * count]:
                total += ref[...].astype(F32)
            refs[-1][part * part_rows : (part + 1) * part_rows, :] = total.astype(BF16)

    return pl.pallas_call(
        kernel,
        in_specs=[pl.BlockSpec(memory_space=pltpu.VMEM)] * (parts * count),
        out_specs=pl.BlockSpec(memory_space=pltpu.VMEM),
        out_shape=jax.ShapeDtypeStruct((rows, columns), BF16),
        compiler_params=params(VMEM_SMALL),
        cost_estimate=QUICK,
        name="total_of",
    )(*[value for group in groups for value in group])


def project(places, feats, weight, order_len, first, blocks):
    rows, depth = feats.shape
    half = rows // 2
    wide = weight.shape[1] // order_len

    def kernel(places_ref, feats_ref, weight_ref, *out_refs):
        product = jnp.dot(
            feats_ref[...], weight_ref[...], preferred_element_type=F32
        ).astype(BF16)
        for block in range(blocks):

            @pl.when(pl.program_id(0) == block)
            def _():
                out_refs[2 * block][...] = product[:half]
                out_refs[2 * block + 1][...] = product[half:]

    halves = pl.pallas_call(
        kernel,
        grid_spec=pltpu.PrefetchScalarGridSpec(
            num_scalar_prefetch=1,
            grid=(blocks,),
            in_specs=[
                pl.BlockSpec((rows, depth), lambda i, places: (0, 0)),
                pl.BlockSpec((depth, wide), lambda i, places: (0, places[first + i])),
            ],
            out_specs=[pl.BlockSpec((half, wide), lambda i, places: (0, 0))] * (2 * blocks),
        ),
        out_shape=[jax.ShapeDtypeStruct((half, wide), BF16)] * (2 * blocks),
        compiler_params=params(VMEM_MOST),
        cost_estimate=pl.CostEstimate(
            flops=2 * rows * depth * wide * blocks,
            bytes_accessed=2 * (depth + rows) * wide * blocks,
            transcendentals=0,
        ),
        name="project",
    )(places, feats, weight)
    return [halves[2 * block : 2 * block + 2] for block in range(blocks)]


def key_values(meta, pieces, weight, order_len, section_count, sharing):
    feat_rows = pieces[0].shape[0]
    depth, width = weight.shape
    kv_rows = SLOTS // sharing
    half_width = width // 2
    count = len(pieces)

    def kernel(meta_ref, *refs):
        piece_refs, weight_ref = refs[:count], refs[count]
        out_refs, kv_ref = refs[count + 1 : -1], refs[-1]
        section = meta_ref[order_len + 1]
        slot = lax.broadcasted_iota(jnp.int32, (BLOCK, feat_rows), 0)
        packed = lax.broadcasted_iota(jnp.int32, (BLOCK, feat_rows), 1)
        for sample in range(SAMP_SECTION):
            start = meta_ref[order_len + 2 + sample]
            live = TT * meta_ref[order_len + 2 + SAMP_SECTION + sample]
            image = jnp.zeros((BLOCK, depth), F32)
            for index in range(count):
                step, swapped = index // 2, index % 2
                origin = lax.rem(section + (section_count - 2 * step), section_count)
                if swapped:
                    origin = origin + 1 - 2 * lax.rem(origin, 2)
                chosen = (slot < live) & (packed == slot + (start - origin * feat_rows))
                image += jnp.dot(
                    chosen.astype(F32).astype(BF16),
                    piece_refs[index][...],
                    preferred_element_type=F32,
                )
            kv_ref[sample * BLOCK : (sample + 1) * BLOCK, :] = jnp.dot(
                image.astype(BF16), weight_ref[...], preferred_element_type=F32
            ).astype(BF16)
        for index in range(order_len):
            target = meta_ref[index]
            row = pl.multiple_of(lax.rem(target, sharing) * kv_rows, kv_rows)
            column = pl.multiple_of(target // sharing * HD, HD)
            out_refs[index][:, :HD] = kv_ref[pl.ds(row, kv_rows), pl.ds(column, HD)]
            out_refs[index][:, HD:] = kv_ref[
                pl.ds(row, kv_rows), pl.ds(pl.multiple_of(column + half_width, HD), HD)
            ]

    whole = pl.BlockSpec(memory_space=pltpu.VMEM)
    return pl.pallas_call(
        kernel,
        in_specs=[pl.BlockSpec(memory_space=pltpu.SMEM)] + [whole] * (count + 1),
        out_specs=[whole] * order_len,
        out_shape=[jax.ShapeDtypeStruct((kv_rows, 2 * HD), BF16)] * order_len,
        scratch_shapes=[pltpu.VMEM((SLOTS, width), BF16)],
        compiler_params=params(),
        cost_estimate=QUICK,
        name="key_values",
    )(meta, *pieces, weight)


def row_scale(rows):
    wider = rows.astype(F32)
    return lax.rsqrt(jnp.mean(wider * wider, axis=-1, keepdims=True) + 1e-05)


def row_scales(chunks):
    rows = sum(chunk.shape[0] for chunk in chunks)
    depth = chunks[0].shape[1]

    def kernel(*refs):
        first = 0
        for chunk_ref in refs[:-1]:
            size = chunk_ref.shape[0]
            refs[-1][first : first + size, :] = jnp.broadcast_to(
                row_scale(chunk_ref[...]), (size, HD)
            )
            first += size

    return pl.pallas_call(
        kernel,
        in_specs=[pl.BlockSpec(memory_space=pltpu.VMEM)] * len(chunks),
        out_specs=pl.BlockSpec(memory_space=pltpu.VMEM),
        out_shape=jax.ShapeDtypeStruct((rows, HD), F32),
        compiler_params=params(VMEM_SMALL),
        cost_estimate=pl.CostEstimate(
            flops=4 * rows * depth, bytes_accessed=8 * rows * depth, transcendentals=0
        ),
        name="row_scales",
    )(*chunks)


def query(chunks, weight, scales=None):
    rows = sum(chunk.shape[0] for chunk in chunks)
    depth, width = weight.shape
    wide = min(2 * HD, width)
    count = len(chunks)
    given = [] if scales is None else [scales]

    def kernel(*refs):
        chunk_refs, weight_ref, out_ref = refs[:count], refs[count], refs[-3]
        rows_ref, scale_ref = refs[-2:]

        @pl.when(pl.program_id(0) == 0)
        def _():
            first = 0
            for chunk_ref in chunk_refs:
                place = slice(first, first + chunk_ref.shape[0])
                chunk = chunk_ref[...]
                rows_ref[place, :] = chunk
                if scales is None:
                    scale_ref[place, :] = row_scale(chunk)
                first += chunk_ref.shape[0]
            if scales is not None:
                scale_ref[...] = refs[count + 1][:, :1]

        projected = jnp.dot(rows_ref[...], weight_ref[...], preferred_element_type=F32)
        projected = projected * scale_ref[...]
        for head in range(wide // HD):
            one = projected[:, head * HD : (head + 1) * HD]
            one = one * lax.rsqrt(jnp.mean(one * one, axis=-1, keepdims=True) + 1e-06)
            out_ref[:, head * HD : (head + 1) * HD] = one.astype(BF16)

    return pl.pallas_call(
        kernel,
        grid=(width // wide,),
        in_specs=[pl.BlockSpec(chunk.shape, lambda i: (0, 0)) for chunk in chunks]
        + [pl.BlockSpec((depth, wide), lambda i: (0, i))]
        + [pl.BlockSpec((rows, HD), lambda i: (0, 0)) for _ in given],
        out_specs=pl.BlockSpec((rows, wide), lambda i: (0, i)),
        out_shape=jax.ShapeDtypeStruct((rows, width), BF16),
        scratch_shapes=[pltpu.VMEM((rows, depth), BF16), pltpu.VMEM((rows, 1), F32)],
        compiler_params=params(),
        cost_estimate=pl.CostEstimate(
            flops=2 * rows * depth * width,
            bytes_accessed=2 * depth * (width + rows),
            transcendentals=0,
        ),
        name="query",
    )(*chunks, weight, *given)


def attend(meta, queries, kv_pieces, weight, indices, sizes, shard_rows, order_len):
    text_rows = queries.shape[0] // len(indices)
    rows, width = queries.shape
    heads = width // HD
    sharing = len(kv_pieces)
    kv_rows = SLOTS // sharing
    columns = weight.shape[1]
    wide = min(1024, columns)
    tall = min(64, width)

    def kernel(meta_ref, query_ref, *refs):
        kv_refs, weight_ref = refs[:sharing], refs[sharing]
        out_refs = refs[sharing + 1 : -5]
        key_ref, value_ref, attended_ref, held_ref, sems = refs[-5:]
        step = pl.program_id(0)

        def fetch(index):
            place = pl.ds(index * tall, tall)
            return pltpu.make_async_copy(
                weight_ref.at[place, :], held_ref.at[place, :], sems.at[index]
            )

        @pl.when(step == 0)
        def _():
            for index in range(width // tall):
                fetch(index).start()
            mine = lax.rem(meta_ref[order_len], sharing)
            for piece in range(sharing):
                row = pl.multiple_of(
                    lax.rem(mine + sharing - piece, sharing) * kv_rows, kv_rows
                )
                keys = kv_refs[piece][:, :HD].astype(F32)
                keys = keys * lax.rsqrt(jnp.mean(keys * keys, axis=-1, keepdims=True) + 1e-06)
                key_ref[pl.ds(row, kv_rows), :] = keys.astype(BF16)
                value_ref[pl.ds(row, kv_rows), :] = kv_refs[piece][:, HD:]
            for place, index in enumerate(indices):
                sample = meta_ref[index] * shard_rows // TXT
                slots = pl.ds(pl.multiple_of(sample * BLOCK, BLOCK), BLOCK)
                live = TT * meta_ref[order_len + 2 + SAMP_SECTION + sample]
                first = place * text_rows
                own = query_ref[first : first + text_rows, :]
                stacked = jnp.concatenate(
                    [own[:, h * HD : (h + 1) * HD] for h in range(heads)], axis=0
                )
                scores = lax.dot_general(
                    stacked,
                    key_ref[slots, :],
                    (((1,), (1,)), ((), ())),
                    preferred_element_type=F32,
                ) * (1.0 / math.sqrt(HD))
                slot = lax.broadcasted_iota(jnp.int32, scores.shape, 1)
                raised = jnp.where(slot < live, jnp.exp(scores), 0.0)
                weights = (raised / jnp.sum(raised, axis=-1, keepdims=True)).astype(BF16)
                result = jnp.dot(
                    weights, value_ref[slots, :], preferred_element_type=F32
                ).astype(BF16)
                for h in range(heads):
                    attended_ref[first : first + text_rows, h * HD : (h + 1) * HD] = result[
                        h * text_rows : (h + 1) * text_rows
                    ]
            for index in range(width // tall):
                fetch(index).wait()

        product = jnp.dot(
            attended_ref[...],
            held_ref[:, pl.ds(pl.multiple_of(step * wide, wide), wide)],
            preferred_element_type=F32,
        ).astype(BF16)
        first = 0
        for out_ref, size in zip(out_refs, sizes):
            out_ref[...] = product[first : first + size]
            first += size

    return pl.pallas_call(
        kernel,
        grid_spec=pltpu.PrefetchScalarGridSpec(
            num_scalar_prefetch=1,
            grid=(columns // wide,),
            in_specs=[pl.BlockSpec((rows, width), lambda i, meta: (0, 0))]
            + [pl.BlockSpec(piece.shape, lambda i, meta: (0, 0)) for piece in kv_pieces]
            + [pl.BlockSpec(memory_space=pl.ANY)],
            out_specs=[pl.BlockSpec((size, wide), lambda i, meta: (0, i)) for size in sizes],
            scratch_shapes=[
                pltpu.VMEM((SLOTS, HD), BF16),
                pltpu.VMEM((SLOTS, HD), BF16),
                pltpu.VMEM((rows, width), BF16),
                pltpu.VMEM((width, columns), BF16),
                pltpu.SemaphoreType.DMA((width // tall,)),
            ],
        ),
        out_shape=[jax.ShapeDtypeStruct((size, columns), BF16) for size in sizes],
        compiler_params=params(),
        cost_estimate=pl.CostEstimate(
            flops=8 * rows * width * columns,
            bytes_accessed=8 * width * columns,
            transcendentals=rows * heads * BLOCK,
        ),
        name="attend",
    )(meta, queries, *kv_pieces, weight)


def after(value, *others):
    if not others:
        return value
    return lax.optimization_barrier((value, *others))[0]


def local(
    mesh_shape,
    text_state,
    tile_feats,
    w_proj,
    w_query,
    w_kv,
    w_out,
    attn_gate,
    tile_counts,
    section_table,
):
    mp_count, section_count = mesh_shape["mp"], mesh_shape["section"]
    ring = ring_order(mp_count)
    far = mp_count // 2
    sharing = mp_count // KVH
    order = [far]
    for distance in range(far - 1, 0, -1):
        order += [-distance, distance]
    order.append(0)
    index_of = {offset: index for index, offset in enumerate(order)}
    index_of[-far] = 0
    table = np.array(
        [
            [ring[(ring.index(m) + offset) % mp_count] for offset in order] + [m, s]
            for s in range(section_count)
            for m in range(mp_count)
        ],
        np.int32,
    )
    device = lax.axis_index(("section", "mp"))
    places = lax.dynamic_slice(
        jnp.asarray(table), (device, 0), (1, mp_count + 2)
    ).reshape(-1)
    starts, counts = own_samples(tile_counts, section_table, places[mp_count + 1])
    meta = jnp.concatenate([places, starts, counts])

    up_pairs = [(ring[i], ring[(i + 1) % mp_count]) for i in range(mp_count)]
    down_pairs = [(target, source) for source, target in up_pairs]

    def up(value):
        return lax.ppermute(value, "mp", up_pairs)

    def down(value):
        return lax.ppermute(value, "mp", down_pairs)

    def across(pairs):
        return [
            (s * mp_count + a, ((s + 1) % section_count) * mp_count + b)
            for s in range(section_count)
            for a, b in pairs
        ]

    def up_across(value):
        return lax.ppermute(value, ("section", "mp"), across(up_pairs))

    def down_across(value):
        return lax.ppermute(value, ("section", "mp"), across(down_pairs))

    def to_next(value):
        return lax.ppermute(
            value, "section", [(s, (s + 1) % section_count) for s in range(section_count)]
        )

    def ring_sums(chains, hold=lambda left, value: value, turn=()):
        running = [part(sign * distance) for part, distance, sign, _, _ in chains]
        for hop in range(far):
            for index, (part, distance, sign, move, last) in enumerate(chains):
                left = distance - hop
                if left == 1:
                    running[index] = last(hold(left, running[index]))
                elif left > 1:
                    came = after(move(hold(left, running[index])), *turn)
                    running[index] = add(came, part(sign * (left - 1)))
                    turn = [running[index]]
        return running

    def both_ways(part, distance_up, distance_down, last_up=up, last_down=down):
        return [
            (part, distance_up, 1, up, last_up),
            (part, distance_down, -1, down, last_down),
        ]

    text_own = text_state[0]
    text_rows = text_own.shape[0]
    parts = 2 if text_rows % 32 == 0 else 1
    cut = text_rows // parts
    reach = [(far, far - 1), (far - 1, far)][:parts]
    text_next = to_next(text_own)
    gate_next = to_next(attn_gate)
    from_below, from_above = [text_own], [text_own]

    def text_round(*first):
        from_below.append(up(after(from_below[-1], *first)))
        from_above.append(down(after(from_above[-1], *first)))

    text_round()

    image_parts = project(places, tile_feats, w_proj, mp_count, 0, 1)
    image_parts += project(places, tile_feats, w_proj, mp_count, 1, mp_count - 1)
    image_chains = [
        chain
        for half, distances in enumerate(((far, far - 1), (far - 1, far)))
        for chain in both_ways(
            lambda offset, half=half: image_parts[index_of[offset]][half], *distances
        )
    ]

    text_scales = row_scales([text_own, from_below[1], from_above[1]])

    turns = [0, 3, 1, 2]
    came = ring_sums(
        [image_chains[turn] for turn in turns], turn=[gate_next, text_scales]
    )
    came = [came[turns.index(index)] for index in range(4)]
    image_cols = total_of(
        [[image_parts[index_of[0]][half], *came[2 * half : 2 * half + 2]] for half in range(2)]
    )

    text_round(image_cols)
    pieces = []
    moving = image_cols
    for step in range(section_count // 2):
        pieces += [
            moving,
            lax.ppermute(moving, "section", [(s, s ^ 1) for s in range(section_count)]),
        ]
        if step + 1 < section_count // 2:
            moving = lax.ppermute(
                moving,
                "section",
                [(s, (s + 2) % section_count) for s in range(section_count)],
            )

    kv_part = key_values(meta, pieces, w_kv[0], mp_count, section_count, sharing)

    for distance in range(3, far - 1):
        text_round(*([kv_part[0]] if distance == 3 else []))
    below, above = (after(value[-1], kv_part[0]) for value in (from_below, from_above))
    low = slice(text_rows - cut, text_rows)
    onward = [up(below[:cut]), down(above[low])]
    far_chunks = [up(onward[0])]
    if parts == 2:
        far_chunks.append(down(onward[1]))

    def kv_hold(left, value):
        return after(value, *onward) if left == min(2, far - 1) else value

    came = ring_sums(
        both_ways(lambda offset: kv_part[index_of[offset]], far, far - 1),
        kv_hold,
        turn=[from_below[2], from_above[2]] if far > 2 else [],
    )
    kv_own = (
        kv_part[index_of[0]].astype(F32) + came[0].astype(F32) + came[1].astype(F32)
    ).astype(BF16)
    weight_query, weight_out = w_query[0], w_out[0]
    queries = [query([text_own, from_below[1], from_above[1]], weight_query, text_scales)]
    kv_own = after(kv_own, queries[0], *far_chunks)
    kv_pieces = [kv_own]
    for step in range(1, sharing):
        pairs = [
            (m, m // sharing * sharing + (m % sharing + step) % sharing) for m in range(mp_count)
        ]
        kv_pieces.append(lax.ppermute(kv_own, "mp", pairs))

    behind = []
    if parts == 2:
        behind = [up(after(below, kv_own)[cut:]), down(after(above, kv_own)[:cut])]

    def attend_to(offsets, rows, sizes):
        indices = [index_of[offset] for offset in offsets]
        return attend(meta, rows, kv_pieces, weight_out, indices, sizes, text_rows, mp_count)

    last = far - 1
    near = [sign * distance for distance in range(1, last) for sign in (-1, 1)]
    out_parts = {offset: [None] * parts for offset in [last, -last]}
    first = [far] * parts + [-last, last]
    first_queries = query(far_chunks + onward, weight_query)
    first_part = attend_to(first, first_queries, [cut] * len(first))
    out_parts[far] = out_parts[-far] = first_part[:parts]
    out_parts[-last][0], out_parts[last][parts - 1] = first_part[parts:]
    ready = first_part[0]
    for distance in range(2, last):
        rows = [after(from_below[distance], ready), from_above[distance]]
        queries.append(query(rows, weight_query))
    rest_queries = jnp.concatenate(queries, axis=0)
    if parts == 2:
        behind_queries = after(query(behind, weight_query), rest_queries, ready)
        behind_part = attend_to([-last, last], behind_queries, [cut] * 2)
        out_parts[-last][1], out_parts[last][0] = behind_part
        ready = behind_part[0]
    sizes = [text_rows] + [cut] * (parts * len(near))
    own_part, *near_part = attend_to([0] + near, after(rest_queries, ready, text_next), sizes)
    for index, offset in enumerate(near):
        out_parts[offset] = near_part[parts * index :][:parts]
    own_next = to_next(own_part)

    branch_chains = [
        chain
        for part, distances in enumerate(reach)
        for chain in both_ways(
            lambda offset, part=part: out_parts[offset][part],
            *distances,
            up_across,
            down_across,
        )
    ]

    def branch_hold(left, value):
        if left == 1:
            return after(value, own_next)
        return after(value, *behind) if left == last else value

    turns = [0, 3, 1, 2] if parts == 2 else [0, 1]
    came = ring_sums([branch_chains[turn] for turn in turns], branch_hold)
    came = [came[turns.index(index)] for index in range(2 * parts)]
    results = []
    for part in range(parts):
        place = slice(part * cut, (part + 1) * cut)
        branch = own_next[place].astype(F32)
        for value in came[2 * part : 2 * part + 2]:
            branch = branch + value.astype(F32)
        results.append(
            (text_next[place].astype(F32) + jnp.tanh(gate_next[0]) * branch).astype(BF16)
        )
    return jnp.concatenate(results, axis=0)[None]


def solution(mesh):
    mesh_shape = dict(mesh.shape)

    def body(*arrays):
        return local(mesh_shape, *arrays)

    return jax.shard_map(
        body,
        mesh=mesh,
        in_specs=(
            P("section", "mp", None),
            P("section", "mp"),
            P("mp", None),
            P("section", None, "mp"),
            P("section", "mp", None),
            P("section", "mp", None),
            P("section"),
            P(),
            P(),
        ),
        out_specs=P("section", "mp", None),
        check_vma=False,
    )
```

```python
import math

import jax
import jax.numpy as jnp
import numpy as np
from jax import lax
from jax.experimental import pallas as pl
from jax.experimental.pallas import tpu as pltpu
from jax.sharding import PartitionSpec as P

HD = 128
HEADS = 32
KVH = 4
SAMP_SECTION = 4
TXT = 128
TT = 32
MAXT = 4
BLOCK = MAXT * TT
SLOTS = SAMP_SECTION * BLOCK
F32 = jnp.float32
BF16 = jnp.bfloat16
VMEM_LIMIT = 24 * 1024 * 1024
VMEM_MOST = 50 * 1024 * 1024
QUICK = pl.CostEstimate(flops=1, bytes_accessed=1, transcendentals=0)
VMEM_SMALL = 16 * 1024 * 1024


def ring_order(count):
    wide = 2 if count <= 8 else 4
    tall = count // wide
    if count < 4 or count % wide or tall % 2:
        return list(range(count))
    order = [row * wide for row in range(tall)]
    for turn, row in enumerate(reversed(range(tall))):
        columns = range(1, wide) if turn % 2 == 0 else range(wide - 1, 0, -1)
        order += [row * wide + column for column in columns]
    return order


def own_samples(tile_counts, section_table, section_id):
    samples_all = tile_counts.shape[0]
    sample_ids = jnp.arange(samples_all, dtype=jnp.int32)
    same_section = section_table[None, :] == section_table[:, None]
    before = sample_ids[None, :] < sample_ids[:, None]
    ranking = jnp.sum((same_section & before).astype(jnp.int32), axis=1)
    picked = (section_table[None, :] == section_id) & (
        ranking[None, :] == jnp.arange(SAMP_SECTION, dtype=jnp.int32)[:, None]
    )
    first_row = TT * jnp.sum(jnp.where(before, tile_counts[None, :], 0), axis=1)
    counts_own = jnp.sum(jnp.where(picked, tile_counts[None, :], 0), axis=1)
    starts_own = jnp.sum(jnp.where(picked, first_row[None, :], 0), axis=1)
    return starts_own, counts_own


def add(one, other):
    return (one.astype(F32) + other.astype(F32)).astype(BF16)


def params(limit=VMEM_LIMIT):
    return pltpu.CompilerParams(vmem_limit_bytes=limit)


def total_of(groups):
    parts, count = len(groups), len(groups[0])
    part_rows, columns = groups[0][0].shape
    rows = parts * part_rows

    def kernel(*refs):
        for part in range(parts):
            total = refs[part * count][...].astype(F32)
            for ref in refs[part * count + 1 : (part + 1) * count]:
                total += ref[...].astype(F32)
            refs[-1][part * part_rows : (part + 1) * part_rows, :] = total.astype(BF16)

    return pl.pallas_call(
        kernel,
        in_specs=[pl.BlockSpec(memory_space=pltpu.VMEM)] * (parts * count),
        out_specs=pl.BlockSpec(memory_space=pltpu.VMEM),
        out_shape=jax.ShapeDtypeStruct((rows, columns), BF16),
        compiler_params=params(VMEM_SMALL),
        cost_estimate=QUICK,
        name="total_of",
    )(*[value for group in groups for value in group])


def project(places, feats, weight, order_len, first, blocks):
    rows, depth = feats.shape
    half = rows // 2
    wide = weight.shape[1] // order_len

    def kernel(places_ref, feats_ref, weight_ref, *out_refs):
        product = jnp.dot(
            feats_ref[...], weight_ref[...], preferred_element_type=F32
        ).astype(BF16)
        for block in range(blocks):

            @pl.when(pl.program_id(0) == block)
            def _():
                out_refs[2 * block][...] = product[:half]
                out_refs[2 * block + 1][...] = product[half:]

    halves = pl.pallas_call(
        kernel,
        grid_spec=pltpu.PrefetchScalarGridSpec(
            num_scalar_prefetch=1,
            grid=(blocks,),
            in_specs=[
                pl.BlockSpec((rows, depth), lambda i, places: (0, 0)),
                pl.BlockSpec((depth, wide), lambda i, places: (0, places[first + i])),
            ],
            out_specs=[pl.BlockSpec((half, wide), lambda i, places: (0, 0))] * (2 * blocks),
        ),
        out_shape=[jax.ShapeDtypeStruct((half, wide), BF16)] * (2 * blocks),
        compiler_params=params(VMEM_MOST),
        cost_estimate=pl.CostEstimate(
            flops=2 * rows * depth * wide * blocks,
            bytes_accessed=2 * (depth + rows) * wide * blocks,
            transcendentals=0,
        ),
        name="project",
    )(places, feats, weight)
    return [halves[2 * block : 2 * block + 2] for block in range(blocks)]


def key_values(meta, pieces, weight, order_len, section_count, sharing):
    feat_rows = pieces[0].shape[0]
    depth, width = weight.shape
    kv_rows = SLOTS // sharing
    half_width = width // 2
    count = len(pieces)

    def kernel(meta_ref, *refs):
        piece_refs, weight_ref = refs[:count], refs[count]
        out_refs, kv_ref = refs[count + 1 : -1], refs[-1]
        section = meta_ref[order_len + 1]
        slot = lax.broadcasted_iota(jnp.int32, (BLOCK, feat_rows), 0)
        packed = lax.broadcasted_iota(jnp.int32, (BLOCK, feat_rows), 1)
        for sample in range(SAMP_SECTION):
            start = meta_ref[order_len + 2 + sample]
            live = TT * meta_ref[order_len + 2 + SAMP_SECTION + sample]
            image = jnp.zeros((BLOCK, depth), F32)
            for index in range(count):
                step, swapped = index // 2, index % 2
                origin = lax.rem(section + (section_count - 2 * step), section_count)
                if swapped:
                    origin = origin + 1 - 2 * lax.rem(origin, 2)
                chosen = (slot < live) & (packed == slot + (start - origin * feat_rows))
                image += jnp.dot(
                    chosen.astype(F32).astype(BF16),
                    piece_refs[index][...],
                    preferred_element_type=F32,
                )
            kv_ref[sample * BLOCK : (sample + 1) * BLOCK, :] = jnp.dot(
                image.astype(BF16), weight_ref[...], preferred_element_type=F32
            ).astype(BF16)
        for index in range(order_len):
            target = meta_ref[index]
            row = pl.multiple_of(lax.rem(target, sharing) * kv_rows, kv_rows)
            column = pl.multiple_of(target // sharing * HD, HD)
            out_refs[index][:, :HD] = kv_ref[pl.ds(row, kv_rows), pl.ds(column, HD)]
            out_refs[index][:, HD:] = kv_ref[
                pl.ds(row, kv_rows), pl.ds(pl.multiple_of(column + half_width, HD), HD)
            ]

    whole = pl.BlockSpec(memory_space=pltpu.VMEM)
    return pl.pallas_call(
        kernel,
        in_specs=[pl.BlockSpec(memory_space=pltpu.SMEM)] + [whole] * (count + 1),
        out_specs=[whole] * order_len,
        out_shape=[jax.ShapeDtypeStruct((kv_rows, 2 * HD), BF16)] * order_len,
        scratch_shapes=[pltpu.VMEM((SLOTS, width), BF16)],
        compiler_params=params(),
        cost_estimate=QUICK,
        name="key_values",
    )(meta, *pieces, weight)


def row_scale(rows):
    wider = rows.astype(F32)
    return lax.rsqrt(jnp.mean(wider * wider, axis=-1, keepdims=True) + 1e-05)


def row_scales(chunks):
    rows = sum(chunk.shape[0] for chunk in chunks)
    depth = chunks[0].shape[1]

    def kernel(*refs):
        first = 0
        for chunk_ref in refs[:-1]:
            size = chunk_ref.shape[0]
            refs[-1][first : first + size, :] = jnp.broadcast_to(
                row_scale(chunk_ref[...]), (size, HD)
            )
            first += size

    return pl.pallas_call(
        kernel,
        in_specs=[pl.BlockSpec(memory_space=pltpu.VMEM)] * len(chunks),
        out_specs=pl.BlockSpec(memory_space=pltpu.VMEM),
        out_shape=jax.ShapeDtypeStruct((rows, HD), F32),
        compiler_params=params(VMEM_SMALL),
        cost_estimate=pl.CostEstimate(
            flops=4 * rows * depth, bytes_accessed=8 * rows * depth, transcendentals=0
        ),
        name="row_scales",
    )(*chunks)


def query(chunks, weight, scales=None):
    rows = sum(chunk.shape[0] for chunk in chunks)
    depth, width = weight.shape
    wide = min(2 * HD, width)
    count = len(chunks)
    given = [] if scales is None else [scales]

    def kernel(*refs):
        chunk_refs, weight_ref, out_ref = refs[:count], refs[count], refs[-3]
        rows_ref, scale_ref = refs[-2:]

        @pl.when(pl.program_id(0) == 0)
        def _():
            first = 0
            for chunk_ref in chunk_refs:
                place = slice(first, first + chunk_ref.shape[0])
                chunk = chunk_ref[...]
                rows_ref[place, :] = chunk
                if scales is None:
                    scale_ref[place, :] = row_scale(chunk)
                first += chunk_ref.shape[0]
            if scales is not None:
                scale_ref[...] = refs[count + 1][:, :1]

        projected = jnp.dot(rows_ref[...], weight_ref[...], preferred_element_type=F32)
        projected = projected * scale_ref[...]
        for head in range(wide // HD):
            one = projected[:, head * HD : (head + 1) * HD]
            one = one * lax.rsqrt(jnp.mean(one * one, axis=-1, keepdims=True) + 1e-06)
            out_ref[:, head * HD : (head + 1) * HD] = one.astype(BF16)

    return pl.pallas_call(
        kernel,
        grid=(width // wide,),
        in_specs=[pl.BlockSpec(chunk.shape, lambda i: (0, 0)) for chunk in chunks]
        + [pl.BlockSpec((depth, wide), lambda i: (0, i))]
        + [pl.BlockSpec((rows, HD), lambda i: (0, 0)) for _ in given],
        out_specs=pl.BlockSpec((rows, wide), lambda i: (0, i)),
        out_shape=jax.ShapeDtypeStruct((rows, width), BF16),
        scratch_shapes=[pltpu.VMEM((rows, depth), BF16), pltpu.VMEM((rows, 1), F32)],
        compiler_params=params(),
        cost_estimate=pl.CostEstimate(
            flops=2 * rows * depth * width,
            bytes_accessed=2 * depth * (width + rows),
            transcendentals=0,
        ),
        name="query",
    )(*chunks, weight, *given)


def attend(meta, queries, kv_pieces, weight, indices, sizes, shard_rows, order_len):
    text_rows = queries.shape[0] // len(indices)
    rows, width = queries.shape
    heads = width // HD
    sharing = len(kv_pieces)
    kv_rows = SLOTS // sharing
    columns = weight.shape[1]
    wide = min(1024, columns)
    tall = min(64, width)

    def kernel(meta_ref, query_ref, *refs):
        kv_refs, weight_ref = refs[:sharing], refs[sharing]
        out_refs = refs[sharing + 1 : -5]
        key_ref, value_ref, attended_ref, held_ref, sems = refs[-5:]
        step = pl.program_id(0)

        def fetch(index):
            place = pl.ds(index * tall, tall)
            return pltpu.make_async_copy(
                weight_ref.at[place, :], held_ref.at[place, :], sems.at[index]
            )

        @pl.when(step == 0)
        def _():
            for index in range(width // tall):
                fetch(index).start()
            mine = lax.rem(meta_ref[order_len], sharing)
            for piece in range(sharing):
                row = pl.multiple_of(
                    lax.rem(mine + sharing - piece, sharing) * kv_rows, kv_rows
                )
                keys = kv_refs[piece][:, :HD].astype(F32)
                keys = keys * lax.rsqrt(jnp.mean(keys * keys, axis=-1, keepdims=True) + 1e-06)
                key_ref[pl.ds(row, kv_rows), :] = keys.astype(BF16)
                value_ref[pl.ds(row, kv_rows), :] = kv_refs[piece][:, HD:]
            for place, index in enumerate(indices):
                sample = meta_ref[index] * shard_rows // TXT
                slots = pl.ds(pl.multiple_of(sample * BLOCK, BLOCK), BLOCK)
                live = TT * meta_ref[order_len + 2 + SAMP_SECTION + sample]
                first = place * text_rows
                own = query_ref[first : first + text_rows, :]
                stacked = jnp.concatenate(
                    [own[:, h * HD : (h + 1) * HD] for h in range(heads)], axis=0
                )
                scores = lax.dot_general(
                    stacked,
                    key_ref[slots, :],
                    (((1,), (1,)), ((), ())),
                    preferred_element_type=F32,
                ) * (1.0 / math.sqrt(HD))
                slot = lax.broadcasted_iota(jnp.int32, scores.shape, 1)
                raised = jnp.where(slot < live, jnp.exp(scores), 0.0)
                weights = (raised / jnp.sum(raised, axis=-1, keepdims=True)).astype(BF16)
                result = jnp.dot(
                    weights, value_ref[slots, :], preferred_element_type=F32
                ).astype(BF16)
                for h in range(heads):
                    attended_ref[first : first + text_rows, h * HD : (h + 1) * HD] = result[
                        h * text_rows : (h + 1) * text_rows
                    ]
            for index in range(width // tall):
                fetch(index).wait()

        product = jnp.dot(
            attended_ref[...],
            held_ref[:, pl.ds(pl.multiple_of(step * wide, wide), wide)],
            preferred_element_type=F32,
        ).astype(BF16)
        first = 0
        for out_ref, size in zip(out_refs, sizes):
            out_ref[...] = product[first : first + size]
            first += size

    return pl.pallas_call(
        kernel,
        grid_spec=pltpu.PrefetchScalarGridSpec(
            num_scalar_prefetch=1,
            grid=(columns // wide,),
            in_specs=[pl.BlockSpec((rows, width), lambda i, meta: (0, 0))]
            + [pl.BlockSpec(piece.shape, lambda i, meta: (0, 0)) for piece in kv_pieces]
            + [pl.BlockSpec(memory_space=pl.ANY)],
            out_specs=[pl.BlockSpec((size, wide), lambda i, meta: (0, i)) for size in sizes],
            scratch_shapes=[
                pltpu.VMEM((SLOTS, HD), BF16),
                pltpu.VMEM((SLOTS, HD), BF16),
                pltpu.VMEM((rows, width), BF16),
                pltpu.VMEM((width, columns), BF16),
                pltpu.SemaphoreType.DMA((width // tall,)),
            ],
        ),
        out_shape=[jax.ShapeDtypeStruct((size, columns), BF16) for size in sizes],
        compiler_params=params(),
        cost_estimate=pl.CostEstimate(
            flops=8 * rows * width * columns,
            bytes_accessed=8 * width * columns,
            transcendentals=rows * heads * BLOCK,
        ),
        name="attend",
    )(meta, queries, *kv_pieces, weight)


def after(value, *others):
    if not others:
        return value
    return lax.optimization_barrier((value, *others))[0]


def local(
    mesh_shape,
    text_state,
    tile_feats,
    w_proj,
    w_query,
    w_kv,
    w_out,
    attn_gate,
    tile_counts,
    section_table,
):
    mp_count, section_count = mesh_shape["mp"], mesh_shape["section"]
    ring = ring_order(mp_count)
    far = mp_count // 2
    sharing = mp_count // KVH
    order = [far]
    for distance in range(far - 1, 0, -1):
        order += [-distance, distance]
    order.append(0)
    index_of = {offset: index for index, offset in enumerate(order)}
    index_of[-far] = 0
    table = np.array(
        [
            [ring[(ring.index(m) + offset) % mp_count] for offset in order] + [m, s]
            for s in range(section_count)
            for m in range(mp_count)
        ],
        np.int32,
    )
    device = lax.axis_index(("section", "mp"))
    places = lax.dynamic_slice(
        jnp.asarray(table), (device, 0), (1, mp_count + 2)
    ).reshape(-1)
    starts, counts = own_samples(tile_counts, section_table, places[mp_count + 1])
    meta = jnp.concatenate([places, starts, counts])

    up_pairs = [(ring[i], ring[(i + 1) % mp_count]) for i in range(mp_count)]
    down_pairs = [(target, source) for source, target in up_pairs]

    def up(value):
        return lax.ppermute(value, "mp", up_pairs)

    def down(value):
        return lax.ppermute(value, "mp", down_pairs)

    def across(pairs):
        return [
            (s * mp_count + a, ((s + 1) % section_count) * mp_count + b)
            for s in range(section_count)
            for a, b in pairs
        ]

    def up_across(value):
        return lax.ppermute(value, ("section", "mp"), across(up_pairs))

    def down_across(value):
        return lax.ppermute(value, ("section", "mp"), across(down_pairs))

    def to_next(value):
        return lax.ppermute(
            value, "section", [(s, (s + 1) % section_count) for s in range(section_count)]
        )

    def ring_sums(chains, hold=lambda left, value: value, turn=()):
        running = [part(sign * distance) for part, distance, sign, _, _ in chains]
        for hop in range(far):
            for index, (part, distance, sign, move, last) in enumerate(chains):
                left = distance - hop
                if left == 1:
                    running[index] = last(hold(left, running[index]))
                elif left > 1:
                    came = after(move(hold(left, running[index])), *turn)
                    running[index] = add(came, part(sign * (left - 1)))
                    turn = [running[index]]
        return running

    def both_ways(part, distance_up, distance_down, last_up=up, last_down=down):
        return [
            (part, distance_up, 1, up, last_up),
            (part, distance_down, -1, down, last_down),
        ]

    text_own = text_state[0]
    text_rows = text_own.shape[0]
    parts = 2 if text_rows % 32 == 0 else 1
    cut = text_rows // parts
    reach = [(far, far - 1), (far - 1, far)][:parts]
    text_next = to_next(text_own)
    gate_next = to_next(attn_gate)
    from_below, from_above = [text_own], [text_own]

    def text_round(*first):
        from_below.append(up(after(from_below[-1], *first)))
        from_above.append(down(after(from_above[-1], *first)))

    text_round()

    image_parts = project(places, tile_feats, w_proj, mp_count, 0, 1)
    image_parts += project(places, tile_feats, w_proj, mp_count, 1, mp_count - 1)
    image_chains = [
        chain
        for half, distances in enumerate(((far, far - 1), (far - 1, far)))
        for chain in both_ways(
            lambda offset, half=half: image_parts[index_of[offset]][half], *distances
        )
    ]

    text_scales = row_scales([text_own, from_below[1], from_above[1]])

    turns = [0, 3, 1, 2]
    came = ring_sums(
        [image_chains[turn] for turn in turns], turn=[gate_next, text_scales]
    )
    came = [came[turns.index(index)] for index in range(4)]
    image_cols = total_of(
        [[image_parts[index_of[0]][half], *came[2 * half : 2 * half + 2]] for half in range(2)]
    )

    text_round(image_cols)
    pieces = []
    moving = image_cols
    for step in range(section_count // 2):
        pieces += [
            moving,
            lax.ppermute(moving, "section", [(s, s ^ 1) for s in range(section_count)]),
        ]
        if step + 1 < section_count // 2:
            moving = lax.ppermute(
                moving,
                "section",
                [(s, (s + 2) % section_count) for s in range(section_count)],
            )

    kv_part = key_values(meta, pieces, w_kv[0], mp_count, section_count, sharing)

    for distance in range(3, far - 1):
        text_round(*([kv_part[0]] if distance == 3 else []))
    below, above = (after(value[-1], kv_part[0]) for value in (from_below, from_above))
    low = slice(text_rows - cut, text_rows)
    fine = 2 if parts == 2 and cut % 32 == 0 and far > 3 else 1
    size = cut // fine

    def both(values, *first):
        return [up(after(values[0], *first)), down(after(values[1], *first))]

    def piece(index):
        start = index * size
        return [below[start : start + size], above[low][start : start + size]]

    onward, distant, sent = [both(piece(0))], [], []

    def kv_hold(left, value):
        sent.append(value)
        if fine == 2 and len(sent) == 4:
            onward.append(both(piece(1), *sent[2:]))
        if fine == 2 and len(sent) == 6:
            distant.append(both(onward[0], *sent[4:]))
        if fine == 2 and len(sent) == 7:
            distant.append(both(onward[1], sent[6]))
        if left == min(2, far - 1):
            return after(value, *onward[0])
        return after(value, *onward[-1]) if left == 1 else value

    came = ring_sums(
        both_ways(lambda offset: kv_part[index_of[offset]], far, far - 1),
        kv_hold,
        turn=[from_below[2], from_above[2]] if far > 2 else [],
    )
    kv_own = (
        kv_part[index_of[0]].astype(F32) + came[0].astype(F32) + came[1].astype(F32)
    ).astype(BF16)
    weight_query, weight_out = w_query[0], w_out[0]
    queries = [query([text_own, from_below[1], from_above[1]], weight_query, text_scales)]
    if fine == 1:
        distant = [both(onward[0])[:parts]]
    kv_own = after(kv_own, queries[0], *distant[0])
    kv_pieces = [kv_own]
    for step in range(1, sharing):
        pairs = [
            (m, m // sharing * sharing + (m % sharing + step) % sharing) for m in range(mp_count)
        ]
        kv_pieces.append(lax.ppermute(kv_own, "mp", pairs))

    behind = []
    if parts == 2:
        behind = [up(after(below, kv_own)[cut:]), down(after(above, kv_own)[:cut])]

    def attend_to(offsets, rows, sizes):
        indices = [index_of[offset] for offset in offsets]
        return attend(meta, rows, kv_pieces, weight_out, indices, sizes, text_rows, mp_count)

    last = far - 1
    near = [sign * distance for distance in range(1, last) for sign in (-1, 1)]
    out_parts = {offset: [None] * parts for offset in [last, -last]}
    first = [far] * parts + [-last, last]
    first_chunks = [
        pair[side]
        for pieces in (distant, onward)
        for side in range(len(pieces[0]))
        for pair in pieces
    ]
    first_queries = query(first_chunks, weight_query)
    first_part = attend_to(first, first_queries, [cut] * len(first))
    out_parts[far] = out_parts[-far] = first_part[:parts]
    out_parts[-last][0], out_parts[last][parts - 1] = first_part[parts:]
    ready = first_part[0]
    for distance in range(2, last):
        rows = [after(from_below[distance], ready), from_above[distance]]
        queries.append(query(rows, weight_query))
    rest_queries = jnp.concatenate(queries, axis=0)
    if parts == 2:
        behind_queries = after(query(behind, weight_query), rest_queries, ready)
        behind_part = attend_to([-last, last], behind_queries, [cut] * 2)
        out_parts[-last][1], out_parts[last][0] = behind_part
        ready = behind_part[0]
    sizes = [text_rows] + [cut] * (parts * len(near))
    own_part, *near_part = attend_to([0] + near, after(rest_queries, ready, text_next), sizes)
    for index, offset in enumerate(near):
        out_parts[offset] = near_part[parts * index :][:parts]
    own_next = to_next(own_part)

    branch_chains = [
        chain
        for part, distances in enumerate(reach)
        for chain in both_ways(
            lambda offset, part=part: out_parts[offset][part],
            *distances,
            up_across,
            down_across,
        )
    ]

    def branch_hold(left, value):
        if left == 1:
            return after(value, own_next)
        return after(value, *behind) if left == last else value

    turns = [0, 3, 1, 2] if parts == 2 else [0, 1]
    came = ring_sums([branch_chains[turn] for turn in turns], branch_hold)
    came = [came[turns.index(index)] for index in range(2 * parts)]
    results = []
    for part in range(parts):
        place = slice(part * cut, (part + 1) * cut)
        branch = own_next[place].astype(F32)
        for value in came[2 * part : 2 * part + 2]:
            branch = branch + value.astype(F32)
        results.append(
            (text_next[place].astype(F32) + jnp.tanh(gate_next[0]) * branch).astype(BF16)
        )
    return jnp.concatenate(results, axis=0)[None]


def solution(mesh):
    mesh_shape = dict(mesh.shape)

    def body(*arrays):
        return local(mesh_shape, *arrays)

    return jax.shard_map(
        body,
        mesh=mesh,
        in_specs=(
            P("section", "mp", None),
            P("section", "mp"),
            P("mp", None),
            P("section", None, "mp"),
            P("section", "mp", None),
            P("section", "mp", None),
            P("section"),
            P(),
            P(),
        ),
        out_specs=P("section", "mp", None),
        check_vma=False,
    )
```

```python
import math

import jax
import jax.numpy as jnp
import numpy as np
from jax import lax
from jax.experimental import pallas as pl
from jax.experimental.pallas import tpu as pltpu
from jax.sharding import PartitionSpec as P

HD = 128
HEADS = 32
KVH = 4
SAMP_SECTION = 4
TXT = 128
TT = 32
MAXT = 4
BLOCK = MAXT * TT
SLOTS = SAMP_SECTION * BLOCK
F32 = jnp.float32
BF16 = jnp.bfloat16
VMEM_LIMIT = 24 * 1024 * 1024
VMEM_MOST = 50 * 1024 * 1024
QUICK = pl.CostEstimate(flops=1, bytes_accessed=1, transcendentals=0)
VMEM_SMALL = 16 * 1024 * 1024


def ring_order(count):
    wide = 2 if count <= 8 else 4
    tall = count // wide
    if count < 4 or count % wide or tall % 2:
        return list(range(count))
    order = [row * wide for row in range(tall)]
    for turn, row in enumerate(reversed(range(tall))):
        columns = range(1, wide) if turn % 2 == 0 else range(wide - 1, 0, -1)
        order += [row * wide + column for column in columns]
    return order


def own_samples(tile_counts, section_table, section_id):
    samples_all = tile_counts.shape[0]
    sample_ids = jnp.arange(samples_all, dtype=jnp.int32)
    same_section = section_table[None, :] == section_table[:, None]
    before = sample_ids[None, :] < sample_ids[:, None]
    ranking = jnp.sum((same_section & before).astype(jnp.int32), axis=1)
    picked = (section_table[None, :] == section_id) & (
        ranking[None, :] == jnp.arange(SAMP_SECTION, dtype=jnp.int32)[:, None]
    )
    first_row = TT * jnp.sum(jnp.where(before, tile_counts[None, :], 0), axis=1)
    counts_own = jnp.sum(jnp.where(picked, tile_counts[None, :], 0), axis=1)
    starts_own = jnp.sum(jnp.where(picked, first_row[None, :], 0), axis=1)
    return starts_own, counts_own


def add(one, other):
    return (one.astype(F32) + other.astype(F32)).astype(BF16)


def params(limit=VMEM_LIMIT):
    return pltpu.CompilerParams(vmem_limit_bytes=limit)


def total_of(groups):
    parts, count = len(groups), len(groups[0])
    part_rows, columns = groups[0][0].shape
    rows = parts * part_rows

    def kernel(*refs):
        for part in range(parts):
            total = refs[part * count][...].astype(F32)
            for ref in refs[part * count + 1 : (part + 1) * count]:
                total += ref[...].astype(F32)
            refs[-1][part * part_rows : (part + 1) * part_rows, :] = total.astype(BF16)

    return pl.pallas_call(
        kernel,
        in_specs=[pl.BlockSpec(memory_space=pltpu.VMEM)] * (parts * count),
        out_specs=pl.BlockSpec(memory_space=pltpu.VMEM),
        out_shape=jax.ShapeDtypeStruct((rows, columns), BF16),
        compiler_params=params(VMEM_SMALL),
        cost_estimate=QUICK,
        name="total_of",
    )(*[value for group in groups for value in group])


def project(places, feats, weight, order_len, first, blocks):
    rows, depth = feats.shape
    half = rows // 2
    wide = weight.shape[1] // order_len

    def kernel(places_ref, feats_ref, weight_ref, *out_refs):
        product = jnp.dot(
            feats_ref[...], weight_ref[...], preferred_element_type=F32
        ).astype(BF16)
        for block in range(blocks):

            @pl.when(pl.program_id(0) == block)
            def _():
                out_refs[2 * block][...] = product[:half]
                out_refs[2 * block + 1][...] = product[half:]

    halves = pl.pallas_call(
        kernel,
        grid_spec=pltpu.PrefetchScalarGridSpec(
            num_scalar_prefetch=1,
            grid=(blocks,),
            in_specs=[
                pl.BlockSpec((rows, depth), lambda i, places: (0, 0)),
                pl.BlockSpec((depth, wide), lambda i, places: (0, places[first + i])),
            ],
            out_specs=[pl.BlockSpec((half, wide), lambda i, places: (0, 0))] * (2 * blocks),
        ),
        out_shape=[jax.ShapeDtypeStruct((half, wide), BF16)] * (2 * blocks),
        compiler_params=params(VMEM_MOST),
        cost_estimate=pl.CostEstimate(
            flops=2 * rows * depth * wide * blocks,
            bytes_accessed=2 * (depth + rows) * wide * blocks,
            transcendentals=0,
        ),
        name="project",
    )(places, feats, weight)
    return [halves[2 * block : 2 * block + 2] for block in range(blocks)]


def key_values(meta, pieces, weight, order_len, section_count, sharing):
    feat_rows = pieces[0].shape[0]
    depth, width = weight.shape
    kv_rows = SLOTS // sharing
    half_width = width // 2
    count = len(pieces)

    def kernel(meta_ref, *refs):
        piece_refs, weight_ref = refs[:count], refs[count]
        out_refs, (image_ref, kv_ref) = refs[count + 1 : -2], refs[-2:]
        section = meta_ref[order_len + 1]
        origins = []
        for index in range(count):
            origin = lax.rem(section + (section_count - 2 * (index // 2)), section_count)
            origins.append(origin + 1 - 2 * lax.rem(origin, 2) if index % 2 else origin)
        for slot in range(SAMP_SECTION * MAXT):
            sample, tile = slot // MAXT, slot % MAXT
            live = tile < meta_ref[order_len + 2 + SAMP_SECTION + sample]
            row = meta_ref[order_len + 2 + sample] + TT * tile
            origin_of = lax.div(row, feat_rows)
            place = pl.ds(pl.multiple_of(row - origin_of * feat_rows, TT), TT)
            own = slice(slot * TT, (slot + 1) * TT)
            for index in range(count):

                @pl.when(live & (origin_of == origins[index]))
                def _(index=index, own=own, place=place):
                    image_ref[own, :] = piece_refs[index][place, :]

            @pl.when(jnp.logical_not(live))
            def _(own=own):
                image_ref[own, :] = jnp.zeros((TT, depth), BF16)

        kv_ref[...] = jnp.dot(
            image_ref[...], weight_ref[...], preferred_element_type=F32
        ).astype(BF16)
        for index in range(order_len):
            target = meta_ref[index]
            row = pl.multiple_of(lax.rem(target, sharing) * kv_rows, kv_rows)
            column = pl.multiple_of(target // sharing * HD, HD)
            out_refs[index][:, :HD] = kv_ref[pl.ds(row, kv_rows), pl.ds(column, HD)]
            out_refs[index][:, HD:] = kv_ref[
                pl.ds(row, kv_rows), pl.ds(pl.multiple_of(column + half_width, HD), HD)
            ]

    whole = pl.BlockSpec(memory_space=pltpu.VMEM)
    return pl.pallas_call(
        kernel,
        in_specs=[pl.BlockSpec(memory_space=pltpu.SMEM)] + [whole] * (count + 1),
        out_specs=[whole] * order_len,
        out_shape=[jax.ShapeDtypeStruct((kv_rows, 2 * HD), BF16)] * order_len,
        scratch_shapes=[pltpu.VMEM((SLOTS, depth), BF16), pltpu.VMEM((SLOTS, width), BF16)],
        compiler_params=params(),
        cost_estimate=QUICK,
        name="key_values",
    )(meta, *pieces, weight)


def row_scale(rows):
    wider = rows.astype(F32)
    return lax.rsqrt(jnp.mean(wider * wider, axis=-1, keepdims=True) + 1e-05)


def row_scales(chunks):
    rows = sum(chunk.shape[0] for chunk in chunks)
    depth = chunks[0].shape[1]

    def kernel(*refs):
        first = 0
        for chunk_ref in refs[:-1]:
            size = chunk_ref.shape[0]
            refs[-1][first : first + size, :] = jnp.broadcast_to(
                row_scale(chunk_ref[...]), (size, HD)
            )
            first += size

    return pl.pallas_call(
        kernel,
        in_specs=[pl.BlockSpec(memory_space=pltpu.VMEM)] * len(chunks),
        out_specs=pl.BlockSpec(memory_space=pltpu.VMEM),
        out_shape=jax.ShapeDtypeStruct((rows, HD), F32),
        compiler_params=params(VMEM_SMALL),
        cost_estimate=pl.CostEstimate(
            flops=4 * rows * depth, bytes_accessed=8 * rows * depth, transcendentals=0
        ),
        name="row_scales",
    )(*chunks)


def query(chunks, weight, scales=None):
    rows = sum(chunk.shape[0] for chunk in chunks)
    depth, width = weight.shape
    wide = min(2 * HD, width)
    count = len(chunks)
    given = [] if scales is None else [scales]

    def kernel(*refs):
        chunk_refs, weight_ref, out_ref = refs[:count], refs[count], refs[-3]
        rows_ref, scale_ref = refs[-2:]

        @pl.when(pl.program_id(0) == 0)
        def _():
            first = 0
            for chunk_ref in chunk_refs:
                place = slice(first, first + chunk_ref.shape[0])
                chunk = chunk_ref[...]
                rows_ref[place, :] = chunk
                if scales is None:
                    scale_ref[place, :] = row_scale(chunk)
                first += chunk_ref.shape[0]
            if scales is not None:
                scale_ref[...] = refs[count + 1][:, :1]

        projected = jnp.dot(rows_ref[...], weight_ref[...], preferred_element_type=F32)
        projected = projected * scale_ref[...]
        for head in range(wide // HD):
            one = projected[:, head * HD : (head + 1) * HD]
            one = one * lax.rsqrt(jnp.mean(one * one, axis=-1, keepdims=True) + 1e-06)
            out_ref[:, head * HD : (head + 1) * HD] = one.astype(BF16)

    return pl.pallas_call(
        kernel,
        grid=(width // wide,),
        in_specs=[pl.BlockSpec(chunk.shape, lambda i: (0, 0)) for chunk in chunks]
        + [pl.BlockSpec((depth, wide), lambda i: (0, i))]
        + [pl.BlockSpec((rows, HD), lambda i: (0, 0)) for _ in given],
        out_specs=pl.BlockSpec((rows, wide), lambda i: (0, i)),
        out_shape=jax.ShapeDtypeStruct((rows, width), BF16),
        scratch_shapes=[pltpu.VMEM((rows, depth), BF16), pltpu.VMEM((rows, 1), F32)],
        compiler_params=params(),
        cost_estimate=pl.CostEstimate(
            flops=2 * rows * depth * width,
            bytes_accessed=2 * depth * (width + rows),
            transcendentals=0,
        ),
        name="query",
    )(*chunks, weight, *given)


def attend(meta, queries, kv_pieces, weight, indices, sizes, shard_rows, order_len):
    text_rows = queries.shape[0] // len(indices)
    rows, width = queries.shape
    heads = width // HD
    sharing = len(kv_pieces)
    kv_rows = SLOTS // sharing
    columns = weight.shape[1]
    wide = min(1024, columns)
    tall = min(64, width)

    def kernel(meta_ref, query_ref, *refs):
        kv_refs, weight_ref = refs[:sharing], refs[sharing]
        out_refs = refs[sharing + 1 : -5]
        key_ref, value_ref, attended_ref, held_ref, sems = refs[-5:]
        step = pl.program_id(0)

        def fetch(index):
            place = pl.ds(index * tall, tall)
            return pltpu.make_async_copy(
                weight_ref.at[place, :], held_ref.at[place, :], sems.at[index]
            )

        @pl.when(step == 0)
        def _():
            for index in range(width // tall):
                fetch(index).start()
            mine = lax.rem(meta_ref[order_len], sharing)
            for piece in range(sharing):
                row = pl.multiple_of(
                    lax.rem(mine + sharing - piece, sharing) * kv_rows, kv_rows
                )
                keys = kv_refs[piece][:, :HD].astype(F32)
                keys = keys * lax.rsqrt(jnp.mean(keys * keys, axis=-1, keepdims=True) + 1e-06)
                key_ref[pl.ds(row, kv_rows), :] = keys.astype(BF16)
                value_ref[pl.ds(row, kv_rows), :] = kv_refs[piece][:, HD:]
            for place, index in enumerate(indices):
                sample = meta_ref[index] * shard_rows // TXT
                slots = pl.ds(pl.multiple_of(sample * BLOCK, BLOCK), BLOCK)
                live = TT * meta_ref[order_len + 2 + SAMP_SECTION + sample]
                first = place * text_rows
                own = query_ref[first : first + text_rows, :]
                stacked = jnp.concatenate(
                    [own[:, h * HD : (h + 1) * HD] for h in range(heads)], axis=0
                )
                scores = lax.dot_general(
                    stacked,
                    key_ref[slots, :],
                    (((1,), (1,)), ((), ())),
                    preferred_element_type=F32,
                ) * (1.0 / math.sqrt(HD))
                slot = lax.broadcasted_iota(jnp.int32, scores.shape, 1)
                raised = jnp.where(slot < live, jnp.exp(scores), 0.0)
                weights = (raised / jnp.sum(raised, axis=-1, keepdims=True)).astype(BF16)
                result = jnp.dot(
                    weights, value_ref[slots, :], preferred_element_type=F32
                ).astype(BF16)
                for h in range(heads):
                    attended_ref[first : first + text_rows, h * HD : (h + 1) * HD] = result[
                        h * text_rows : (h + 1) * text_rows
                    ]
            for index in range(width // tall):
                fetch(index).wait()

        product = jnp.dot(
            attended_ref[...],
            held_ref[:, pl.ds(pl.multiple_of(step * wide, wide), wide)],
            preferred_element_type=F32,
        ).astype(BF16)
        first = 0
        for out_ref, size in zip(out_refs, sizes):
            out_ref[...] = product[first : first + size]
            first += size

    return pl.pallas_call(
        kernel,
        grid_spec=pltpu.PrefetchScalarGridSpec(
            num_scalar_prefetch=1,
            grid=(columns // wide,),
            in_specs=[pl.BlockSpec((rows, width), lambda i, meta: (0, 0))]
            + [pl.BlockSpec(piece.shape, lambda i, meta: (0, 0)) for piece in kv_pieces]
            + [pl.BlockSpec(memory_space=pl.ANY)],
            out_specs=[pl.BlockSpec((size, wide), lambda i, meta: (0, i)) for size in sizes],
            scratch_shapes=[
                pltpu.VMEM((SLOTS, HD), BF16),
                pltpu.VMEM((SLOTS, HD), BF16),
                pltpu.VMEM((rows, width), BF16),
                pltpu.VMEM((width, columns), BF16),
                pltpu.SemaphoreType.DMA((width // tall,)),
            ],
        ),
        out_shape=[jax.ShapeDtypeStruct((size, columns), BF16) for size in sizes],
        compiler_params=params(),
        cost_estimate=pl.CostEstimate(
            flops=8 * rows * width * columns,
            bytes_accessed=8 * width * columns,
            transcendentals=rows * heads * BLOCK,
        ),
        name="attend",
    )(meta, queries, *kv_pieces, weight)


def after(value, *others):
    if not others:
        return value
    return lax.optimization_barrier((value, *others))[0]


def local(
    mesh_shape,
    text_state,
    tile_feats,
    w_proj,
    w_query,
    w_kv,
    w_out,
    attn_gate,
    tile_counts,
    section_table,
):
    mp_count, section_count = mesh_shape["mp"], mesh_shape["section"]
    ring = ring_order(mp_count)
    far = mp_count // 2
    sharing = mp_count // KVH
    order = [far]
    for distance in range(far - 1, 0, -1):
        order += [-distance, distance]
    order.append(0)
    index_of = {offset: index for index, offset in enumerate(order)}
    index_of[-far] = 0
    table = np.array(
        [
            [ring[(ring.index(m) + offset) % mp_count] for offset in order] + [m, s]
            for s in range(section_count)
            for m in range(mp_count)
        ],
        np.int32,
    )
    device = lax.axis_index(("section", "mp"))
    places = lax.dynamic_slice(
        jnp.asarray(table), (device, 0), (1, mp_count + 2)
    ).reshape(-1)
    starts, counts = own_samples(tile_counts, section_table, places[mp_count + 1])
    meta = jnp.concatenate([places, starts, counts])

    up_pairs = [(ring[i], ring[(i + 1) % mp_count]) for i in range(mp_count)]
    down_pairs = [(target, source) for source, target in up_pairs]

    def up(value):
        return lax.ppermute(value, "mp", up_pairs)

    def down(value):
        return lax.ppermute(value, "mp", down_pairs)

    def across(pairs):
        return [
            (s * mp_count + a, ((s + 1) % section_count) * mp_count + b)
            for s in range(section_count)
            for a, b in pairs
        ]

    def up_across(value):
        return lax.ppermute(value, ("section", "mp"), across(up_pairs))

    def down_across(value):
        return lax.ppermute(value, ("section", "mp"), across(down_pairs))

    def to_next(value):
        return lax.ppermute(
            value, "section", [(s, (s + 1) % section_count) for s in range(section_count)]
        )

    def ring_sums(chains, hold=lambda left, value: value, turn=()):
        running = [part(sign * distance) for part, distance, sign, _, _ in chains]
        for hop in range(far):
            for index, (part, distance, sign, move, last) in enumerate(chains):
                left = distance - hop
                if left == 1:
                    running[index] = last(hold(left, running[index]))
                elif left > 1:
                    came = after(move(hold(left, running[index])), *turn)
                    running[index] = add(came, part(sign * (left - 1)))
                    turn = [running[index]]
        return running

    def both_ways(part, distance_up, distance_down, last_up=up, last_down=down):
        return [
            (part, distance_up, 1, up, last_up),
            (part, distance_down, -1, down, last_down),
        ]

    text_own = text_state[0]
    text_rows = text_own.shape[0]
    parts = 2 if text_rows % 32 == 0 else 1
    cut = text_rows // parts
    reach = [(far, far - 1), (far - 1, far)][:parts]
    text_next = to_next(text_own)
    gate_next = to_next(attn_gate)
    from_below, from_above = [text_own], [text_own]

    def text_round(*first):
        from_below.append(up(after(from_below[-1], *first)))
        from_above.append(down(after(from_above[-1], *first)))

    text_round()

    image_parts = project(places, tile_feats, w_proj, mp_count, 0, 1)
    image_parts += project(places, tile_feats, w_proj, mp_count, 1, mp_count - 1)
    image_chains = [
        chain
        for half, distances in enumerate(((far, far - 1), (far - 1, far)))
        for chain in both_ways(
            lambda offset, half=half: image_parts[index_of[offset]][half], *distances
        )
    ]

    text_scales = row_scales([text_own, from_below[1], from_above[1]])

    turns = [0, 3, 1, 2]
    came = ring_sums(
        [image_chains[turn] for turn in turns], turn=[gate_next, text_scales]
    )
    came = [came[turns.index(index)] for index in range(4)]
    image_cols = total_of(
        [[image_parts[index_of[0]][half], *came[2 * half : 2 * half + 2]] for half in range(2)]
    )

    text_round(image_cols)
    pieces = []
    moving = image_cols
    for step in range(section_count // 2):
        pieces += [
            moving,
            lax.ppermute(moving, "section", [(s, s ^ 1) for s in range(section_count)]),
        ]
        if step + 1 < section_count // 2:
            moving = lax.ppermute(
                moving,
                "section",
                [(s, (s + 2) % section_count) for s in range(section_count)],
            )

    kv_part = key_values(meta, pieces, w_kv[0], mp_count, section_count, sharing)

    for distance in range(3, far - 1):
        text_round(*([kv_part[0]] if distance == 3 else []))
    below, above = (after(value[-1], kv_part[0]) for value in (from_below, from_above))
    low = slice(text_rows - cut, text_rows)
    onward = [up(below[:cut]), down(above[low])]
    far_chunks = [up(onward[0])]
    if parts == 2:
        far_chunks.append(down(onward[1]))

    def kv_hold(left, value):
        return after(value, *onward) if left == min(2, far - 1) else value

    came = ring_sums(
        both_ways(lambda offset: kv_part[index_of[offset]], far, far - 1),
        kv_hold,
        turn=[from_below[2], from_above[2]] if far > 2 else [],
    )
    kv_own = (
        kv_part[index_of[0]].astype(F32) + came[0].astype(F32) + came[1].astype(F32)
    ).astype(BF16)
    weight_query, weight_out = w_query[0], w_out[0]
    queries = [query([text_own, from_below[1], from_above[1]], weight_query, text_scales)]
    kv_own = after(kv_own, queries[0], *far_chunks)
    kv_pieces = [kv_own]
    for step in range(1, sharing):
        pairs = [
            (m, m // sharing * sharing + (m % sharing + step) % sharing) for m in range(mp_count)
        ]
        kv_pieces.append(lax.ppermute(kv_own, "mp", pairs))

    behind = []
    if parts == 2:
        behind = [up(after(below, kv_own)[cut:]), down(after(above, kv_own)[:cut])]

    def attend_to(offsets, rows, sizes):
        indices = [index_of[offset] for offset in offsets]
        return attend(meta, rows, kv_pieces, weight_out, indices, sizes, text_rows, mp_count)

    last = far - 1
    near = [sign * distance for distance in range(1, last) for sign in (-1, 1)]
    out_parts = {offset: [None] * parts for offset in [last, -last]}
    first = [far] * parts + [-last, last]
    first_queries = query(far_chunks + onward, weight_query)
    first_part = attend_to(first, first_queries, [cut] * len(first))
    out_parts[far] = out_parts[-far] = first_part[:parts]
    out_parts[-last][0], out_parts[last][parts - 1] = first_part[parts:]
    ready = first_part[0]
    for distance in range(2, last):
        rows = [after(from_below[distance], ready), from_above[distance]]
        queries.append(query(rows, weight_query))
    rest_queries = jnp.concatenate(queries, axis=0)
    if parts == 2:
        behind_queries = after(query(behind, weight_query), rest_queries, ready)
        behind_part = attend_to([-last, last], behind_queries, [cut] * 2)
        out_parts[-last][1], out_parts[last][0] = behind_part
        ready = behind_part[0]
    sizes = [text_rows] + [cut] * (parts * len(near))
    own_part, *near_part = attend_to([0] + near, after(rest_queries, ready, text_next), sizes)
    for index, offset in enumerate(near):
        out_parts[offset] = near_part[parts * index :][:parts]
    own_next = to_next(own_part)

    branch_chains = [
        chain
        for part, distances in enumerate(reach)
        for chain in both_ways(
            lambda offset, part=part: out_parts[offset][part],
            *distances,
            up_across,
            down_across,
        )
    ]

    def branch_hold(left, value):
        if left == 1:
            return after(value, own_next)
        return after(value, *behind) if left == last else value

    turns = [0, 3, 1, 2] if parts == 2 else [0, 1]
    came = ring_sums([branch_chains[turn] for turn in turns], branch_hold)
    came = [came[turns.index(index)] for index in range(2 * parts)]
    results = []
    for part in range(parts):
        place = slice(part * cut, (part + 1) * cut)
        branch = own_next[place].astype(F32)
        for value in came[2 * part : 2 * part + 2]:
            branch = branch + value.astype(F32)
        results.append(
            (text_next[place].astype(F32) + jnp.tanh(gate_next[0]) * branch).astype(BF16)
        )
    return jnp.concatenate(results, axis=0)[None]


def solution(mesh):
    mesh_shape = dict(mesh.shape)

    def body(*arrays):
        return local(mesh_shape, *arrays)

    return jax.shard_map(
        body,
        mesh=mesh,
        in_specs=(
            P("section", "mp", None),
            P("section", "mp"),
            P("mp", None),
            P("section", None, "mp"),
            P("section", "mp", None),
            P("section", "mp", None),
            P("section"),
            P(),
            P(),
        ),
        out_specs=P("section", "mp", None),
        check_vma=False,
    )
```

```python
import math

import jax
import jax.numpy as jnp
import numpy as np
from jax import lax
from jax.experimental import pallas as pl
from jax.experimental.pallas import tpu as pltpu
from jax.sharding import PartitionSpec as P

HD = 128
HEADS = 32
KVH = 4
SAMP_SECTION = 4
TXT = 128
TT = 32
MAXT = 4
BLOCK = MAXT * TT
SLOTS = SAMP_SECTION * BLOCK
F32 = jnp.float32
BF16 = jnp.bfloat16
VMEM_LIMIT = 24 * 1024 * 1024
VMEM_MOST = 50 * 1024 * 1024
QUICK = pl.CostEstimate(flops=1, bytes_accessed=1, transcendentals=0)
VMEM_SMALL = 16 * 1024 * 1024


def ring_order(count):
    wide = 2 if count <= 8 else 4
    tall = count // wide
    if count < 4 or count % wide or tall % 2:
        return list(range(count))
    order = [row * wide for row in range(tall)]
    for turn, row in enumerate(reversed(range(tall))):
        columns = range(1, wide) if turn % 2 == 0 else range(wide - 1, 0, -1)
        order += [row * wide + column for column in columns]
    return order


def own_samples(tile_counts, section_table, section_id):
    samples_all = tile_counts.shape[0]
    sample_ids = jnp.arange(samples_all, dtype=jnp.int32)
    same_section = section_table[None, :] == section_table[:, None]
    before = sample_ids[None, :] < sample_ids[:, None]
    ranking = jnp.sum((same_section & before).astype(jnp.int32), axis=1)
    picked = (section_table[None, :] == section_id) & (
        ranking[None, :] == jnp.arange(SAMP_SECTION, dtype=jnp.int32)[:, None]
    )
    first_row = TT * jnp.sum(jnp.where(before, tile_counts[None, :], 0), axis=1)
    counts_own = jnp.sum(jnp.where(picked, tile_counts[None, :], 0), axis=1)
    starts_own = jnp.sum(jnp.where(picked, first_row[None, :], 0), axis=1)
    return starts_own, counts_own


def add(one, other):
    return (one.astype(F32) + other.astype(F32)).astype(BF16)


def params(limit=VMEM_LIMIT):
    return pltpu.CompilerParams(vmem_limit_bytes=limit)


def total_of(groups):
    parts, count = len(groups), len(groups[0])
    part_rows, columns = groups[0][0].shape
    rows = parts * part_rows

    def kernel(*refs):
        for part in range(parts):
            total = refs[part * count][...].astype(F32)
            for ref in refs[part * count + 1 : (part + 1) * count]:
                total += ref[...].astype(F32)
            refs[-1][part * part_rows : (part + 1) * part_rows, :] = total.astype(BF16)

    return pl.pallas_call(
        kernel,
        in_specs=[pl.BlockSpec(memory_space=pltpu.VMEM)] * (parts * count),
        out_specs=pl.BlockSpec(memory_space=pltpu.VMEM),
        out_shape=jax.ShapeDtypeStruct((rows, columns), BF16),
        compiler_params=params(VMEM_SMALL),
        cost_estimate=QUICK,
        name="total_of",
    )(*[value for group in groups for value in group])


def project(places, feats, weight, order_len, first, blocks):
    rows, depth = feats.shape
    half = rows // 2
    wide = weight.shape[1] // order_len

    def kernel(places_ref, feats_ref, weight_ref, *out_refs):
        product = jnp.dot(
            feats_ref[...], weight_ref[...], preferred_element_type=F32
        ).astype(BF16)
        for block in range(blocks):

            @pl.when(pl.program_id(0) == block)
            def _():
                out_refs[2 * block][...] = product[:half]
                out_refs[2 * block + 1][...] = product[half:]

    halves = pl.pallas_call(
        kernel,
        grid_spec=pltpu.PrefetchScalarGridSpec(
            num_scalar_prefetch=1,
            grid=(blocks,),
            in_specs=[
                pl.BlockSpec((rows, depth), lambda i, places: (0, 0)),
                pl.BlockSpec((depth, wide), lambda i, places: (0, places[first + i])),
            ],
            out_specs=[pl.BlockSpec((half, wide), lambda i, places: (0, 0))] * (2 * blocks),
        ),
        out_shape=[jax.ShapeDtypeStruct((half, wide), BF16)] * (2 * blocks),
        compiler_params=params(VMEM_MOST),
        cost_estimate=pl.CostEstimate(
            flops=2 * rows * depth * wide * blocks,
            bytes_accessed=2 * (depth + rows) * wide * blocks,
            transcendentals=0,
        ),
        name="project",
    )(places, feats, weight)
    return [halves[2 * block : 2 * block + 2] for block in range(blocks)]


def key_values(meta, pieces, weight, order_len, section_count, sharing):
    feat_rows = pieces[0].shape[0]
    depth, width = weight.shape
    kv_rows = SLOTS // sharing
    half_width = width // 2
    count = len(pieces)

    def kernel(meta_ref, *refs):
        piece_refs, weight_ref = refs[:count], refs[count]
        out_refs, (image_ref, kv_ref) = refs[count + 1 : -2], refs[-2:]
        section = meta_ref[order_len + 1]
        origins = []
        for index in range(count):
            origin = lax.rem(section + (section_count - 2 * (index // 2)), section_count)
            origins.append(origin + 1 - 2 * lax.rem(origin, 2) if index % 2 else origin)
        for slot in range(SAMP_SECTION * MAXT):
            sample, tile = slot // MAXT, slot % MAXT
            live = tile < meta_ref[order_len + 2 + SAMP_SECTION + sample]
            row = meta_ref[order_len + 2 + sample] + TT * tile
            origin_of = lax.div(row, feat_rows)
            place = pl.ds(pl.multiple_of(row - origin_of * feat_rows, TT), TT)
            own = slice(slot * TT, (slot + 1) * TT)
            for index in range(count):

                @pl.when(live & (origin_of == origins[index]))
                def _(index=index, own=own, place=place):
                    image_ref[own, :] = piece_refs[index][place, :]

            @pl.when(jnp.logical_not(live))
            def _(own=own):
                image_ref[own, :] = jnp.zeros((TT, depth), BF16)

        kv_ref[...] = jnp.dot(
            image_ref[...], weight_ref[...], preferred_element_type=F32
        ).astype(BF16)
        for index in range(order_len):
            target = meta_ref[index]
            row = pl.multiple_of(lax.rem(target, sharing) * kv_rows, kv_rows)
            column = pl.multiple_of(target // sharing * HD, HD)
            out_refs[index][:, :HD] = kv_ref[pl.ds(row, kv_rows), pl.ds(column, HD)]
            out_refs[index][:, HD:] = kv_ref[
                pl.ds(row, kv_rows), pl.ds(pl.multiple_of(column + half_width, HD), HD)
            ]

    whole = pl.BlockSpec(memory_space=pltpu.VMEM)
    return pl.pallas_call(
        kernel,
        in_specs=[pl.BlockSpec(memory_space=pltpu.SMEM)] + [whole] * (count + 1),
        out_specs=[whole] * order_len,
        out_shape=[jax.ShapeDtypeStruct((kv_rows, 2 * HD), BF16)] * order_len,
        scratch_shapes=[pltpu.VMEM((SLOTS, depth), BF16), pltpu.VMEM((SLOTS, width), BF16)],
        compiler_params=params(),
        cost_estimate=QUICK,
        name="key_values",
    )(meta, *pieces, weight)


def row_scale(rows):
    wider = rows.astype(F32)
    return lax.rsqrt(jnp.mean(wider * wider, axis=-1, keepdims=True) + 1e-05)


def row_scales(chunks):
    rows = sum(chunk.shape[0] for chunk in chunks)
    depth = chunks[0].shape[1]

    def kernel(*refs):
        first = 0
        for chunk_ref in refs[:-1]:
            size = chunk_ref.shape[0]
            refs[-1][first : first + size, :] = jnp.broadcast_to(
                row_scale(chunk_ref[...]), (size, HD)
            )
            first += size

    return pl.pallas_call(
        kernel,
        in_specs=[pl.BlockSpec(memory_space=pltpu.VMEM)] * len(chunks),
        out_specs=pl.BlockSpec(memory_space=pltpu.VMEM),
        out_shape=jax.ShapeDtypeStruct((rows, HD), F32),
        compiler_params=params(VMEM_SMALL),
        cost_estimate=pl.CostEstimate(
            flops=4 * rows * depth, bytes_accessed=8 * rows * depth, transcendentals=0
        ),
        name="row_scales",
    )(*chunks)


def query(chunks, weight, scales=None):
    rows = sum(chunk.shape[0] for chunk in chunks)
    depth, width = weight.shape
    wide = min(2 * HD, width)
    count = len(chunks)
    given = [] if scales is None else [scales]

    def kernel(*refs):
        chunk_refs, weight_ref, out_ref = refs[:count], refs[count], refs[-3]
        rows_ref, scale_ref = refs[-2:]

        @pl.when(pl.program_id(0) == 0)
        def _():
            first = 0
            for chunk_ref in chunk_refs:
                place = slice(first, first + chunk_ref.shape[0])
                chunk = chunk_ref[...]
                rows_ref[place, :] = chunk
                if scales is None:
                    scale_ref[place, :] = row_scale(chunk)
                first += chunk_ref.shape[0]
            if scales is not None:
                scale_ref[...] = refs[count + 1][:, :1]

        projected = jnp.dot(rows_ref[...], weight_ref[...], preferred_element_type=F32)
        projected = projected * scale_ref[...]
        for head in range(wide // HD):
            one = projected[:, head * HD : (head + 1) * HD]
            one = one * lax.rsqrt(jnp.mean(one * one, axis=-1, keepdims=True) + 1e-06)
            out_ref[:, head * HD : (head + 1) * HD] = one.astype(BF16)

    return pl.pallas_call(
        kernel,
        grid=(width // wide,),
        in_specs=[pl.BlockSpec(chunk.shape, lambda i: (0, 0)) for chunk in chunks]
        + [pl.BlockSpec((depth, wide), lambda i: (0, i))]
        + [pl.BlockSpec((rows, HD), lambda i: (0, 0)) for _ in given],
        out_specs=pl.BlockSpec((rows, wide), lambda i: (0, i)),
        out_shape=jax.ShapeDtypeStruct((rows, width), BF16),
        scratch_shapes=[pltpu.VMEM((rows, depth), BF16), pltpu.VMEM((rows, 1), F32)],
        compiler_params=params(),
        cost_estimate=pl.CostEstimate(
            flops=2 * rows * depth * width,
            bytes_accessed=2 * depth * (width + rows),
            transcendentals=0,
        ),
        name="query",
    )(*chunks, weight, *given)


def attend(meta, queries, kv_pieces, weight, indices, sizes, shard_rows, order_len):
    text_rows = queries.shape[0] // len(indices)
    rows, width = queries.shape
    heads = width // HD
    sharing = len(kv_pieces)
    kv_rows = SLOTS // sharing
    columns = weight.shape[1]
    wide = min(1024, columns)

    def kernel(meta_ref, query_ref, *refs):
        kv_refs, weight_ref = refs[:sharing], refs[sharing]
        out_refs = refs[sharing + 1 : -5]
        key_ref, value_ref, attended_ref, held_ref, sems = refs[-5:]
        step = pl.program_id(0)

        def fetch(index):
            place = pl.ds(pl.multiple_of(index * wide, wide), wide)
            return pltpu.make_async_copy(
                weight_ref.at[:, place], held_ref.at[index], sems.at[index]
            )

        @pl.when(step == 0)
        def _():
            for index in range(columns // wide):
                fetch(index).start()
            mine = lax.rem(meta_ref[order_len], sharing)
            for piece in range(sharing):
                row = pl.multiple_of(
                    lax.rem(mine + sharing - piece, sharing) * kv_rows, kv_rows
                )
                keys = kv_refs[piece][:, :HD].astype(F32)
                keys = keys * lax.rsqrt(jnp.mean(keys * keys, axis=-1, keepdims=True) + 1e-06)
                key_ref[pl.ds(row, kv_rows), :] = keys.astype(BF16)
                value_ref[pl.ds(row, kv_rows), :] = kv_refs[piece][:, HD:]
            for place, index in enumerate(indices):
                sample = meta_ref[index] * shard_rows // TXT
                slots = pl.ds(pl.multiple_of(sample * BLOCK, BLOCK), BLOCK)
                live = TT * meta_ref[order_len + 2 + SAMP_SECTION + sample]
                first = place * text_rows
                own = query_ref[first : first + text_rows, :]
                stacked = jnp.concatenate(
                    [own[:, h * HD : (h + 1) * HD] for h in range(heads)], axis=0
                )
                scores = lax.dot_general(
                    stacked,
                    key_ref[slots, :],
                    (((1,), (1,)), ((), ())),
                    preferred_element_type=F32,
                ) * (1.0 / math.sqrt(HD))
                slot = lax.broadcasted_iota(jnp.int32, scores.shape, 1)
                raised = jnp.where(slot < live, jnp.exp(scores), 0.0)
                weights = (raised / jnp.sum(raised, axis=-1, keepdims=True)).astype(BF16)
                result = jnp.dot(
                    weights, value_ref[slots, :], preferred_element_type=F32
                ).astype(BF16)
                for h in range(heads):
                    attended_ref[first : first + text_rows, h * HD : (h + 1) * HD] = result[
                        h * text_rows : (h + 1) * text_rows
                    ]

        fetch(step).wait()
        product = jnp.dot(
            attended_ref[...], held_ref[step], preferred_element_type=F32
        ).astype(BF16)
        first = 0
        for out_ref, size in zip(out_refs, sizes):
            out_ref[...] = product[first : first + size]
            first += size

    return pl.pallas_call(
        kernel,
        grid_spec=pltpu.PrefetchScalarGridSpec(
            num_scalar_prefetch=1,
            grid=(columns // wide,),
            in_specs=[pl.BlockSpec((rows, width), lambda i, meta: (0, 0))]
            + [pl.BlockSpec(piece.shape, lambda i, meta: (0, 0)) for piece in kv_pieces]
            + [pl.BlockSpec(memory_space=pl.ANY)],
            out_specs=[pl.BlockSpec((size, wide), lambda i, meta: (0, i)) for size in sizes],
            scratch_shapes=[
                pltpu.VMEM((SLOTS, HD), BF16),
                pltpu.VMEM((SLOTS, HD), BF16),
                pltpu.VMEM((rows, width), BF16),
                pltpu.VMEM((columns // wide, width, wide), BF16),
                pltpu.SemaphoreType.DMA((columns // wide,)),
            ],
        ),
        out_shape=[jax.ShapeDtypeStruct((size, columns), BF16) for size in sizes],
        compiler_params=params(),
        cost_estimate=pl.CostEstimate(
            flops=8 * rows * width * columns,
            bytes_accessed=8 * width * columns,
            transcendentals=rows * heads * BLOCK,
        ),
        name="attend",
    )(meta, queries, *kv_pieces, weight)


def after(value, *others):
    if not others:
        return value
    return lax.optimization_barrier((value, *others))[0]


def local(
    mesh_shape,
    text_state,
    tile_feats,
    w_proj,
    w_query,
    w_kv,
    w_out,
    attn_gate,
    tile_counts,
    section_table,
):
    mp_count, section_count = mesh_shape["mp"], mesh_shape["section"]
    ring = ring_order(mp_count)
    far = mp_count // 2
    sharing = mp_count // KVH
    order = [far]
    for distance in range(far - 1, 0, -1):
        order += [-distance, distance]
    order.append(0)
    index_of = {offset: index for index, offset in enumerate(order)}
    index_of[-far] = 0
    table = np.array(
        [
            [ring[(ring.index(m) + offset) % mp_count] for offset in order] + [m, s]
            for s in range(section_count)
            for m in range(mp_count)
        ],
        np.int32,
    )
    device = lax.axis_index(("section", "mp"))
    places = lax.dynamic_slice(
        jnp.asarray(table), (device, 0), (1, mp_count + 2)
    ).reshape(-1)
    starts, counts = own_samples(tile_counts, section_table, places[mp_count + 1])
    meta = jnp.concatenate([places, starts, counts])

    up_pairs = [(ring[i], ring[(i + 1) % mp_count]) for i in range(mp_count)]
    down_pairs = [(target, source) for source, target in up_pairs]

    def up(value):
        return lax.ppermute(value, "mp", up_pairs)

    def down(value):
        return lax.ppermute(value, "mp", down_pairs)

    def across(pairs):
        return [
            (s * mp_count + a, ((s + 1) % section_count) * mp_count + b)
            for s in range(section_count)
            for a, b in pairs
        ]

    def up_across(value):
        return lax.ppermute(value, ("section", "mp"), across(up_pairs))

    def down_across(value):
        return lax.ppermute(value, ("section", "mp"), across(down_pairs))

    def to_next(value):
        return lax.ppermute(
            value, "section", [(s, (s + 1) % section_count) for s in range(section_count)]
        )

    def ring_sums(chains, hold=lambda left, value: value, turn=()):
        running = [part(sign * distance) for part, distance, sign, _, _ in chains]
        for hop in range(far):
            for index, (part, distance, sign, move, last) in enumerate(chains):
                left = distance - hop
                if left == 1:
                    running[index] = last(hold(left, running[index]))
                elif left > 1:
                    came = after(move(hold(left, running[index])), *turn)
                    running[index] = add(came, part(sign * (left - 1)))
                    turn = [running[index]]
        return running

    def both_ways(part, distance_up, distance_down, last_up=up, last_down=down):
        return [
            (part, distance_up, 1, up, last_up),
            (part, distance_down, -1, down, last_down),
        ]

    text_own = text_state[0]
    text_rows = text_own.shape[0]
    parts = 2 if text_rows % 32 == 0 else 1
    cut = text_rows // parts
    reach = [(far, far - 1), (far - 1, far)][:parts]
    text_next = to_next(text_own)
    gate_next = to_next(attn_gate)
    from_below, from_above = [text_own], [text_own]

    def text_round(*first):
        from_below.append(up(after(from_below[-1], *first)))
        from_above.append(down(after(from_above[-1], *first)))

    text_round()

    image_parts = project(places, tile_feats, w_proj, mp_count, 0, 1)
    image_parts += project(places, tile_feats, w_proj, mp_count, 1, mp_count - 1)
    image_chains = [
        chain
        for half, distances in enumerate(((far, far - 1), (far - 1, far)))
        for chain in both_ways(
            lambda offset, half=half: image_parts[index_of[offset]][half], *distances
        )
    ]

    text_scales = row_scales([text_own, from_below[1], from_above[1]])

    turns = [0, 3, 1, 2]
    came = ring_sums(
        [image_chains[turn] for turn in turns], turn=[gate_next, text_scales]
    )
    came = [came[turns.index(index)] for index in range(4)]
    image_cols = total_of(
        [[image_parts[index_of[0]][half], *came[2 * half : 2 * half + 2]] for half in range(2)]
    )

    text_round(image_cols)
    pieces = []
    moving = image_cols
    for step in range(section_count // 2):
        pieces += [
            moving,
            lax.ppermute(moving, "section", [(s, s ^ 1) for s in range(section_count)]),
        ]
        if step + 1 < section_count // 2:
            moving = lax.ppermute(
                moving,
                "section",
                [(s, (s + 2) % section_count) for s in range(section_count)],
            )

    kv_part = key_values(meta, pieces, w_kv[0], mp_count, section_count, sharing)

    for distance in range(3, far - 1):
        text_round(*([kv_part[0]] if distance == 3 else []))
    below, above = (after(value[-1], kv_part[0]) for value in (from_below, from_above))
    low = slice(text_rows - cut, text_rows)
    onward = [up(below[:cut]), down(above[low])]
    far_chunks = [up(onward[0])]
    if parts == 2:
        far_chunks.append(down(onward[1]))

    def kv_hold(left, value):
        return after(value, *onward) if left == min(2, far - 1) else value

    came = ring_sums(
        both_ways(lambda offset: kv_part[index_of[offset]], far, far - 1),
        kv_hold,
        turn=[from_below[2], from_above[2]] if far > 2 else [],
    )
    kv_own = (
        kv_part[index_of[0]].astype(F32) + came[0].astype(F32) + came[1].astype(F32)
    ).astype(BF16)
    weight_query, weight_out = w_query[0], w_out[0]
    queries = [query([text_own, from_below[1], from_above[1]], weight_query, text_scales)]
    kv_own = after(kv_own, queries[0], *far_chunks)
    kv_pieces = [kv_own]
    for step in range(1, sharing):
        pairs = [
            (m, m // sharing * sharing + (m % sharing + step) % sharing) for m in range(mp_count)
        ]
        kv_pieces.append(lax.ppermute(kv_own, "mp", pairs))

    behind = []
    if parts == 2:
        behind = [up(after(below, kv_own)[cut:]), down(after(above, kv_own)[:cut])]

    def attend_to(offsets, rows, sizes):
        indices = [index_of[offset] for offset in offsets]
        return attend(meta, rows, kv_pieces, weight_out, indices, sizes, text_rows, mp_count)

    last = far - 1
    near = [sign * distance for distance in range(1, last) for sign in (-1, 1)]
    out_parts = {offset: [None] * parts for offset in [last, -last]}
    first = [far] * parts + [-last, last]
    first_queries = query(far_chunks + onward, weight_query)
    first_part = attend_to(first, first_queries, [cut] * len(first))
    out_parts[far] = out_parts[-far] = first_part[:parts]
    out_parts[-last][0], out_parts[last][parts - 1] = first_part[parts:]
    ready = first_part[0]
    for distance in range(2, last):
        rows = [after(from_below[distance], ready), from_above[distance]]
        queries.append(query(rows, weight_query))
    rest_queries = jnp.concatenate(queries, axis=0)
    if parts == 2:
        behind_queries = after(query(behind, weight_query), rest_queries, ready)
        behind_part = attend_to([-last, last], behind_queries, [cut] * 2)
        out_parts[-last][1], out_parts[last][0] = behind_part
        ready = behind_part[0]
    sizes = [text_rows] + [cut] * (parts * len(near))
    own_part, *near_part = attend_to([0] + near, after(rest_queries, ready, text_next), sizes)
    for index, offset in enumerate(near):
        out_parts[offset] = near_part[parts * index :][:parts]
    own_next = to_next(own_part)

    branch_chains = [
        chain
        for part, distances in enumerate(reach)
        for chain in both_ways(
            lambda offset, part=part: out_parts[offset][part],
            *distances,
            up_across,
            down_across,
        )
    ]

    def branch_hold(left, value):
        if left == 1:
            return after(value, own_next)
        return after(value, *behind) if left == last else value

    turns = [0, 3, 1, 2] if parts == 2 else [0, 1]
    came = ring_sums([branch_chains[turn] for turn in turns], branch_hold)
    came = [came[turns.index(index)] for index in range(2 * parts)]
    results = []
    for part in range(parts):
        place = slice(part * cut, (part + 1) * cut)
        branch = own_next[place].astype(F32)
        for value in came[2 * part : 2 * part + 2]:
            branch = branch + value.astype(F32)
        results.append(
            (text_next[place].astype(F32) + jnp.tanh(gate_next[0]) * branch).astype(BF16)
        )
    return jnp.concatenate(results, axis=0)[None]


def solution(mesh):
    mesh_shape = dict(mesh.shape)

    def body(*arrays):
        return local(mesh_shape, *arrays)

    return jax.shard_map(
        body,
        mesh=mesh,
        in_specs=(
            P("section", "mp", None),
            P("section", "mp"),
            P("mp", None),
            P("section", None, "mp"),
            P("section", "mp", None),
            P("section", "mp", None),
            P("section"),
            P(),
            P(),
        ),
        out_specs=P("section", "mp", None),
        check_vma=False,
    )
```

```python
import math

import jax
import jax.numpy as jnp
import numpy as np
from jax import lax
from jax.experimental import pallas as pl
from jax.experimental.pallas import tpu as pltpu
from jax.sharding import PartitionSpec as P

HD = 128
HEADS = 32
KVH = 4
SAMP_SECTION = 4
TXT = 128
TT = 32
MAXT = 4
BLOCK = MAXT * TT
SLOTS = SAMP_SECTION * BLOCK
F32 = jnp.float32
BF16 = jnp.bfloat16
VMEM_LIMIT = 24 * 1024 * 1024
VMEM_MOST = 50 * 1024 * 1024
QUICK = pl.CostEstimate(flops=1, bytes_accessed=1, transcendentals=0)
VMEM_SMALL = 16 * 1024 * 1024


def ring_order(count):
    wide = 2 if count <= 8 else 4
    tall = count // wide
    if count < 4 or count % wide or tall % 2:
        return list(range(count))
    order = [row * wide for row in range(tall)]
    for turn, row in enumerate(reversed(range(tall))):
        columns = range(1, wide) if turn % 2 == 0 else range(wide - 1, 0, -1)
        order += [row * wide + column for column in columns]
    return order


def own_samples(tile_counts, section_table, section_id):
    samples_all = tile_counts.shape[0]
    sample_ids = jnp.arange(samples_all, dtype=jnp.int32)
    same_section = section_table[None, :] == section_table[:, None]
    before = sample_ids[None, :] < sample_ids[:, None]
    ranking = jnp.sum((same_section & before).astype(jnp.int32), axis=1)
    picked = (section_table[None, :] == section_id) & (
        ranking[None, :] == jnp.arange(SAMP_SECTION, dtype=jnp.int32)[:, None]
    )
    first_row = TT * jnp.sum(jnp.where(before, tile_counts[None, :], 0), axis=1)
    counts_own = jnp.sum(jnp.where(picked, tile_counts[None, :], 0), axis=1)
    starts_own = jnp.sum(jnp.where(picked, first_row[None, :], 0), axis=1)
    return starts_own, counts_own


def add(one, other):
    return (one.astype(F32) + other.astype(F32)).astype(BF16)


def params(limit=VMEM_LIMIT):
    return pltpu.CompilerParams(vmem_limit_bytes=limit)


def total_of(groups):
    parts, count = len(groups), len(groups[0])
    part_rows, columns = groups[0][0].shape
    rows = parts * part_rows

    def kernel(*refs):
        for part in range(parts):
            total = refs[part * count][...].astype(F32)
            for ref in refs[part * count + 1 : (part + 1) * count]:
                total += ref[...].astype(F32)
            refs[-1][part * part_rows : (part + 1) * part_rows, :] = total.astype(BF16)

    return pl.pallas_call(
        kernel,
        in_specs=[pl.BlockSpec(memory_space=pltpu.VMEM)] * (parts * count),
        out_specs=pl.BlockSpec(memory_space=pltpu.VMEM),
        out_shape=jax.ShapeDtypeStruct((rows, columns), BF16),
        compiler_params=params(VMEM_SMALL),
        cost_estimate=QUICK,
        name="total_of",
    )(*[value for group in groups for value in group])


def project(places, feats, weight, order_len, first, blocks):
    rows, depth = feats.shape
    half = rows // 2
    wide = weight.shape[1] // order_len

    def kernel(places_ref, feats_ref, weight_ref, *out_refs):
        product = jnp.dot(
            feats_ref[...], weight_ref[...], preferred_element_type=F32
        ).astype(BF16)
        for block in range(blocks):

            @pl.when(pl.program_id(0) == block)
            def _():
                out_refs[2 * block][...] = product[:half]
                out_refs[2 * block + 1][...] = product[half:]

    halves = pl.pallas_call(
        kernel,
        grid_spec=pltpu.PrefetchScalarGridSpec(
            num_scalar_prefetch=1,
            grid=(blocks,),
            in_specs=[
                pl.BlockSpec((rows, depth), lambda i, places: (0, 0)),
                pl.BlockSpec((depth, wide), lambda i, places: (0, places[first + i])),
            ],
            out_specs=[pl.BlockSpec((half, wide), lambda i, places: (0, 0))] * (2 * blocks),
        ),
        out_shape=[jax.ShapeDtypeStruct((half, wide), BF16)] * (2 * blocks),
        compiler_params=params(VMEM_MOST),
        cost_estimate=pl.CostEstimate(
            flops=2 * rows * depth * wide * blocks,
            bytes_accessed=2 * (depth + rows) * wide * blocks,
            transcendentals=0,
        ),
        name="project",
    )(places, feats, weight)
    return [halves[2 * block : 2 * block + 2] for block in range(blocks)]


def key_values(meta, pieces, weight, order_len, section_count, sharing):
    feat_rows = pieces[0].shape[0]
    depth, width = weight.shape
    kv_rows = SLOTS // sharing
    half_width = width // 2
    count = len(pieces)

    def kernel(meta_ref, *refs):
        piece_refs, weight_ref = refs[:count], refs[count]
        out_refs, (image_ref, kv_ref) = refs[count + 1 : -2], refs[-2:]
        section = meta_ref[order_len + 1]
        origins = []
        for index in range(count):
            origin = lax.rem(section + (section_count - 2 * (index // 2)), section_count)
            origins.append(origin + 1 - 2 * lax.rem(origin, 2) if index % 2 else origin)
        for slot in range(SAMP_SECTION * MAXT):
            sample, tile = slot // MAXT, slot % MAXT
            live = tile < meta_ref[order_len + 2 + SAMP_SECTION + sample]
            row = meta_ref[order_len + 2 + sample] + TT * tile
            origin_of = lax.div(row, feat_rows)
            place = pl.ds(pl.multiple_of(row - origin_of * feat_rows, TT), TT)
            own = slice(slot * TT, (slot + 1) * TT)
            for index in range(count):

                @pl.when(live & (origin_of == origins[index]))
                def _(index=index, own=own, place=place):
                    image_ref[own, :] = piece_refs[index][place, :]

            @pl.when(jnp.logical_not(live))
            def _(own=own):
                image_ref[own, :] = jnp.zeros((TT, depth), BF16)

        kv_ref[...] = jnp.dot(
            image_ref[...], weight_ref[...], preferred_element_type=F32
        ).astype(BF16)
        for index in range(order_len):
            target = meta_ref[index]
            row = pl.multiple_of(lax.rem(target, sharing) * kv_rows, kv_rows)
            column = pl.multiple_of(target // sharing * HD, HD)
            out_refs[index][:, :HD] = kv_ref[pl.ds(row, kv_rows), pl.ds(column, HD)]
            out_refs[index][:, HD:] = kv_ref[
                pl.ds(row, kv_rows), pl.ds(pl.multiple_of(column + half_width, HD), HD)
            ]

    whole = pl.BlockSpec(memory_space=pltpu.VMEM)
    return pl.pallas_call(
        kernel,
        in_specs=[pl.BlockSpec(memory_space=pltpu.SMEM)] + [whole] * (count + 1),
        out_specs=[whole] * order_len,
        out_shape=[jax.ShapeDtypeStruct((kv_rows, 2 * HD), BF16)] * order_len,
        scratch_shapes=[pltpu.VMEM((SLOTS, depth), BF16), pltpu.VMEM((SLOTS, width), BF16)],
        compiler_params=params(),
        cost_estimate=QUICK,
        name="key_values",
    )(meta, *pieces, weight)


def row_scale(rows):
    wider = rows.astype(F32)
    return lax.rsqrt(jnp.mean(wider * wider, axis=-1, keepdims=True) + 1e-05)


def row_scales(chunks):
    rows = sum(chunk.shape[0] for chunk in chunks)
    depth = chunks[0].shape[1]

    def kernel(*refs):
        first = 0
        for chunk_ref in refs[:-1]:
            size = chunk_ref.shape[0]
            refs[-1][first : first + size, :] = jnp.broadcast_to(
                row_scale(chunk_ref[...]), (size, HD)
            )
            first += size

    return pl.pallas_call(
        kernel,
        in_specs=[pl.BlockSpec(memory_space=pltpu.VMEM)] * len(chunks),
        out_specs=pl.BlockSpec(memory_space=pltpu.VMEM),
        out_shape=jax.ShapeDtypeStruct((rows, HD), F32),
        compiler_params=params(VMEM_SMALL),
        cost_estimate=pl.CostEstimate(
            flops=4 * rows * depth, bytes_accessed=8 * rows * depth, transcendentals=0
        ),
        name="row_scales",
    )(*chunks)


def query(chunks, weight, scales=None):
    rows = sum(chunk.shape[0] for chunk in chunks)
    depth, width = weight.shape
    wide = min(2 * HD, width)
    count = len(chunks)
    given = [] if scales is None else [scales]

    def kernel(*refs):
        chunk_refs, weight_ref, out_ref = refs[:count], refs[count], refs[-3]
        rows_ref, scale_ref = refs[-2:]

        @pl.when(pl.program_id(0) == 0)
        def _():
            first = 0
            for chunk_ref in chunk_refs:
                place = slice(first, first + chunk_ref.shape[0])
                chunk = chunk_ref[...]
                rows_ref[place, :] = chunk
                if scales is None:
                    scale_ref[place, :] = row_scale(chunk)
                first += chunk_ref.shape[0]
            if scales is not None:
                scale_ref[...] = refs[count + 1][:, :1]

        projected = jnp.dot(rows_ref[...], weight_ref[...], preferred_element_type=F32)
        projected = projected * scale_ref[...]
        for head in range(wide // HD):
            one = projected[:, head * HD : (head + 1) * HD]
            one = one * lax.rsqrt(jnp.mean(one * one, axis=-1, keepdims=True) + 1e-06)
            out_ref[:, head * HD : (head + 1) * HD] = one.astype(BF16)

    return pl.pallas_call(
        kernel,
        grid=(width // wide,),
        in_specs=[pl.BlockSpec(chunk.shape, lambda i: (0, 0)) for chunk in chunks]
        + [pl.BlockSpec((depth, wide), lambda i: (0, i))]
        + [pl.BlockSpec((rows, HD), lambda i: (0, 0)) for _ in given],
        out_specs=pl.BlockSpec((rows, wide), lambda i: (0, i)),
        out_shape=jax.ShapeDtypeStruct((rows, width), BF16),
        scratch_shapes=[pltpu.VMEM((rows, depth), BF16), pltpu.VMEM((rows, 1), F32)],
        compiler_params=params(),
        cost_estimate=pl.CostEstimate(
            flops=2 * rows * depth * width,
            bytes_accessed=2 * depth * (width + rows),
            transcendentals=0,
        ),
        name="query",
    )(*chunks, weight, *given)


def attend(meta, queries, kv_pieces, weight, indices, sizes, shard_rows, order_len):
    text_rows = queries.shape[0] // len(indices)
    rows, width = queries.shape
    heads = width // HD
    sharing = len(kv_pieces)
    kv_rows = SLOTS // sharing
    columns = weight.shape[1]
    wide = min(2048, columns)
    tall = min(64, width)

    def kernel(meta_ref, query_ref, *refs):
        kv_refs, weight_ref = refs[:sharing], refs[sharing]
        out_refs = refs[sharing + 1 : -5]
        key_ref, value_ref, attended_ref, held_ref, sems = refs[-5:]
        step = pl.program_id(0)

        def fetch(index):
            place = pl.ds(index * tall, tall)
            return pltpu.make_async_copy(
                weight_ref.at[place, :], held_ref.at[place, :], sems.at[index]
            )

        @pl.when(step == 0)
        def _():
            for index in range(width // tall):
                fetch(index).start()
            mine = lax.rem(meta_ref[order_len], sharing)
            for piece in range(sharing):
                row = pl.multiple_of(
                    lax.rem(mine + sharing - piece, sharing) * kv_rows, kv_rows
                )
                keys = kv_refs[piece][:, :HD].astype(F32)
                keys = keys * lax.rsqrt(jnp.mean(keys * keys, axis=-1, keepdims=True) + 1e-06)
                key_ref[pl.ds(row, kv_rows), :] = keys.astype(BF16)
                value_ref[pl.ds(row, kv_rows), :] = kv_refs[piece][:, HD:]
            for place, index in enumerate(indices):
                sample = meta_ref[index] * shard_rows // TXT
                slots = pl.ds(pl.multiple_of(sample * BLOCK, BLOCK), BLOCK)
                live = TT * meta_ref[order_len + 2 + SAMP_SECTION + sample]
                first = place * text_rows
                own = query_ref[first : first + text_rows, :]
                stacked = jnp.concatenate(
                    [own[:, h * HD : (h + 1) * HD] for h in range(heads)], axis=0
                )
                scores = lax.dot_general(
                    stacked,
                    key_ref[slots, :],
                    (((1,), (1,)), ((), ())),
                    preferred_element_type=F32,
                ) * (1.0 / math.sqrt(HD))
                slot = lax.broadcasted_iota(jnp.int32, scores.shape, 1)
                raised = jnp.where(slot < live, jnp.exp(scores), 0.0)
                weights = (raised / jnp.sum(raised, axis=-1, keepdims=True)).astype(BF16)
                result = jnp.dot(
                    weights, value_ref[slots, :], preferred_element_type=F32
                ).astype(BF16)
                for h in range(heads):
                    attended_ref[first : first + text_rows, h * HD : (h + 1) * HD] = result[
                        h * text_rows : (h + 1) * text_rows
                    ]
            for index in range(width // tall):
                fetch(index).wait()

        product = jnp.dot(
            attended_ref[...],
            held_ref[:, pl.ds(pl.multiple_of(step * wide, wide), wide)],
            preferred_element_type=F32,
        ).astype(BF16)
        first = 0
        for out_ref, size in zip(out_refs, sizes):
            out_ref[...] = product[first : first + size]
            first += size

    return pl.pallas_call(
        kernel,
        grid_spec=pltpu.PrefetchScalarGridSpec(
            num_scalar_prefetch=1,
            grid=(columns // wide,),
            in_specs=[pl.BlockSpec((rows, width), lambda i, meta: (0, 0))]
            + [pl.BlockSpec(piece.shape, lambda i, meta: (0, 0)) for piece in kv_pieces]
            + [pl.BlockSpec(memory_space=pl.ANY)],
            out_specs=[pl.BlockSpec((size, wide), lambda i, meta: (0, i)) for size in sizes],
            scratch_shapes=[
                pltpu.VMEM((SLOTS, HD), BF16),
                pltpu.VMEM((SLOTS, HD), BF16),
                pltpu.VMEM((rows, width), BF16),
                pltpu.VMEM((width, columns), BF16),
                pltpu.SemaphoreType.DMA((width // tall,)),
            ],
        ),
        out_shape=[jax.ShapeDtypeStruct((size, columns), BF16) for size in sizes],
        compiler_params=params(),
        cost_estimate=pl.CostEstimate(
            flops=8 * rows * width * columns,
            bytes_accessed=8 * width * columns,
            transcendentals=rows * heads * BLOCK,
        ),
        name="attend",
    )(meta, queries, *kv_pieces, weight)


def after(value, *others):
    if not others:
        return value
    return lax.optimization_barrier((value, *others))[0]


def local(
    mesh_shape,
    text_state,
    tile_feats,
    w_proj,
    w_query,
    w_kv,
    w_out,
    attn_gate,
    tile_counts,
    section_table,
):
    mp_count, section_count = mesh_shape["mp"], mesh_shape["section"]
    ring = ring_order(mp_count)
    far = mp_count // 2
    sharing = mp_count // KVH
    order = [far]
    for distance in range(far - 1, 0, -1):
        order += [-distance, distance]
    order.append(0)
    index_of = {offset: index for index, offset in enumerate(order)}
    index_of[-far] = 0
    table = np.array(
        [
            [ring[(ring.index(m) + offset) % mp_count] for offset in order] + [m, s]
            for s in range(section_count)
            for m in range(mp_count)
        ],
        np.int32,
    )
    device = lax.axis_index(("section", "mp"))
    places = lax.dynamic_slice(
        jnp.asarray(table), (device, 0), (1, mp_count + 2)
    ).reshape(-1)
    starts, counts = own_samples(tile_counts, section_table, places[mp_count + 1])
    meta = jnp.concatenate([places, starts, counts])

    up_pairs = [(ring[i], ring[(i + 1) % mp_count]) for i in range(mp_count)]
    down_pairs = [(target, source) for source, target in up_pairs]

    def up(value):
        return lax.ppermute(value, "mp", up_pairs)

    def down(value):
        return lax.ppermute(value, "mp", down_pairs)

    def across(pairs):
        return [
            (s * mp_count + a, ((s + 1) % section_count) * mp_count + b)
            for s in range(section_count)
            for a, b in pairs
        ]

    def up_across(value):
        return lax.ppermute(value, ("section", "mp"), across(up_pairs))

    def down_across(value):
        return lax.ppermute(value, ("section", "mp"), across(down_pairs))

    def to_next(value):
        return lax.ppermute(
            value, "section", [(s, (s + 1) % section_count) for s in range(section_count)]
        )

    def ring_sums(chains, hold=lambda left, value: value, turn=()):
        running = [part(sign * distance) for part, distance, sign, _, _ in chains]
        for hop in range(far):
            for index, (part, distance, sign, move, last) in enumerate(chains):
                left = distance - hop
                if left == 1:
                    running[index] = last(hold(left, running[index]))
                elif left > 1:
                    came = after(move(hold(left, running[index])), *turn)
                    running[index] = add(came, part(sign * (left - 1)))
                    turn = [running[index]]
        return running

    def both_ways(part, distance_up, distance_down, last_up=up, last_down=down):
        return [
            (part, distance_up, 1, up, last_up),
            (part, distance_down, -1, down, last_down),
        ]

    text_own = text_state[0]
    text_rows = text_own.shape[0]
    parts = 2 if text_rows % 32 == 0 else 1
    cut = text_rows // parts
    reach = [(far, far - 1), (far - 1, far)][:parts]
    text_next = to_next(text_own)
    gate_next = to_next(attn_gate)
    from_below, from_above = [text_own], [text_own]

    def text_round(*first):
        from_below.append(up(after(from_below[-1], *first)))
        from_above.append(down(after(from_above[-1], *first)))

    text_round()

    image_parts = project(places, tile_feats, w_proj, mp_count, 0, 1)
    image_parts += project(places, tile_feats, w_proj, mp_count, 1, mp_count - 1)
    image_chains = [
        chain
        for half, distances in enumerate(((far, far - 1), (far - 1, far)))
        for chain in both_ways(
            lambda offset, half=half: image_parts[index_of[offset]][half], *distances
        )
    ]

    text_scales = row_scales([text_own, from_below[1], from_above[1]])

    turns = [0, 3, 1, 2]
    came = ring_sums(
        [image_chains[turn] for turn in turns], turn=[gate_next, text_scales]
    )
    came = [came[turns.index(index)] for index in range(4)]
    image_cols = total_of(
        [[image_parts[index_of[0]][half], *came[2 * half : 2 * half + 2]] for half in range(2)]
    )

    text_round(image_cols)
    pieces = []
    moving = image_cols
    for step in range(section_count // 2):
        pieces += [
            moving,
            lax.ppermute(moving, "section", [(s, s ^ 1) for s in range(section_count)]),
        ]
        if step + 1 < section_count // 2:
            moving = lax.ppermute(
                moving,
                "section",
                [(s, (s + 2) % section_count) for s in range(section_count)],
            )

    kv_part = key_values(meta, pieces, w_kv[0], mp_count, section_count, sharing)

    for distance in range(3, far - 1):
        text_round(*([kv_part[0]] if distance == 3 else []))
    below, above = (after(value[-1], kv_part[0]) for value in (from_below, from_above))
    low = slice(text_rows - cut, text_rows)
    onward = [up(below[:cut]), down(above[low])]
    far_chunks = [up(onward[0])]
    if parts == 2:
        far_chunks.append(down(onward[1]))

    def kv_hold(left, value):
        return after(value, *onward) if left == min(2, far - 1) else value

    came = ring_sums(
        both_ways(lambda offset: kv_part[index_of[offset]], far, far - 1),
        kv_hold,
        turn=[from_below[2], from_above[2]] if far > 2 else [],
    )
    kv_own = (
        kv_part[index_of[0]].astype(F32) + came[0].astype(F32) + came[1].astype(F32)
    ).astype(BF16)
    weight_query, weight_out = w_query[0], w_out[0]
    queries = [query([text_own, from_below[1], from_above[1]], weight_query, text_scales)]
    kv_own = after(kv_own, queries[0], *far_chunks)
    kv_pieces = [kv_own]
    for step in range(1, sharing):
        pairs = [
            (m, m // sharing * sharing + (m % sharing + step) % sharing) for m in range(mp_count)
        ]
        kv_pieces.append(lax.ppermute(kv_own, "mp", pairs))

    behind = []
    if parts == 2:
        behind = [up(after(below, kv_own)[cut:]), down(after(above, kv_own)[:cut])]

    def attend_to(offsets, rows, sizes):
        indices = [index_of[offset] for offset in offsets]
        return attend(meta, rows, kv_pieces, weight_out, indices, sizes, text_rows, mp_count)

    last = far - 1
    near = [sign * distance for distance in range(1, last) for sign in (-1, 1)]
    out_parts = {offset: [None] * parts for offset in [last, -last]}
    first = [far] * parts + [-last, last]
    first_queries = query(far_chunks + onward, weight_query)
    first_part = attend_to(first, first_queries, [cut] * len(first))
    out_parts[far] = out_parts[-far] = first_part[:parts]
    out_parts[-last][0], out_parts[last][parts - 1] = first_part[parts:]
    ready = first_part[0]
    for distance in range(2, last):
        rows = [after(from_below[distance], ready), from_above[distance]]
        queries.append(query(rows, weight_query))
    rest_queries = jnp.concatenate(queries, axis=0)
    if parts == 2:
        behind_queries = after(query(behind, weight_query), rest_queries, ready)
        behind_part = attend_to([-last, last], behind_queries, [cut] * 2)
        out_parts[-last][1], out_parts[last][0] = behind_part
        ready = behind_part[0]
    sizes = [text_rows] + [cut] * (parts * len(near))
    own_part, *near_part = attend_to([0] + near, after(rest_queries, ready, text_next), sizes)
    for index, offset in enumerate(near):
        out_parts[offset] = near_part[parts * index :][:parts]
    own_next = to_next(own_part)

    branch_chains = [
        chain
        for part, distances in enumerate(reach)
        for chain in both_ways(
            lambda offset, part=part: out_parts[offset][part],
            *distances,
            up_across,
            down_across,
        )
    ]

    def branch_hold(left, value):
        if left == 1:
            return after(value, own_next)
        return after(value, *behind) if left == last else value

    turns = [0, 3, 1, 2] if parts == 2 else [0, 1]
    came = ring_sums([branch_chains[turn] for turn in turns], branch_hold)
    came = [came[turns.index(index)] for index in range(2 * parts)]
    results = []
    for part in range(parts):
        place = slice(part * cut, (part + 1) * cut)
        branch = own_next[place].astype(F32)
        for value in came[2 * part : 2 * part + 2]:
            branch = branch + value.astype(F32)
        results.append(
            (text_next[place].astype(F32) + jnp.tanh(gate_next[0]) * branch).astype(BF16)
        )
    return jnp.concatenate(results, axis=0)[None]


def solution(mesh):
    mesh_shape = dict(mesh.shape)

    def body(*arrays):
        return local(mesh_shape, *arrays)

    return jax.shard_map(
        body,
        mesh=mesh,
        in_specs=(
            P("section", "mp", None),
            P("section", "mp"),
            P("mp", None),
            P("section", None, "mp"),
            P("section", "mp", None),
            P("section", "mp", None),
            P("section"),
            P(),
            P(),
        ),
        out_specs=P("section", "mp", None),
        check_vma=False,
    )
```
